32 devices in a mesh: slab: 16 (over z, x, core), ang: 2 (over y).
Axes of the slice: x: 2, y: 2, z: 4, core: 2. Of those that a mesh axis runs over, the one named last changes fastest.
Arguments:
- volume: float32 [128, 256, 4096], P('slab', 'ang'), may hold values from 0.1 to 3
- measured: bfloat16 [8, 512, 4096], P('ang', 'slab'), may hold values from 0 to 2
- foot_start: int32 [16, 8], P('slab', 'ang'), may hold values from 0 to 480, as said below
- foot_len: int32 [16, 8], P('slab', 'ang'), may hold values from 32 to 96
- order: int32 [64], replicated, may hold values from 0 to 63, each once
- ray_table: float32 [64, 256], replicated, may hold values from 0.001953125 to 0.0078125
Outputs:
- updated: float32 [128, 256, 4096], P('slab', 'ang')
- residual: float32 [8, 512, 4096], P('ang', 'slab')
The draws below stay inside these ranges and needn't reach their ends.
Inputs may be any that keep to these rules, and one draw needn't show every extreme that they name: foot_start[s, j] + foot_len[s, j] <= 512; the footprint of slab s lies within rows (s - 2) * 32 to (s + 3) * 32.
All inputs are finite; a program needn't handle non-finite values.
Results may differ from the reference program's by a relative error of at most 0.0003.
Values sent between devices are 32-bit elements; how exact they have to be, the bound alone decides.
No kernel may reach another device: no remote copies, remote signals or barrier semaphores. Data moves between devices by JAX's collectives and lax.ppermute only.
A program may use at most 128 MiB of HBM per device.

```python
import math
import jax
import jax.numpy as jnp
from jax import lax

ZDEV = 8
NY = 256
NU = 4096
RDEV = 32
ANGLES = 8
ALL_ANG = 64
NZ = 128
NR = 512
N_SLAB = 16


def footprint(key):
    base = jax.random.fold_in(key, 7)
    first_key, second_key = jax.random.split(base)
    slab_ids = jnp.arange(N_SLAB, dtype=jnp.int32)[:, None]
    spread = 2 * RDEV * jnp.abs(2 * slab_ids + 1 - N_SLAB) // (2 * N_SLAB)
    lengths = RDEV + spread + jax.random.randint(first_key, (N_SLAB, ANGLES), 0, RDEV + 1, dtype=jnp.int32)
    lengths = jnp.minimum(lengths, 3 * RDEV)
    jitter = jax.random.randint(second_key, (N_SLAB, ANGLES), -(RDEV // 2), RDEV // 2 + 1, dtype=jnp.int32)
    centre = slab_ids * RDEV + RDEV // 2 + jitter
    starts = jnp.clip(centre - lengths // 2, 0, RDEV * N_SLAB - lengths)
    return (starts.astype(jnp.int32), lengths.astype(jnp.int32))


def draw_foot_start(key, part):
    return footprint(key)[0]


def draw_foot_len(key, part):
    return footprint(key)[1]


def level_of(own_key, extent, shards, least, high):
    level, own = 1.0, jax.random.fold_in(own_key, 6)
    for axis_at, parts in shards:
        heights = jnp.exp(jax.random.uniform(jax.random.fold_in(own, axis_at), (parts,), jnp.float32, least / len(shards), high / len(shards)))
        level = level * jnp.repeat(heights, extent[axis_at] // parts).reshape([-1 if axis == axis_at else 1 for axis in range(len(extent))])
    return level


def setup_inputs(seed: int = 0) -> dict:
    key_list = jax.random.split(jax.random.key(seed), 7)
    return {
        "volume": jnp.clip(jnp.exp(math.log(3.0) - 3.4011974 * jax.random.uniform(key_list[0], (NZ, NY, NU), jnp.float32) ** level_of(key_list[0], (NZ, NY, NU), ((0, 16), (1, 2)), -0.2, 0.2)), 0.1, 3.0),
        "measured": jnp.clip(2.0 * jax.random.uniform(key_list[1], (ANGLES, NR, NU), jnp.float32) ** level_of(key_list[1], (ANGLES, NR, NU), ((0, 2), (1, 16)), -0.2, 0.2), 0.0, 2.0).astype(jnp.bfloat16),
        "foot_start": draw_foot_start(jax.random.fold_in(key_list[6], 71), 0),
        "foot_len": draw_foot_len(jax.random.fold_in(key_list[6], 71), 0),
        "order": jax.random.permutation(key_list[4], ALL_ANG).astype(jnp.int32),
        "ray_table": jnp.clip(jnp.exp(jax.random.uniform(key_list[5], (ALL_ANG, NY), jnp.float32, math.log(0.001953125), math.log(0.0078125))), 0.001953125, 0.0078125),
    }


def hat_weights(starts, lengths, rows):
    first = starts[..., None, None]
    span_len = lengths[..., None, None]
    span = span_len / ZDEV
    centre = first + (jnp.arange(ZDEV, dtype=jnp.float32)[None, :] + 0.5) * span
    row_pos = rows[:, None]
    weight = jnp.maximum(0.0, 1.0 - jnp.abs(row_pos + 0.5 - centre) / span)
    inside = jnp.logical_and(row_pos >= first, row_pos < first + span_len)
    return jnp.where(inside, weight, 0.0)


def reference(volume, measured, foot_start, foot_len, order, ray_table):
    high = lax.Precision.HIGHEST
    picked = order[:ANGLES]
    onehot = (picked[:, None] == jnp.arange(ALL_ANG, dtype=jnp.int32)[None, :]).astype(jnp.float32)
    weights = jnp.dot(onehot, ray_table, precision=high)
    path = weights.sum(1)
    rows = jnp.arange(NR, dtype=jnp.float32)
    kernel = hat_weights(foot_start.T.astype(jnp.float32), foot_len.T.astype(jnp.float32), rows)
    kernel = kernel.transpose(0, 2, 1, 3).reshape(ANGLES, NR, NZ)
    summed = jnp.einsum('ay,zyx->azx', weights, volume, precision=high)
    project = jnp.einsum('arz,azx->arx', kernel, summed, precision=high)
    coverage = kernel.sum(-1)
    denom = jnp.maximum(path[:, None] * coverage, 0.25)
    residual = (measured.astype(jnp.float32) - project) / denom[:, :, None]
    back = jnp.einsum('arz,arx->azx', kernel, residual, precision=high)
    update = jnp.einsum('ay,azx->zyx', weights, back, precision=high)
    column = jnp.einsum('ay,az->zy', weights, kernel.sum(1), precision=high)
    updated = volume + update / column[:, :, None]
    return updated, residual
```

```python
import functools

import jax
import jax.numpy as jnp
from jax import lax
from jax.experimental import pallas as pl
from jax.experimental.pallas import tpu as pltpu
from jax.sharding import PartitionSpec as P

F32, BF16 = jnp.float32, jnp.bfloat16
CHUNKS = 2
TILE = 512
LANES = 128
SUBLANES = 8
VMEM = 56 * 1024 * 1024


def split(value):
    high = value.astype(BF16)
    return high, (value - high.astype(F32)).astype(BF16)


def dot(a, b):
    return jnp.dot(a, b, preferred_element_type=F32)


def dot3(a, b):
    ah, al = split(a)
    bh, bl = split(b)
    return dot(ah, bh) + (dot(ah, bl) + dot(al, bh))


def iota(shape, dim):
    return lax.broadcasted_iota(jnp.int32, shape, dim)


def pick(index, values):
    out = jnp.zeros(index.shape, values[0].dtype)
    for at, value in enumerate(values):
        out = jnp.where(index == at, value, out)
    return out


def slice_weights(dims, sign, pos_ref, order_ref, table_ref, rows_ref):
    per, groups, zb, cells = dims
    ang = pos_ref[1]
    for d in range(groups):
        group = lax.rem(ang + sign * d + groups, groups)
        for z in range(zb):
            for a in range(per):
                at = (d * zb + z) * per + a
                rows_ref[at:at + 1, :] = table_ref[pl.ds(order_ref[group * per + a], 1), :]
    wide = rows_ref[...]
    total = wide.shape[1]
    row_slice = lax.rem(iota(wide.shape, 0) // per, zb)
    lane_slice = iota(wide.shape, 1) // cells
    out = jnp.zeros_like(wide)
    for z in range(zb):
        shift = lax.rem(z * cells - ang * cells + total, total)
        here = jnp.logical_and(row_slice == z, lane_slice == z)
        out = jnp.where(here, pltpu.roll(wide, shift, 1), out)
    return out


def rays_kernel(dims, width, tile, extra, pos_ref, order_ref, start_ref, len_ref, table_ref, vol_ref, *refs):
    per, groups, zb, cells = dims
    outs, (rows_ref, left_ref) = refs[:2 * groups], refs[2 * groups:]
    half, t = pl.program_id(0), pl.program_id(1)
    zdev = vol_ref.shape[0]
    count = groups * SUBLANES

    @pl.when(jnp.logical_and(half == 0, t == 0))
    def _():
        weights = slice_weights(dims, 1, pos_ref, order_ref, table_ref, rows_ref)
        high, low = split(weights)
        both = jnp.concatenate([high, low], axis=0)
        left_ref[...] = jnp.concatenate([both, both], axis=1)
        if extra:
            shape = (zdev * per, LANES)
            angle, lane = lax.rem(iota(shape, 0), per), iota(shape, 1)
            starts = pick(angle, [start_ref[0, a].astype(F32) for a in range(per)])
            lengths = pick(angle, [len_ref[0, a].astype(F32) for a in range(per)])
            foot = jnp.where(lane == 0, starts, jnp.where(lane == 1, lengths, 0.0))
            for h in range(2):
                for d in range(groups):
                    outs[h * groups + d][:, width:] = foot if d == 0 else jnp.zeros_like(foot)

    left = left_ref[...]
    columns = pl.ds(pl.multiple_of(t * tile, tile), tile)
    for zp in range(zdev // zb):
        parts = [split(vol_ref[zp * zb + z]) for z in range(zb)]
        right = jnp.concatenate([p[0] for p in parts] + [p[1] for p in parts], axis=0)
        product = dot(left, right)
        sums = product[:count] + product[count:]
        for h in range(2):
            @pl.when(half == h)
            def _():
                for d in range(groups):
                    outs[h * groups + d][zp * SUBLANES:(zp + 1) * SUBLANES, columns] = (
                        sums[d * SUBLANES:(d + 1) * SUBLANES]
                    )


def ray_sums(dims, chunk, pos, order, foot_start, foot_len, table, volume):
    per, groups, zb, cells = dims
    zdev, _, total = volume.shape
    half = total // 2
    width = half // CHUNKS
    tile = min(TILE, width)
    steps = width // tile
    extra = LANES if chunk == 0 else 0
    out = jax.ShapeDtypeStruct((zdev * per, width + extra), F32)
    grid = pltpu.PrefetchScalarGridSpec(
        num_scalar_prefetch=4,
        grid=(2, steps),
        in_specs=[
            pl.BlockSpec(table.shape, lambda h, t, *_: (0, 0)),
            pl.BlockSpec(
                (zdev, cells, tile),
                lambda h, t, pos, *_: (0, 0, lax.rem(pos[0] + h, 2) * (half // tile) + chunk * steps + t),
            ),
        ],
        out_specs=[pl.BlockSpec(out.shape, lambda h, t, *_: (0, 0))] * (2 * groups),
        scratch_shapes=[
            pltpu.VMEM((groups * SUBLANES, table.shape[1]), F32),
            pltpu.VMEM((2 * groups * SUBLANES, 2 * zb * cells), BF16),
        ],
    )
    size = zdev * cells * width * 2
    return pl.pallas_call(
        functools.partial(rays_kernel, dims, width, tile, extra),
        grid_spec=grid,
        out_shape=[out] * (2 * groups),
        compiler_params=pltpu.CompilerParams(vmem_limit_bytes=VMEM),
        cost_estimate=pl.CostEstimate(flops=2 * size * 16, bytes_accessed=size * 4, transcendentals=0),
        name=f"ray_sums_{chunk}",
    )(pos, order, foot_start, foot_len, table, volume)


def residual_kernel(
    dims, rdev, zdev, width, extra, pos_ref, order_ref, table_ref, own_ref, near_ref, far_ref,
    own_foot, near_foot, far_foot, mine_ref, theirs_ref, _, res_ref, sent_ref, own_out, near_out, far_out,
):
    per, groups, zb, cells = dims
    slab, ang = pos_ref[0], pos_ref[1]
    block = zdev * per
    count, rows = 6 * block, 2 * per * rdev
    odd = lax.rem(slab, 2)
    sibling = slab + 1 - 2 * odd
    shape = (count, rows)
    foot = jnp.concatenate(
        [r[i] for r in (own_foot, near_foot, far_foot) for i in range(2)], axis=0
    )
    start, length = foot[:, 0:1], foot[:, 1:2]
    at = iota((count, 1), 0)
    at_in = lax.rem(at, block)
    slice_at = (at_in // (zb * per)) * zb + lax.rem(at_in // per, zb)
    span = jnp.where(length > 0.0, length, 1.0) / zdev
    centre = start + (slice_at.astype(F32) + 0.5) * span
    row_id = iota((1, rows), 1)
    row_slab = jnp.where(row_id // (per * rdev) == 0, slab, sibling)
    row = (row_slab * rdev + lax.rem(row_id, rdev)).astype(F32)
    same_angle = iota(shape, 0) % per == (iota(shape, 1) // rdev) % per
    hat = jnp.maximum(0.0, 1.0 - jnp.abs(row + 0.5 - centre) / span)
    inside = jnp.logical_and(row >= start, row < start + length)
    kernel = jnp.where(jnp.logical_and(same_angle, inside), hat, 0.0)
    if extra:
        weight = jnp.broadcast_to(jnp.sum(kernel, axis=1, keepdims=True), (count, LANES))
        for i, ref in enumerate((own_out, near_out, far_out)):
            for j in range(2):
                ref[j, :, width:] = weight[(2 * i + j) * block:(2 * i + j + 1) * block]
    kernel_t = kernel.T
    cover = jnp.sum(kernel_t, axis=1, keepdims=True)
    angle = lax.rem(iota((rows, 1), 0) // rdev, per)
    path = jnp.zeros((rows, 1), F32)
    for a in range(per):
        total = jnp.sum(table_ref[pl.ds(order_ref[ang * per + a], 1), :], axis=1, keepdims=True)
        path = jnp.where(angle == a, total, path)
    inverse = 1.0 / jnp.maximum(path * cover, 0.25)

    tile = min(TILE, width)
    for t in range(width // tile):
        columns = slice(t * tile, (t + 1) * tile)
        sums = jnp.concatenate(
            [r[i, :, columns] for r in (own_ref, near_ref, far_ref) for i in range(2)], axis=0
        )
        project = dot3(kernel_t, sums)
        measured = jnp.concatenate(
            [
                mine_ref[:, :, columns].astype(F32).reshape(per * rdev, tile),
                theirs_ref[:, :, columns].reshape(per * rdev, tile),
            ],
            axis=0,
        )
        residual = (measured - project) * inverse
        res_ref[:, :, columns] = residual[:per * rdev].reshape(per, rdev, tile)
        sent_ref[:, :, columns] = residual[per * rdev:].reshape(per, rdev, tile)
        back = dot3(kernel, residual)
        for i, ref in enumerate((own_out, near_out, far_out)):
            for j in range(2):
                ref[j, :, columns] = back[(2 * i + j) * block:(2 * i + j + 1) * block]


def residual_step(dims, zdev, chunk, pos, order, table, sums, first, measured, theirs, res):
    per, groups, zb, cells = dims
    _, rdev, total = measured.shape
    half = total // 2
    width = half // CHUNKS
    extra = LANES if chunk == 0 else 0
    block = zdev * per
    full = pl.BlockSpec((2, block, width), lambda i, *_: (0, 0, 0))
    foot = pl.BlockSpec((2, block, LANES), lambda i, *_: (0, 0, width // LANES))
    mine = pl.BlockSpec((per, rdev, width), lambda i, pos, *_: (0, 0, lax.rem(pos[0], 2) * CHUNKS + chunk))
    given = jax.ShapeDtypeStruct((2, block, width + extra), F32)
    whole = pl.BlockSpec(given.shape, lambda i, *_: (0, 0, 0))
    piece = pl.BlockSpec((per, rdev, width), lambda i, *_: (0, 0, 0))
    inputs = [*sums, *first, measured, theirs]
    specs = [full] * 3 + [foot] * 3 + [mine, pl.BlockSpec((per, rdev, width), lambda i, *_: (0, 0, chunk))]
    aliases = {}
    if res is None:
        inputs.append(pos)
        specs.append(pl.BlockSpec(memory_space=pltpu.SMEM))
    else:
        inputs.append(res)
        specs.append(pl.BlockSpec(memory_space=pl.ANY))
        aliases = {2 + 1 + 8: 0}
    flops = 2 * 3 * 2 * 6 * block * 2 * per * rdev * width
    size = 4 * width * (12 * block + 4 * per * rdev)
    return pl.pallas_call(
        functools.partial(residual_kernel, dims, rdev, zdev, width, extra),
        grid_spec=pltpu.PrefetchScalarGridSpec(
            num_scalar_prefetch=2,
            grid=(1,),
            in_specs=[pl.BlockSpec(table.shape, lambda i, *_: (0, 0))] + specs,
            out_specs=[mine, piece, whole, whole, whole],
        ),
        out_shape=[
            jax.ShapeDtypeStruct((per, rdev, total), F32),
            jax.ShapeDtypeStruct((per, rdev, width), F32),
            given, given, given,
        ],
        input_output_aliases=aliases,
        compiler_params=pltpu.CompilerParams(vmem_limit_bytes=VMEM),
        cost_estimate=pl.CostEstimate(flops=flops, bytes_accessed=size, transcendentals=0),
        name=f"residual_{chunk}",
    )(pos, order, table, *inputs)


def update_kernel(dims, width, tile, depth, pos_ref, order_ref, table_ref, vol_ref, *refs):
    per, groups, zb, cells = dims
    backs, refs = refs[:2 * groups], refs[2 * groups:]
    feet, (piece_ref, _, _, out_ref, res_ref, rows_ref, left_ref) = refs[:groups], refs[groups:]
    half, t = pl.program_id(0), pl.program_id(1)
    zdev = vol_ref.shape[0]
    count = groups * SUBLANES

    @pl.when(jnp.logical_and(half == 0, t == 0))
    def _():
        res_ref[...] = piece_ref[...]
        weights = slice_weights(dims, -1, pos_ref, order_ref, table_ref, rows_ref)
        pad = jnp.zeros((depth - 3 * count, weights.shape[1]), F32)
        for zp in range(zdev // zb):
            rows = slice(zp * SUBLANES, (zp + 1) * SUBLANES)
            slices = jnp.concatenate([ref[rows, 0:1] for ref in feet], axis=0)
            scaled = weights / jnp.sum(weights * slices, axis=0, keepdims=True)
            high = scaled.astype(BF16).astype(F32)
            stacked = jnp.concatenate([high, high, scaled - high, pad], axis=0)
            left_ref[zp] = stacked.T.astype(BF16)

    columns = pl.ds(pl.multiple_of(t * tile, tile), tile)
    pad = jnp.zeros((depth - 3 * count, tile), BF16)
    for zp in range(zdev // zb):
        rows = slice(zp * SUBLANES, (zp + 1) * SUBLANES)
        back = jnp.concatenate(
            [jnp.where(half == 0, backs[d][rows, columns], backs[groups + d][rows, columns]) for d in range(groups)],
            axis=0,
        )
        high, low = split(back)
        change = dot(left_ref[zp], jnp.concatenate([high, low, high, pad], axis=0))
        for z in range(zb):
            out_ref[zp * zb + z] = vol_ref[zp * zb + z] + change[z * cells:(z + 1) * cells]


def update_step(dims, chunk, pos, order, table, volume, backs, feet, piece, res, out):
    per, groups, zb, cells = dims
    zdev, _, total = volume.shape
    half = total // 2
    width = half // CHUNKS
    tile = min(TILE, width)
    steps = width // tile
    depth = -(-3 * groups * SUBLANES // LANES) * LANES
    block = zdev * per
    rdev = res.shape[1]
    vol = pl.BlockSpec(
        (zdev, cells, tile),
        lambda h, t, pos, *_: (0, 0, lax.rem(pos[0] + h, 2) * (half // tile) + chunk * steps + t),
    )
    inputs = [table, volume, *backs, *feet, piece, res]
    specs = [pl.BlockSpec(table.shape, lambda h, t, *_: (0, 0)), vol]
    specs += [pl.BlockSpec((block, width), lambda h, t, *_: (0, 0))] * (2 * groups)
    specs += [pl.BlockSpec((block, LANES), lambda h, t, *_: (0, width // LANES))] * groups
    specs += [pl.BlockSpec((per, rdev, width), lambda h, t, *_: (0, 0, 0)), pl.BlockSpec(memory_space=pl.ANY)]
    aliases = {2 + len(inputs) - 1: 1}
    if out is None:
        inputs.append(pos)
        specs.append(pl.BlockSpec(memory_space=pltpu.SMEM))
    else:
        inputs.append(out)
        specs.append(pl.BlockSpec(memory_space=pl.ANY))
        aliases[2 + len(inputs) - 1] = 0
    size = zdev * cells * width * 2
    return pl.pallas_call(
        functools.partial(update_kernel, dims, width, tile, depth),
        grid_spec=pltpu.PrefetchScalarGridSpec(
            num_scalar_prefetch=2,
            grid=(2, steps),
            in_specs=specs,
            out_specs=[
                vol,
                pl.BlockSpec(
                    (per, rdev, width),
                    lambda h, t, pos, *_: (0, 0, (1 - lax.rem(pos[0], 2)) * CHUNKS + chunk),
                ),
            ],
            scratch_shapes=[
                pltpu.VMEM((groups * SUBLANES, table.shape[1]), F32),
                pltpu.VMEM((zdev // zb, zb * cells, depth), BF16),
            ],
        ),
        out_shape=[jax.ShapeDtypeStruct(volume.shape, F32), jax.ShapeDtypeStruct(res.shape, F32)],
        input_output_aliases=aliases,
        compiler_params=pltpu.CompilerParams(vmem_limit_bytes=VMEM),
        cost_estimate=pl.CostEstimate(flops=2 * size * 48, bytes_accessed=size * 8, transcendentals=0),
        name=f"update_{chunk}",
    )(pos, order, *inputs)


def body(volume, measured, foot_start, foot_len, order, table):
    slabs, groups = lax.axis_size("slab"), lax.axis_size("ang")
    per, rdev, total = measured.shape
    zdev, cells, _ = volume.shape
    half = total // 2
    zb = SUBLANES // per
    dims = (per, groups, zb, cells)
    pos = jnp.stack([lax.axis_index("slab"), lax.axis_index("ang")]).astype(jnp.int32)

    def along(value, to):
        pairs = [(s, to(s)) for s in range(slabs) if 0 <= to(s) < slabs]
        return lax.ppermute(value, "slab", pairs)

    def spread(value, other, d):
        if not (other or d):
            return value
        pairs = [
            (s * groups + a, (s ^ other) * groups + (a + d) % groups) for s in range(slabs) for a in range(groups)
        ]
        return lax.ppermute(value, ("slab", "ang"), pairs)

    def facing(s):
        return s ^ 2

    def beyond(s):
        return s - 4 if s & 2 else s + 4

    def back_from_beyond(s):
        return s + 4 if s & 2 else s - 4

    odd = lax.rem(pos[0], 2)
    theirs = along(
        lax.dynamic_slice_in_dim(measured, (1 - odd) * half, half, 2).astype(F32), lambda s: s ^ 1
    )

    sums, res, sent, given = [], None, [], []
    for c in range(CHUNKS):
        parts = ray_sums(dims, c, pos, order, foot_start, foot_len, table, volume)
        parts = [spread(parts[h * groups + d], h, d) for h in range(2) for d in range(groups)]
        own = jnp.stack([sum(parts[:groups]), sum(parts[groups:])])
        near = along(own, facing)
        far = along(near, beyond)
        sums.append((own, near, far))
    for c in range(CHUNKS):
        res, piece, own, near, far = residual_step(
            dims, zdev, c, pos, order, table, sums[c], sums[0], measured, theirs, res
        )
        sent.append(along(piece, lambda s: s ^ 1))
        near = near + along(far, back_from_beyond)
        arrived = along(near, facing)
        halves = [own[i] + arrived[i] for i in range(2)]
        given.append([spread(halves[h], h, d) for h in range(2) for d in range(groups)])
    out = None
    for c in range(CHUNKS):
        out, res = update_step(
            dims, c, pos, order, table, volume, given[c], given[0][:groups], sent[c], res, out
        )
    return out, res


def solution(mesh):
    return jax.shard_map(
        body,
        mesh=mesh,
        in_specs=(
            P("slab", "ang", None),
            P("ang", "slab", None),
            P("slab", "ang"),
            P("slab", "ang"),
            P(),
            P(),
        ),
        out_specs=(P("slab", "ang", None), P("ang", "slab", None)),
        check_vma=False,
    )
```

```python
import functools

import jax
import jax.numpy as jnp
from jax import lax
from jax.experimental import pallas as pl
from jax.experimental.pallas import tpu as pltpu
from jax.sharding import PartitionSpec as P

F32, BF16 = jnp.float32, jnp.bfloat16
CHUNKS = 2
TILE = 512
LANES = 128
SUBLANES = 8
MIB = 1024 * 1024

IN_VMEM = pl.BlockSpec(memory_space=pltpu.VMEM)
IN_SMEM = pl.BlockSpec(memory_space=pltpu.SMEM)
ANYWHERE = pl.BlockSpec(memory_space=pl.ANY)


def split(value):
    high = value.astype(BF16)
    return high, (value - high.astype(F32)).astype(BF16)


def dot(a, b):
    return jnp.dot(a, b, preferred_element_type=F32)


def dot3(a, b):
    return dot(a[0], b[0]) + (dot(a[0], b[1]) + dot(a[1], b[0]))


def iota(shape, dim):
    return lax.broadcasted_iota(jnp.int32, shape, dim)


def low_bits(value, size):
    assert size & (size - 1) == 0
    return value & (size - 1)


def over(value, size):
    assert size & (size - 1) == 0
    return value >> (size.bit_length() - 1)


def pick(index, values):
    out = jnp.zeros(index.shape, values[0].dtype)
    for at, value in enumerate(values):
        out = jnp.where(index == at, value, out)
    return out


def tiles(width):
    step = min(TILE, width)
    return [(at, min(step, width - at)) for at in range(0, width, step)]


def slice_weights(dims, sign, order_ref, table_ref, rows_ref):
    per, groups, zb, cells = dims
    ang = lax.axis_index("ang")
    for d in range(groups):
        group = lax.rem(ang + sign * d + groups, groups)
        for z in range(zb):
            for a in range(per):
                at = (d * zb + z) * per + a
                rows_ref[at:at + 1, :] = table_ref[pl.ds(order_ref[group * per + a], 1), :]
    wide = rows_ref[...]
    total = wide.shape[1]
    row_slice = low_bits(over(iota(wide.shape, 0), per), zb)
    lane_slice = over(iota(wide.shape, 1), cells)
    out = jnp.zeros_like(wide)
    for z in range(zb):
        shift = lax.rem(z * cells - ang * cells + total, total)
        here = jnp.logical_and(row_slice == z, lane_slice == z)
        out = jnp.where(here, pltpu.roll(wide, shift, 1), out)
    return out


def volume_pieces(dims, zdev, half, offset, width):
    odd = lax.rem(lax.axis_index("slab"), 2)
    zb = dims[2]
    for h in range(2):
        start = lax.rem(odd + h, 2) * half + offset
        for zp in range(zdev // zb):
            yield h, zp, slice(zp * zb, (zp + 1) * zb), pl.ds(pl.multiple_of(start, LANES), width)


def rays_kernel(dims, first, half, offset, width, *refs):
    per, groups, zb, cells = dims
    count = groups * SUBLANES
    if first:
        order_ref, start_ref, len_ref, table_ref, vol_ref, *refs = refs
    else:
        given_ref, vol_ref, *refs = refs
    outs, refs = refs[:2 * groups], refs[2 * groups:]
    if first:
        left_ref, base_ref, buf, sems, table_buf, rows_ref, table_sem = refs
    else:
        buf, sems = refs
    zdev = vol_ref.shape[0]
    copies = {}
    if first:
        table_copy = pltpu.make_async_copy(table_ref, table_buf, table_sem)
        table_copy.start()
    for h, zp, slices, columns in volume_pieces(dims, zdev, half, offset, width):
        copies[h, zp] = pltpu.make_async_copy(
            vol_ref.at[slices, :, columns], buf.at[h, slices], sems.at[h, zp]
        )
        copies[h, zp].start()
    if first:
        shape = (zdev * per, LANES)
        angle, lane = low_bits(iota(shape, 0), per), iota(shape, 1)
        starts = pick(angle, [start_ref[0, a].astype(F32) for a in range(per)])
        lengths = pick(angle, [len_ref[0, a].astype(F32) for a in range(per)])
        foot = jnp.where(lane == 0, starts, jnp.where(lane == 1, lengths, 0.0))
        for h in range(2):
            for d in range(groups):
                outs[h * groups + d][:, width:] = foot if d == 0 else jnp.zeros_like(foot)
        table_copy.wait()
        both = jnp.concatenate(split(slice_weights(dims, 1, order_ref, table_buf, rows_ref)), axis=0)
        left = jnp.concatenate([both, both], axis=1)
        left_ref[...] = left
        base_ref[...] = slice_weights(dims, -1, order_ref, table_buf, rows_ref)
    else:
        left = given_ref[...]
    for (h, zp), copy in copies.items():
        copy.wait()
        for at, size in tiles(width):
            columns = slice(at, at + size)
            parts = [split(buf[h, zp * zb + z, :, columns]) for z in range(zb)]
            product = dot(left, jnp.concatenate([p[0] for p in parts] + [p[1] for p in parts], axis=0))
            sums = product[:count] + product[count:]
            for d in range(groups):
                outs[h * groups + d][zp * SUBLANES:(zp + 1) * SUBLANES, columns] = (
                    sums[d * SUBLANES:(d + 1) * SUBLANES]
                )


def ray_sums(dims, chunk, offset, width, given, small, table, volume):
    per, groups, zb, cells = dims
    zdev, _, total = volume.shape
    first = chunk == 0
    count, all_cells = groups * SUBLANES, table.shape[1]
    out = jax.ShapeDtypeStruct((zdev * per, width + (LANES if first else 0)), F32)
    left = jax.ShapeDtypeStruct((2 * count, 2 * zb * cells), BF16)
    base = jax.ShapeDtypeStruct((count, all_cells), F32)
    assert zb * cells == all_cells
    scratch = [pltpu.VMEM((2, zdev, cells, width), F32), pltpu.SemaphoreType.DMA((2, zdev // zb))]
    if first:
        scratch += [pltpu.VMEM(table.shape, F32), pltpu.VMEM(base.shape, F32), pltpu.SemaphoreType.DMA]
        args, specs = [*small, table, volume], [IN_SMEM] * 3 + [ANYWHERE, ANYWHERE]
        shapes = [out] * (2 * groups) + [left, base]
    else:
        args, specs = [given, volume], [IN_VMEM, ANYWHERE]
        shapes = [out] * (2 * groups)
    size = zdev * cells * width * 2
    return pl.pallas_call(
        functools.partial(rays_kernel, dims, first, total // 2, offset, width),
        in_specs=specs,
        out_specs=[IN_VMEM] * len(shapes),
        out_shape=shapes,
        scratch_shapes=scratch,
        compiler_params=pltpu.CompilerParams(vmem_limit_bytes=(58 if first else 50) * MIB),
        cost_estimate=pl.CostEstimate(flops=2 * size * 16, bytes_accessed=size * 4, transcendentals=0),
        name=f"ray_sums_{chunk}",
    )(*args)


def footprint_matrix(dims, zdev, rdev, foot):
    per, groups, zb, cells = dims
    block = zdev * per
    count, rows = 6 * block, 2 * per * rdev
    slab = lax.axis_index("slab")
    sibling = slab + 1 - 2 * lax.rem(slab, 2)
    start, length = foot[:, 0:1], foot[:, 1:2]
    at = low_bits(iota((count, 1), 0), block)
    slice_at = over(at, zb * per) * zb + low_bits(over(at, per), zb)
    span = jnp.where(length > 0.0, length, 1.0) / zdev
    centre = start + (slice_at.astype(F32) + 0.5) * span
    row_id = iota((1, rows), 1)
    row_slab = jnp.where(row_id < per * rdev, slab, sibling)
    row = (row_slab * rdev + low_bits(row_id, rdev)).astype(F32)
    shape = (count, rows)
    same_angle = low_bits(iota(shape, 0), per) == low_bits(over(iota(shape, 1), rdev), per)
    hat = jnp.maximum(0.0, 1.0 - jnp.abs(row + 0.5 - centre) / span)
    inside = jnp.logical_and(row >= start, row < start + length)
    return jnp.where(jnp.logical_and(same_angle, inside), hat, 0.0)


def residual_kernel(dims, first, half, rdev, zdev, offset, width, *refs):
    per, groups, zb, cells = dims
    block = zdev * per
    if first:
        order_ref, table_ref, *refs = refs
    else:
        mats, inverse_ref, refs = refs[:4], refs[4], refs[5:]
    sums_refs, (mine_ref, theirs_ref), refs = refs[:3], refs[3:5], refs[5:]
    mine_out, sent_out, *refs = refs
    outs, refs = refs[:3], refs[3:]
    if first:
        foot = jnp.concatenate([r[i, :, width:] for r in sums_refs for i in range(2)], axis=0)
        kernel = footprint_matrix(dims, zdev, rdev, foot)
        count, rows = kernel.shape
        weight = jnp.broadcast_to(jnp.sum(kernel, axis=1, keepdims=True), (count, LANES))
        for i, ref in enumerate(outs):
            for j in range(2):
                ref[j, :, width:] = weight[(2 * i + j) * block:(2 * i + j + 1) * block]
        kernel_t = kernel.T
        cover = jnp.sum(kernel_t, axis=1, keepdims=True)
        angle = low_bits(over(iota((rows, 1), 0), rdev), per)
        path = jnp.zeros((rows, 1), F32)
        for a in range(per):
            at = order_ref[lax.axis_index("ang") * per + a]
            path = jnp.where(angle == a, jnp.sum(table_ref[pl.ds(at, 1), :], axis=1, keepdims=True), path)
        inverse = 1.0 / jnp.maximum(path * cover, 0.25)
        ahead, back = split(kernel_t), split(kernel)
        for ref, value in zip(refs, (*ahead, *back)):
            ref[...] = value
        refs[4][...] = jnp.broadcast_to(inverse, (rows, LANES))
    else:
        ahead, back = (mats[0][...], mats[1][...]), (mats[2][...], mats[3][...])
        inverse = inverse_ref[:, 0:1]
    start = lax.rem(lax.axis_index("slab"), 2) * half + offset
    for at, size in tiles(width):
        columns = slice(at, at + size)
        mine = mine_ref[:, :, pl.ds(pl.multiple_of(start + at, LANES), size)].astype(F32)
        theirs = theirs_ref[:, :, offset + at:offset + at + size]
        measured = jnp.concatenate([m.reshape(per * rdev, size) for m in (mine, theirs)], axis=0)
        sums = jnp.concatenate([r[i, :, columns] for r in sums_refs for i in range(2)], axis=0)
        residual = (measured - dot3(ahead, split(sums))) * inverse
        mine_out[:, :, columns] = residual[:per * rdev].reshape(per, rdev, size)
        sent_out[:, :, columns] = residual[per * rdev:].reshape(per, rdev, size)
        given = dot3(back, split(residual))
        for i, ref in enumerate(outs):
            for j in range(2):
                ref[j, :, columns] = given[(2 * i + j) * block:(2 * i + j + 1) * block]


def residual_step(dims, zdev, chunk, offset, width, mats, order, table, sums, measured, theirs):
    per, groups, zb, cells = dims
    _, rdev, total = measured.shape
    first = chunk == 0
    block = zdev * per
    count, rows = 6 * block, 2 * per * rdev
    given = jax.ShapeDtypeStruct((2, block, width + (LANES if first else 0)), F32)
    piece = jax.ShapeDtypeStruct((per, rdev, width), F32)
    shapes = [piece, piece, given, given, given]
    if first:
        args, specs = [order, table], [IN_SMEM, IN_VMEM]
        ahead, back = jax.ShapeDtypeStruct((rows, count), BF16), jax.ShapeDtypeStruct((count, rows), BF16)
        shapes += [ahead, ahead, back, back, jax.ShapeDtypeStruct((rows, LANES), F32)]
    else:
        args, specs = list(mats), [IN_VMEM] * len(mats)
    args += [*sums, measured, theirs]
    specs += [IN_VMEM] * 5
    return pl.pallas_call(
        functools.partial(residual_kernel, dims, first, total // 2, rdev, zdev, offset, width),
        in_specs=specs,
        out_specs=[IN_VMEM] * len(shapes),
        out_shape=shapes,
        compiler_params=pltpu.CompilerParams(vmem_limit_bytes=16 * MIB),
        cost_estimate=pl.CostEstimate(
            flops=12 * count * rows * width, bytes_accessed=8 * width * (count + rows), transcendentals=0
        ),
        name=f"residual_{chunk}",
    )(*args)


def update_kernel(dims, first, half, offset, width, depth, *refs):
    per, groups, zb, cells = dims
    count = groups * SUBLANES
    left_in, backs, refs = refs[0], refs[1:1 + 2 * groups], refs[1 + 2 * groups:]
    mine_ref, theirs_ref, vol_ref, *refs = refs
    if not first:
        refs = refs[2:]
    out_ref, res_ref, *refs = refs
    if first:
        left_out, *refs = refs
    buf, in_sems, out_sems, res_sems = refs
    zdev = vol_ref.shape[0]
    odd = lax.rem(lax.axis_index("slab"), 2)
    arrive, leave = {}, {}
    pieces = list(volume_pieces(dims, zdev, half, offset, width))
    for h, zp, slices, columns in pieces:
        arrive[h, zp] = pltpu.make_async_copy(
            vol_ref.at[slices, :, columns], buf.at[h, slices], in_sems.at[h, zp]
        )
        arrive[h, zp].start()
        leave[h, zp] = pltpu.make_async_copy(
            buf.at[h, slices], out_ref.at[slices, :, columns], out_sems.at[h, zp]
        )
    kept = []
    for h, ref in enumerate((mine_ref, theirs_ref)):
        start = pl.multiple_of(lax.rem(odd + h, 2) * half + offset, LANES)
        kept.append(pltpu.make_async_copy(ref, res_ref.at[:, :, pl.ds(start, width)], res_sems.at[h]))
        kept[h].start()
    if first:
        weights = left_in[...]
        pad = jnp.zeros((depth - 3 * count, weights.shape[1]), F32)
        lefts = left_out
        for zp in range(zdev // zb):
            rows = slice(zp * SUBLANES, (zp + 1) * SUBLANES)
            slices = jnp.concatenate([ref[rows, width:width + 1] for ref in backs[:groups]], axis=0)
            scaled = weights / jnp.sum(weights * slices, axis=0, keepdims=True)
            high = scaled.astype(BF16).astype(F32)
            stacked = jnp.concatenate([high, high, scaled - high, pad], axis=0)
            left_out[zp] = stacked.T.astype(BF16)
    else:
        lefts = left_in
    for h, zp, _, _ in pieces:
        rows = slice(zp * SUBLANES, (zp + 1) * SUBLANES)
        arrive[h, zp].wait()
        left = lefts[zp]
        for at, size in tiles(width):
            columns = slice(at, at + size)
            back = jnp.concatenate([backs[h * groups + d][rows, columns] for d in range(groups)], axis=0)
            high, low = split(back)
            pad = jnp.zeros((depth - 3 * count, size), BF16)
            change = dot(left, jnp.concatenate([high, low, high, pad], axis=0))
            for z in range(zb):
                buf[h, zp * zb + z, :, columns] += change[z * cells:(z + 1) * cells]
        leave[h, zp].start()
    for copy in kept + list(leave.values()):
        copy.wait()


def update_step(dims, chunk, offset, width, left, backs, mine, theirs, volume, out, res):
    per, groups, zb, cells = dims
    zdev, _, total = volume.shape
    first = chunk == 0
    count = groups * SUBLANES
    depth = -(-3 * count // LANES) * LANES
    args = [left, *backs, mine, theirs, volume]
    specs = [IN_VMEM] * (3 + len(backs)) + [ANYWHERE]
    shapes = [jax.ShapeDtypeStruct(volume.shape, F32), jax.ShapeDtypeStruct((*mine.shape[:2], total), F32)]
    aliases = {}
    if first:
        shapes.append(jax.ShapeDtypeStruct((zdev // zb, zb * cells, depth), BF16))
    else:
        aliases = {len(args): 0, len(args) + 1: 1}
        args += [out, res]
        specs += [ANYWHERE, ANYWHERE]
    size = zdev * cells * width * 2
    return pl.pallas_call(
        functools.partial(update_kernel, dims, first, total // 2, offset, width, depth),
        in_specs=specs,
        out_specs=[ANYWHERE, ANYWHERE] + [IN_VMEM] * (len(shapes) - 2),
        out_shape=shapes,
        scratch_shapes=[
            pltpu.VMEM((2, zdev, cells, width), F32),
            pltpu.SemaphoreType.DMA((2, zdev // zb)),
            pltpu.SemaphoreType.DMA((2, zdev // zb)),
            pltpu.SemaphoreType.DMA((2,)),
        ],
        input_output_aliases=aliases,
        compiler_params=pltpu.CompilerParams(vmem_limit_bytes=50 * MIB),
        cost_estimate=pl.CostEstimate(flops=2 * size * 48, bytes_accessed=size * 8, transcendentals=0),
        name=f"update_{chunk}",
    )(*args)


def body(volume, measured, foot_start, foot_len, order, table):
    slabs, groups = lax.axis_size("slab"), lax.axis_size("ang")
    per, rdev, total = measured.shape
    zdev, cells, _ = volume.shape
    half = total // 2
    zb = SUBLANES // per
    dims = (per, groups, zb, cells)
    base_width = half // CHUNKS
    widths = [base_width] * CHUNKS
    offsets = [sum(widths[:c]) for c in range(CHUNKS)]

    def along(value, to):
        pairs = [(s, to(s)) for s in range(slabs) if 0 <= to(s) < slabs]
        return lax.ppermute(value, "slab", pairs)

    def spread(value, other, d):
        if not (other or d):
            return value
        pairs = [
            (s * groups + a, (s ^ other) * groups + (a + d) % groups) for s in range(slabs) for a in range(groups)
        ]
        return lax.ppermute(value, ("slab", "ang"), pairs)

    def facing(s):
        return s ^ 2

    def beyond(s):
        return s - 4 if s & 2 else s + 4

    def back_from_beyond(s):
        return s + 4 if s & 2 else s - 4

    odd = lax.rem(lax.axis_index("slab"), 2)
    theirs = along(
        lax.dynamic_slice_in_dim(measured, (1 - odd) * half, half, 2).astype(F32), lambda s: s ^ 1
    )

    sums, left, base = [], None, None
    for c in range(CHUNKS):
        parts = ray_sums(
            dims, c, offsets[c], widths[c], left, (order, foot_start, foot_len), table, volume
        )
        if c == 0:
            left, base = parts[2 * groups:]
        parts = [spread(parts[h * groups + d], h, d) for h in range(2) for d in range(groups)]
        own = jnp.stack([sum(parts[:groups]), sum(parts[groups:])])
        near = along(own, facing)
        far = along(near, beyond)
        sums.append((own, near, far))
    pieces, given, mats = [], [], None
    for c in range(CHUNKS):
        mine, piece, own, near, far, *rest = residual_step(
            dims, zdev, c, offsets[c], widths[c], mats, order, table, sums[c], measured, theirs
        )
        mats = rest if c == 0 else mats
        pieces.append((mine, along(piece, lambda s: s ^ 1)))
        near = near + along(far, back_from_beyond)
        arrived = along(near, facing)
        halves = [own[i] + arrived[i] for i in range(2)]
        given.append([spread(halves[h], h, d) for h in range(2) for d in range(groups)])
    out, res, left = None, None, base
    for c in range(CHUNKS):
        out, res, *rest = update_step(
            dims, c, offsets[c], widths[c], left, given[c], *pieces[c], volume, out, res
        )
        left = rest[0] if c == 0 else left
    return out, res


def solution(mesh):
    return jax.shard_map(
        body,
        mesh=mesh,
        in_specs=(
            P("slab", "ang", None),
            P("ang", "slab", None),
            P("slab", "ang"),
            P("slab", "ang"),
            P(),
            P(),
        ),
        out_specs=(P("slab", "ang", None), P("ang", "slab", None)),
        check_vma=False,
    )
```

```python
import functools

import jax
import jax.numpy as jnp
from jax import lax
from jax.experimental import pallas as pl
from jax.experimental.pallas import tpu as pltpu
from jax.sharding import PartitionSpec as P

F32, BF16 = jnp.float32, jnp.bfloat16
CHUNKS = 2
TILE = 512
LANES = 128
SUBLANES = 8
MIB = 1024 * 1024

IN_VMEM = pl.BlockSpec(memory_space=pltpu.VMEM)
IN_SMEM = pl.BlockSpec(memory_space=pltpu.SMEM)
ANYWHERE = pl.BlockSpec(memory_space=pl.ANY)


def split(value):
    high = value.astype(BF16)
    return high, (value - high.astype(F32)).astype(BF16)


def dot(a, b):
    return jnp.dot(a, b, preferred_element_type=F32)


def dot3(a, b):
    return dot(a[0], b[0]) + (dot(a[0], b[1]) + dot(a[1], b[0]))


def iota(shape, dim):
    return lax.broadcasted_iota(jnp.int32, shape, dim)


def low_bits(value, size):
    assert size & (size - 1) == 0
    return value & (size - 1)


def over(value, size):
    assert size & (size - 1) == 0
    return value >> (size.bit_length() - 1)


def pick(index, values):
    out = jnp.zeros(index.shape, values[0].dtype)
    for at, value in enumerate(values):
        out = jnp.where(index == at, value, out)
    return out


def tiles(width):
    step = min(TILE, width)
    return [(at, min(step, width - at)) for at in range(0, width, step)]


def slice_weights(dims, sign, order_ref, table_ref, rows_ref):
    per, groups, zb, cells = dims
    ang = lax.axis_index("ang")
    for d in range(groups):
        group = lax.rem(ang + sign * d + groups, groups)
        for z in range(zb):
            for a in range(per):
                at = (d * zb + z) * per + a
                rows_ref[at:at + 1, :] = table_ref[pl.ds(order_ref[group * per + a], 1), :]
    wide = rows_ref[...]
    total = wide.shape[1]
    row_slice = low_bits(over(iota(wide.shape, 0), per), zb)
    lane_slice = over(iota(wide.shape, 1), cells)
    out = jnp.zeros_like(wide)
    for z in range(zb):
        shift = lax.rem(z * cells - ang * cells + total, total)
        here = jnp.logical_and(row_slice == z, lane_slice == z)
        out = jnp.where(here, pltpu.roll(wide, shift, 1), out)
    return out


def volume_pieces(dims, zdev, half, offset, width):
    odd = lax.rem(lax.axis_index("slab"), 2)
    zb = dims[2]
    for h in range(2):
        start = lax.rem(odd + h, 2) * half + offset
        for zp in range(zdev // zb):
            yield h, zp, slice(zp * zb, (zp + 1) * zb), pl.ds(pl.multiple_of(start, LANES), width)


def rays_kernel(dims, first, half, offset, width, *refs):
    per, groups, zb, cells = dims
    count = groups * SUBLANES
    if first:
        order_ref, start_ref, len_ref, table_ref, vol_ref, *refs = refs
    else:
        given_ref, vol_ref, *refs = refs
    outs, refs = refs[:2 * groups], refs[2 * groups:]
    if first:
        left_ref, buf, sems, table_buf, rows_ref, table_sem = refs
    else:
        buf, sems = refs
    zdev = vol_ref.shape[0]
    copies = {}
    if first:
        table_copy = pltpu.make_async_copy(table_ref, table_buf, table_sem)
        table_copy.start()
    for h, zp, slices, columns in volume_pieces(dims, zdev, half, offset, width):
        copies[h, zp] = pltpu.make_async_copy(
            vol_ref.at[slices, :, columns], buf.at[h, slices], sems.at[h, zp]
        )
        copies[h, zp].start()
    if first:
        shape = (zdev * per, LANES)
        angle, lane = low_bits(iota(shape, 0), per), iota(shape, 1)
        starts = pick(angle, [start_ref[0, a].astype(F32) for a in range(per)])
        lengths = pick(angle, [len_ref[0, a].astype(F32) for a in range(per)])
        for d in range(groups):
            foot = jnp.where(lane == 2 * d, starts, jnp.where(lane == 2 * d + 1, lengths, 0.0))
            for h in range(2):
                outs[h * groups + d][:, width:] = foot
        table_copy.wait()
        both = jnp.concatenate(split(slice_weights(dims, 1, order_ref, table_buf, rows_ref)), axis=0)
        left = jnp.concatenate([both, both], axis=1)
        left_ref[...] = left
    else:
        left = given_ref[...]
    for (h, zp), copy in copies.items():
        copy.wait()
        for at, size in tiles(width):
            columns = slice(at, at + size)
            parts = [split(buf[h, zp * zb + z, :, columns]) for z in range(zb)]
            product = dot(left, jnp.concatenate([p[0] for p in parts] + [p[1] for p in parts], axis=0))
            sums = product[:count] + product[count:]
            for d in range(groups):
                outs[h * groups + d][zp * SUBLANES:(zp + 1) * SUBLANES, columns] = (
                    sums[d * SUBLANES:(d + 1) * SUBLANES]
                )


def ray_sums(dims, chunk, offset, width, given, small, table, volume):
    per, groups, zb, cells = dims
    zdev, _, total = volume.shape
    first = chunk == 0
    count, all_cells = groups * SUBLANES, table.shape[1]
    out = jax.ShapeDtypeStruct((zdev * per, width + (LANES if first else 0)), F32)
    left = jax.ShapeDtypeStruct((2 * count, 2 * zb * cells), BF16)
    assert zb * cells == all_cells
    scratch = [pltpu.VMEM((2, zdev, cells, width), F32), pltpu.SemaphoreType.DMA((2, zdev // zb))]
    if first:
        scratch += [pltpu.VMEM(table.shape, F32), pltpu.VMEM((count, all_cells), F32), pltpu.SemaphoreType.DMA]
        args, specs = [*small, table, volume], [IN_SMEM] * 3 + [ANYWHERE, ANYWHERE]
        shapes = [out] * (2 * groups) + [left]
    else:
        args, specs = [given, volume], [IN_VMEM, ANYWHERE]
        shapes = [out] * (2 * groups)
    size = zdev * cells * width * 2
    return pl.pallas_call(
        functools.partial(rays_kernel, dims, first, total // 2, offset, width),
        in_specs=specs,
        out_specs=[IN_VMEM] * len(shapes),
        out_shape=shapes,
        scratch_shapes=scratch,
        compiler_params=pltpu.CompilerParams(vmem_limit_bytes=(58 if first else 50) * MIB),
        cost_estimate=pl.CostEstimate(flops=2 * size * 16, bytes_accessed=size * 4, transcendentals=0),
        name=f"ray_sums_{chunk}",
    )(*args)


def hat_weights(dims, zdev, start, length, row):
    per, groups, zb, cells = dims
    at = low_bits(iota(start.shape, 0), zdev * per)
    slice_at = over(at, zb * per) * zb + low_bits(over(at, per), zb)
    span = jnp.where(length > 0.0, length, 1.0) / zdev
    centre = start + (slice_at.astype(F32) + 0.5) * span
    hat = jnp.maximum(0.0, 1.0 - jnp.abs(row + 0.5 - centre) / span)
    return jnp.where(jnp.logical_and(row >= start, row < start + length), hat, 0.0)


def footprint_matrix(dims, zdev, rdev, foot):
    per = dims[0]
    rows = 2 * per * rdev
    slab = lax.axis_index("slab")
    sibling = slab + 1 - 2 * lax.rem(slab, 2)
    row_id = iota((1, rows), 1)
    row_slab = jnp.where(row_id < per * rdev, slab, sibling)
    row = (row_slab * rdev + low_bits(row_id, rdev)).astype(F32)
    shape = (foot.shape[0], rows)
    same_angle = low_bits(iota(shape, 0), per) == low_bits(over(iota(shape, 1), rdev), per)
    return jnp.where(same_angle, hat_weights(dims, zdev, foot[:, 0:1], foot[:, 1:2], row), 0.0)


def update_weights(dims, zdev, rdev, foot, order_ref, table_ref, rows_ref, out_ref):
    per, groups, zb, cells = dims
    count = groups * SUBLANES
    weights = slice_weights(dims, -1, order_ref, table_ref, rows_ref)
    window = -(-5 * rdev // LANES) * LANES
    row = ((lax.axis_index("slab") - 2) * rdev + iota((1, window), 1)).astype(F32)
    sums = [
        jnp.sum(hat_weights(dims, zdev, foot[:, 2 * d:2 * d + 1], foot[:, 2 * d + 1:2 * d + 2], row), axis=1, keepdims=True)
        for d in range(groups)
    ]
    pad = jnp.zeros((out_ref.shape[2] - 3 * count, weights.shape[1]), F32)
    for zp in range(zdev // zb):
        slices = jnp.concatenate([s[zp * SUBLANES:(zp + 1) * SUBLANES] for s in sums], axis=0)
        scaled = weights / jnp.sum(weights * slices, axis=0, keepdims=True)
        high = scaled.astype(BF16).astype(F32)
        stacked = jnp.concatenate([high, high, scaled - high, pad], axis=0)
        out_ref[zp] = stacked.T.astype(BF16)


def residual_kernel(dims, first, last, half, rdev, zdev, offset, width, *refs):
    per, groups, zb, cells = dims
    block = zdev * per
    if first or last:
        order_ref, table_ref, *refs = refs
    if last:
        foot_ref, *refs = refs
    if not first:
        mats, inverse_ref, refs = refs[:4], refs[4], refs[5:]
    sums_refs, (mine_ref, theirs_ref), refs = refs[:3], refs[3:5], refs[5:]
    mine_out, sent_out, *refs = refs
    outs, refs = refs[:3], refs[3:]
    if first:
        foot = jnp.concatenate([r[i, :, width:] for r in sums_refs for i in range(2)], axis=0)
        refs[5][...] = sums_refs[0][0, :, width:]
        kernel = footprint_matrix(dims, zdev, rdev, foot)
        count, rows = kernel.shape
        kernel_t = kernel.T
        cover = jnp.sum(kernel_t, axis=1, keepdims=True)
        angle = low_bits(over(iota((rows, 1), 0), rdev), per)
        path = jnp.zeros((rows, 1), F32)
        for a in range(per):
            at = order_ref[lax.axis_index("ang") * per + a]
            path = jnp.where(angle == a, jnp.sum(table_ref[pl.ds(at, 1), :], axis=1, keepdims=True), path)
        inverse = 1.0 / jnp.maximum(path * cover, 0.25)
        ahead, back = split(kernel_t), split(kernel)
        for ref, value in zip(refs, (*ahead, *back)):
            ref[...] = value
        refs[4][...] = jnp.broadcast_to(inverse, (rows, LANES))
    else:
        ahead, back = (mats[0][...], mats[1][...]), (mats[2][...], mats[3][...])
        inverse = inverse_ref[:, 0:1]
    start = lax.rem(lax.axis_index("slab"), 2) * half + offset
    for at, size in tiles(width):
        columns = slice(at, at + size)
        mine = mine_ref[:, :, pl.ds(pl.multiple_of(start + at, LANES), size)].astype(F32)
        theirs = theirs_ref[:, :, offset + at:offset + at + size]
        measured = jnp.concatenate([m.reshape(per * rdev, size) for m in (mine, theirs)], axis=0)
        sums = jnp.concatenate([r[i, :, columns] for r in sums_refs for i in range(2)], axis=0)
        residual = (measured - dot3(ahead, split(sums))) * inverse
        mine_out[:, :, columns] = residual[:per * rdev].reshape(per, rdev, size)
        sent_out[:, :, columns] = residual[per * rdev:].reshape(per, rdev, size)
        given = dot3(back, split(residual))
        for i, ref in enumerate(outs):
            for j in range(2):
                ref[j, :, columns] = given[(2 * i + j) * block:(2 * i + j + 1) * block]
    if last:
        update_weights(dims, zdev, rdev, foot_ref[...], order_ref, table_ref, refs[1], refs[0])


def residual_step(dims, zdev, chunk, offset, width, mats, order, table, sums, measured, theirs):
    per, groups, zb, cells = dims
    _, rdev, total = measured.shape
    first = chunk == 0
    block = zdev * per
    count, rows = 6 * block, 2 * per * rdev
    last = chunk == CHUNKS - 1
    assert not (first and last)
    given = jax.ShapeDtypeStruct((2, block, width), F32)
    piece = jax.ShapeDtypeStruct((per, rdev, width), F32)
    shapes = [piece, piece, given, given, given]
    args, specs, scratch = [], [], []
    if first or last:
        args, specs = [order, table], [IN_SMEM, IN_VMEM]
    if last:
        depth = -(-3 * groups * SUBLANES // LANES) * LANES
        shapes.append(jax.ShapeDtypeStruct((zdev // zb, zb * cells, depth), BF16))
        scratch.append(pltpu.VMEM((groups * SUBLANES, table.shape[1]), F32))
        args += [mats[5]]
        specs += [IN_VMEM]
    if first:
        ahead, back = jax.ShapeDtypeStruct((rows, count), BF16), jax.ShapeDtypeStruct((count, rows), BF16)
        shapes += [ahead, ahead, back, back, jax.ShapeDtypeStruct((rows, LANES), F32)]
        shapes += [jax.ShapeDtypeStruct((block, LANES), F32)]
    else:
        args += mats[:5]
        specs += [IN_VMEM] * 5
    args += [*sums, measured, theirs]
    specs += [IN_VMEM] * 5
    return pl.pallas_call(
        functools.partial(residual_kernel, dims, first, last, total // 2, rdev, zdev, offset, width),
        in_specs=specs,
        out_specs=[IN_VMEM] * len(shapes),
        out_shape=shapes,
        scratch_shapes=scratch,
        compiler_params=pltpu.CompilerParams(vmem_limit_bytes=16 * MIB),
        cost_estimate=pl.CostEstimate(
            flops=12 * count * rows * width, bytes_accessed=8 * width * (count + rows), transcendentals=0
        ),
        name=f"residual_{chunk}",
    )(*args)


def update_kernel(dims, first, half, offset, width, *refs):
    per, groups, zb, cells = dims
    count = groups * SUBLANES
    left_ref, backs, refs = refs[0], refs[1:1 + 2 * groups], refs[1 + 2 * groups:]
    backs = [backs[-1], *backs[groups:-1], *backs[:groups]]
    mine_ref, theirs_ref, vol_ref, *refs = refs
    if not first:
        refs = refs[2:]
    out_ref, res_ref, buf, sems, res_sems = refs
    zdev, _, depth = vol_ref.shape[0], cells, left_ref.shape[2]
    odd = lax.rem(lax.axis_index("slab"), 2)
    kept = []
    for h, ref in enumerate((mine_ref, theirs_ref)):
        start = pl.multiple_of(lax.rem(odd + h, 2) * half + offset, LANES)
        kept.append(pltpu.make_async_copy(ref, res_ref.at[:, :, pl.ds(start, width)], res_sems.at[h]))
    for h, zp, slices, columns in volume_pieces(dims, zdev, half, offset, width):
        rows = slice(zp * SUBLANES, (zp + 1) * SUBLANES)
        left = left_ref[zp]
        start = lax.rem(odd + h, 2) * half + offset
        for at, size in tiles(width):
            piece = slice(at, at + size)
            source = pl.ds(pl.multiple_of(start + at, LANES), size)
            back = jnp.concatenate([backs[h * groups + d][rows, piece] for d in range(groups)], axis=0)
            high, low = split(back)
            pad = jnp.zeros((depth - 3 * count, size), BF16)
            change = dot(left, jnp.concatenate([high, low, high, pad], axis=0))
            for z in range(zb):
                buf[h, zp * zb + z, :, piece] = (
                    vol_ref[zp * zb + z, :, source] + change[z * cells:(z + 1) * cells]
                )
        kept.append(pltpu.make_async_copy(buf.at[h, slices], out_ref.at[slices, :, columns], sems.at[h, zp]))
        kept[-1].start()
    for copy in kept[:2]:
        copy.start()
    for copy in kept:
        copy.wait()


def update_step(dims, chunk, offset, width, left, backs, mine, theirs, volume, out, res):
    per, groups, zb, cells = dims
    zdev, _, total = volume.shape
    first = chunk == 0
    args = [left, *backs[groups:], *backs[1:groups], backs[0], mine, theirs, volume]
    specs = [IN_VMEM] * len(args)
    shapes = [jax.ShapeDtypeStruct(volume.shape, F32), jax.ShapeDtypeStruct((*mine.shape[:2], total), F32)]
    aliases = {}
    if not first:
        aliases = {len(args): 0, len(args) + 1: 1}
        args += [out, res]
        specs += [ANYWHERE, ANYWHERE]
    size = zdev * cells * width * 2
    return pl.pallas_call(
        functools.partial(update_kernel, dims, first, total // 2, offset, width),
        in_specs=specs,
        out_specs=[ANYWHERE, ANYWHERE],
        out_shape=shapes,
        scratch_shapes=[
            pltpu.VMEM((2, zdev, cells, width), F32),
            pltpu.SemaphoreType.DMA((2, zdev // zb)),
            pltpu.SemaphoreType.DMA((2,)),
        ],
        input_output_aliases=aliases,
        compiler_params=pltpu.CompilerParams(vmem_limit_bytes=20 * MIB),
        cost_estimate=pl.CostEstimate(flops=2 * size * 48, bytes_accessed=size * 8, transcendentals=0),
        name=f"update_{chunk}",
    )(*args)


def body(volume, measured, foot_start, foot_len, order, table):
    slabs, groups = lax.axis_size("slab"), lax.axis_size("ang")
    per, rdev, total = measured.shape
    zdev, cells, _ = volume.shape
    half = total // 2
    zb = SUBLANES // per
    dims = (per, groups, zb, cells)
    each = half // CHUNKS
    widths = [each - LANES] + [each] * (CHUNKS - 2) + [each + LANES]
    offsets = [sum(widths[:c]) for c in range(CHUNKS)]

    def along(value, to):
        pairs = [(s, to(s)) for s in range(slabs) if 0 <= to(s) < slabs]
        return lax.ppermute(value, "slab", pairs)

    def spread(value, other, d):
        if not (other or d):
            return value
        pairs = [
            (s * groups + a, (s ^ other) * groups + (a + d) % groups) for s in range(slabs) for a in range(groups)
        ]
        return lax.ppermute(value, ("slab", "ang"), pairs)

    def facing(s):
        return s ^ 2

    def beyond(s):
        return s - 4 if s & 2 else s + 4

    def back_from_beyond(s):
        return s + 4 if s & 2 else s - 4

    odd = lax.rem(lax.axis_index("slab"), 2)
    theirs = along(
        lax.dynamic_slice_in_dim(measured, (1 - odd) * half, half, 2).astype(F32), lambda s: s ^ 1
    )

    sums, left = [], None
    for c in range(CHUNKS):
        parts = ray_sums(
            dims, c, offsets[c], widths[c], left, (order, foot_start, foot_len), table, volume
        )
        if c == 0:
            left = parts[2 * groups]
        parts = [spread(parts[h * groups + d], h, d) for h in range(2) for d in range(groups)]
        own = jnp.stack([sum(parts[:groups]), sum(parts[groups:])])
        near = along(own, facing)
        far = along(near, beyond)
        sums.append((own, near, far))
    pieces, given, mats = [], [], None
    for c in range(CHUNKS):
        mine, piece, own, near, far, *rest = residual_step(
            dims, zdev, c, offsets[c], widths[c], mats, order, table, sums[c], measured, theirs
        )
        mats = rest if c == 0 else mats
        left = rest[0]
        pieces.append((mine, along(piece, lambda s: s ^ 1)))
        near = near + along(far, back_from_beyond)
        arrived = along(near, facing)
        halves = [own[i] + arrived[i] for i in range(2)]
        given.append([spread(halves[h], h, d) for h in range(2) for d in range(groups)])
    out, res = None, None
    for c in range(CHUNKS):
        out, res = update_step(dims, c, offsets[c], widths[c], left, given[c], *pieces[c], volume, out, res)
    return out, res


def solution(mesh):
    return jax.shard_map(
        body,
        mesh=mesh,
        in_specs=(
            P("slab", "ang", None),
            P("ang", "slab", None),
            P("slab", "ang"),
            P("slab", "ang"),
            P(),
            P(),
        ),
        out_specs=(P("slab", "ang", None), P("ang", "slab", None)),
        check_vma=False,
    )
```

```python
import functools

import jax
import jax.numpy as jnp
from jax import lax
from jax.experimental import pallas as pl
from jax.experimental.pallas import tpu as pltpu
from jax.sharding import PartitionSpec as P

F32, BF16 = jnp.float32, jnp.bfloat16
CHUNKS = 2
TILE = 512
LANES = 128
SUBLANES = 8
MIB = 1024 * 1024

IN_VMEM = pl.BlockSpec(memory_space=pltpu.VMEM)
IN_SMEM = pl.BlockSpec(memory_space=pltpu.SMEM)
ANYWHERE = pl.BlockSpec(memory_space=pl.ANY)


def split(value):
    high = value.astype(BF16)
    return high, (value - high.astype(F32)).astype(BF16)


def dot(a, b):
    return jnp.dot(a, b, preferred_element_type=F32)


def dot3(a, b):
    return dot(a[0], b[0]) + (dot(a[0], b[1]) + dot(a[1], b[0]))


def iota(shape, dim):
    return lax.broadcasted_iota(jnp.int32, shape, dim)


def low_bits(value, size):
    assert size & (size - 1) == 0
    return value & (size - 1)


def over(value, size):
    assert size & (size - 1) == 0
    return value >> (size.bit_length() - 1)


def pick(index, values):
    out = jnp.zeros(index.shape, values[0].dtype)
    for at, value in enumerate(values):
        out = jnp.where(index == at, value, out)
    return out


def tiles(width):
    step = min(TILE, width)
    return [(at, min(step, width - at)) for at in range(0, width, step)]


def slice_weights(dims, sign, order_ref, table_ref, rows_ref):
    per, groups, zb, cells = dims
    ang = lax.axis_index("ang")
    for d in range(groups):
        group = lax.rem(ang + sign * d + groups, groups)
        for z in range(zb):
            for a in range(per):
                at = (d * zb + z) * per + a
                rows_ref[at:at + 1, :] = table_ref[pl.ds(order_ref[group * per + a], 1), :]
    wide = rows_ref[...]
    total = wide.shape[1]
    row_slice = low_bits(over(iota(wide.shape, 0), per), zb)
    lane_slice = over(iota(wide.shape, 1), cells)
    out = jnp.zeros_like(wide)
    for z in range(zb):
        shift = lax.rem(z * cells - ang * cells + total, total)
        here = jnp.logical_and(row_slice == z, lane_slice == z)
        out = jnp.where(here, pltpu.roll(wide, shift, 1), out)
    return out


def volume_pieces(dims, zdev, half, offset):
    odd = lax.rem(lax.axis_index("slab"), 2)
    zb = dims[2]
    for h in range(2):
        start = pl.multiple_of(lax.rem(odd + h, 2) * half + offset, LANES)
        for zp in range(zdev // zb):
            yield h, zp, slice(zp * zb, (zp + 1) * zb), start


def rays_kernel(dims, first, last, half, offset, width, *refs):
    per, groups, zb, cells = dims
    count = groups * SUBLANES
    if first:
        order_ref, start_ref, len_ref, table_ref, vol_ref, *refs = refs
    else:
        given_ref, vol_ref, *refs = refs
    outs, refs = refs[:2 * groups], refs[2 * groups:]
    if first:
        left_ref, buf, sems, table_buf, rows_ref, table_sem = refs
    elif last:
        kept_ref, sems, rest_sems = refs
    else:
        buf, sems = refs
    zdev = vol_ref.shape[0]
    copies, rest = [], []
    if first:
        table_copy = pltpu.make_async_copy(table_ref, table_buf, table_sem)
        table_copy.start()
    for h, zp, slices, start in volume_pieces(dims, zdev, half, offset):
        columns = pl.ds(start, width)
        to = kept_ref.at[slices, :, columns] if last else buf.at[h, slices]
        copies.append((h, zp, start, pltpu.make_async_copy(vol_ref.at[slices, :, columns], to, sems.at[h, zp])))
        copies[-1][-1].start()
    if last:
        for h in range(2):
            columns = pl.ds(h * half, offset)
            rest.append(pltpu.make_async_copy(vol_ref.at[:, :, columns], kept_ref.at[:, :, columns], rest_sems.at[h]))
            rest[h].start()
    if first:
        shape = (zdev * per, LANES)
        angle, lane = low_bits(iota(shape, 0), per), iota(shape, 1)
        starts = pick(angle, [start_ref[0, a].astype(F32) for a in range(per)])
        lengths = pick(angle, [len_ref[0, a].astype(F32) for a in range(per)])
        for d in range(groups):
            foot = jnp.where(lane == 2 * d, starts, jnp.where(lane == 2 * d + 1, lengths, 0.0))
            for h in range(2):
                outs[h * groups + d][:, width:] = foot
        table_copy.wait()
        both = jnp.concatenate(split(slice_weights(dims, 1, order_ref, table_buf, rows_ref)), axis=0)
        left = jnp.concatenate([both, both], axis=1)
        left_ref[...] = left
    else:
        left = given_ref[...]
    for h, zp, start, copy in copies:
        copy.wait()
        for at, size in tiles(width):
            parts = []
            for z in range(zb):
                if last:
                    cells_at = kept_ref[zp * zb + z, :, pl.ds(pl.multiple_of(start + at, LANES), size)]
                else:
                    cells_at = buf[h, zp * zb + z, :, at:at + size]
                parts.append(split(cells_at))
            product = dot(left, jnp.concatenate([p[0] for p in parts] + [p[1] for p in parts], axis=0))
            sums = product[:count] + product[count:]
            for d in range(groups):
                outs[h * groups + d][zp * SUBLANES:(zp + 1) * SUBLANES, at:at + size] = (
                    sums[d * SUBLANES:(d + 1) * SUBLANES]
                )
    for copy in rest:
        copy.wait()


def ray_sums(dims, chunk, offset, width, given, small, table, volume):
    per, groups, zb, cells = dims
    zdev, _, total = volume.shape
    first, last = chunk == 0, chunk == CHUNKS - 1
    count, all_cells = groups * SUBLANES, table.shape[1]
    out = jax.ShapeDtypeStruct((zdev * per, width + (LANES if first else 0)), F32)
    left = jax.ShapeDtypeStruct((2 * count, 2 * zb * cells), BF16)
    assert zb * cells == all_cells and not (first and last)
    sems = pltpu.SemaphoreType.DMA((2, zdev // zb))
    shapes = [out] * (2 * groups)
    scratch = [pltpu.VMEM((2, zdev, cells, width), F32), sems]
    args, specs, limit = [given, volume], [IN_VMEM, ANYWHERE], 50
    if first:
        scratch += [pltpu.VMEM(table.shape, F32), pltpu.VMEM((count, all_cells), F32), pltpu.SemaphoreType.DMA]
        args, specs, limit = [*small, table, volume], [IN_SMEM] * 3 + [ANYWHERE, ANYWHERE], 58
        shapes += [left]
    if last:
        scratch = [sems, pltpu.SemaphoreType.DMA((2,))]
        shapes += [jax.ShapeDtypeStruct(volume.shape, F32)]
        limit = 28
    size = zdev * cells * width * 2
    return pl.pallas_call(
        functools.partial(rays_kernel, dims, first, last, total // 2, offset, width),
        in_specs=specs,
        out_specs=[IN_VMEM] * len(shapes),
        out_shape=shapes,
        scratch_shapes=scratch,
        compiler_params=pltpu.CompilerParams(vmem_limit_bytes=limit * MIB),
        cost_estimate=pl.CostEstimate(flops=2 * size * 16, bytes_accessed=size * 4, transcendentals=0),
        name=f"ray_sums_{chunk}",
    )(*args)


def hat_weights(dims, zdev, start, length, row):
    per, groups, zb, cells = dims
    at = low_bits(iota(start.shape, 0), zdev * per)
    slice_at = over(at, zb * per) * zb + low_bits(over(at, per), zb)
    span = jnp.where(length > 0.0, length, 1.0) / zdev
    centre = start + (slice_at.astype(F32) + 0.5) * span
    hat = jnp.maximum(0.0, 1.0 - jnp.abs(row + 0.5 - centre) / span)
    return jnp.where(jnp.logical_and(row >= start, row < start + length), hat, 0.0)


def footprint_matrix(dims, zdev, rdev, foot):
    per = dims[0]
    rows = 2 * per * rdev
    slab = lax.axis_index("slab")
    sibling = slab + 1 - 2 * lax.rem(slab, 2)
    row_id = iota((1, rows), 1)
    row_slab = jnp.where(row_id < per * rdev, slab, sibling)
    row = (row_slab * rdev + low_bits(row_id, rdev)).astype(F32)
    shape = (foot.shape[0], rows)
    same_angle = low_bits(iota(shape, 0), per) == low_bits(over(iota(shape, 1), rdev), per)
    beyond = slab + jnp.where(low_bits(slab, 4) < 2, -2, 2)
    there = jnp.logical_and(beyond >= 0, beyond < lax.axis_size("slab"))
    known = jnp.where(there, foot.shape[0], foot.shape[0] // 3 * 2)
    meets = jnp.logical_and(same_angle, iota(shape, 0) < known)
    return jnp.where(meets, hat_weights(dims, zdev, foot[:, 0:1], foot[:, 1:2], row), 0.0)


def update_weights(dims, zdev, rdev, foot, order_ref, table_ref, rows_ref, out_ref):
    per, groups, zb, cells = dims
    count = groups * SUBLANES
    weights = slice_weights(dims, -1, order_ref, table_ref, rows_ref)
    window = -(-5 * rdev // LANES) * LANES
    row = ((lax.axis_index("slab") - 2) * rdev + iota((1, window), 1)).astype(F32)
    sums = [
        jnp.sum(hat_weights(dims, zdev, foot[:, 2 * d:2 * d + 1], foot[:, 2 * d + 1:2 * d + 2], row), axis=1, keepdims=True)
        for d in range(groups)
    ]
    pad = jnp.zeros((out_ref.shape[2] - 3 * count, weights.shape[1]), F32)
    for zp in range(zdev // zb):
        slices = jnp.concatenate([s[zp * SUBLANES:(zp + 1) * SUBLANES] for s in sums], axis=0)
        scaled = weights / jnp.sum(weights * slices, axis=0, keepdims=True)
        high = scaled.astype(BF16).astype(F32)
        stacked = jnp.concatenate([high, high, scaled - high, pad], axis=0)
        out_ref[zp] = stacked.T.astype(BF16)


def residual_kernel(dims, first, last, half, rdev, zdev, offset, width, *refs):
    per, groups, zb, cells = dims
    block = zdev * per
    if first or last:
        order_ref, table_ref, *refs = refs
    if last:
        foot_ref, *refs = refs
    if not first:
        mats, inverse_ref, refs = refs[:4], refs[4], refs[5:]
    sums_refs, (mine_ref, theirs_ref), refs = refs[:3], refs[3:5], refs[5:]
    if not first:
        mine_before, sent_before, *refs = refs
    mine_out, sent_out, *refs = refs
    if not first:
        mine_out[:, :, :offset] = mine_before[...]
        sent_out[:, :, :offset] = sent_before[...]
    outs, refs = refs[:3], refs[3:]
    if first:
        foot = jnp.concatenate([r[i, :, width:] for r in sums_refs for i in range(2)], axis=0)
        refs[5][...] = sums_refs[0][0, :, width:]
        kernel = footprint_matrix(dims, zdev, rdev, foot)
        count, rows = kernel.shape
        kernel_t = kernel.T
        cover = jnp.sum(kernel_t, axis=1, keepdims=True)
        angle = low_bits(over(iota((rows, 1), 0), rdev), per)
        path = jnp.zeros((rows, 1), F32)
        for a in range(per):
            at = order_ref[lax.axis_index("ang") * per + a]
            path = jnp.where(angle == a, jnp.sum(table_ref[pl.ds(at, 1), :], axis=1, keepdims=True), path)
        inverse = 1.0 / jnp.maximum(path * cover, 0.25)
        ahead, back = split(kernel_t), split(kernel)
        for ref, value in zip(refs, (*ahead, *back)):
            ref[...] = value
        refs[4][...] = jnp.broadcast_to(inverse, (rows, LANES))
    else:
        ahead, back = (mats[0][...], mats[1][...]), (mats[2][...], mats[3][...])
        inverse = inverse_ref[:, 0:1]
    start = lax.rem(lax.axis_index("slab"), 2) * half + offset
    for at, size in tiles(width):
        columns = slice(at, at + size)
        mine = mine_ref[:, :, pl.ds(pl.multiple_of(start + at, LANES), size)].astype(F32)
        theirs = theirs_ref[:, :, offset + at:offset + at + size]
        measured = jnp.concatenate([m.reshape(per * rdev, size) for m in (mine, theirs)], axis=0)
        sums = jnp.concatenate([r[i, :, columns] for r in sums_refs for i in range(2)], axis=0)
        residual = (measured - dot3(ahead, split(sums))) * inverse
        placed = slice(offset + at, offset + at + size)
        mine_out[:, :, placed] = residual[:per * rdev].reshape(per, rdev, size)
        sent_out[:, :, placed] = residual[per * rdev:].reshape(per, rdev, size)
        given = dot3(back, split(residual))
        for i, ref in enumerate(outs):
            for j in range(2):
                ref[j, :, columns] = given[(2 * i + j) * block:(2 * i + j + 1) * block]
    if last:
        update_weights(dims, zdev, rdev, foot_ref[...], order_ref, table_ref, refs[1], refs[0])


def residual_step(dims, zdev, chunk, offset, width, mats, before, order, table, sums, measured, theirs):
    per, groups, zb, cells = dims
    _, rdev, total = measured.shape
    first = chunk == 0
    block = zdev * per
    count, rows = 6 * block, 2 * per * rdev
    last = chunk == CHUNKS - 1
    assert not (first and last)
    given = jax.ShapeDtypeStruct((2, block, width), F32)
    piece = jax.ShapeDtypeStruct((per, rdev, offset + width), F32)
    shapes = [piece, piece, given, given, given]
    args, specs, scratch = [], [], []
    if first or last:
        args, specs = [order, table], [IN_SMEM, IN_VMEM]
    if last:
        depth = -(-3 * groups * SUBLANES // LANES) * LANES
        shapes.append(jax.ShapeDtypeStruct((zdev // zb, zb * cells, depth), BF16))
        scratch.append(pltpu.VMEM((groups * SUBLANES, table.shape[1]), F32))
        args += [mats[5]]
        specs += [IN_VMEM]
    if first:
        ahead, back = jax.ShapeDtypeStruct((rows, count), BF16), jax.ShapeDtypeStruct((count, rows), BF16)
        shapes += [ahead, ahead, back, back, jax.ShapeDtypeStruct((rows, LANES), F32)]
        shapes += [jax.ShapeDtypeStruct((block, LANES), F32)]
    else:
        args += mats[:5]
        specs += [IN_VMEM] * 5
    args += [*sums, measured, theirs, *before]
    specs += [IN_VMEM] * (5 + len(before))
    return pl.pallas_call(
        functools.partial(residual_kernel, dims, first, last, total // 2, rdev, zdev, offset, width),
        in_specs=specs,
        out_specs=[IN_VMEM] * len(shapes),
        out_shape=shapes,
        scratch_shapes=scratch,
        compiler_params=pltpu.CompilerParams(vmem_limit_bytes=16 * MIB),
        cost_estimate=pl.CostEstimate(
            flops=12 * count * rows * width, bytes_accessed=8 * width * (count + rows), transcendentals=0
        ),
        name=f"residual_{chunk}",
    )(*args)


def update_kernel(dims, first, last, half, offset, width, *refs):
    per, groups, zb, cells = dims
    count = groups * SUBLANES
    left_ref, backs, vol_ref, refs = refs[0], refs[1:1 + 2 * groups], refs[1 + 2 * groups], refs[2 + 2 * groups:]
    backs = [backs[-1], *backs[groups:-1], *backs[:groups]]
    zdev, depth = vol_ref.shape[0], left_ref.shape[2]
    if last:
        pieces, refs = refs[:2], refs[2:]
    if not first:
        refs = refs[1:]
    if last:
        out_ref, res_ref, buf, sems, res_sems = refs
    else:
        out_ref, buf, sems = refs
    odd = lax.rem(lax.axis_index("slab"), 2)
    leaving = []
    for h, zp, slices, start in volume_pieces(dims, zdev, half, offset):
        rows = slice(zp * SUBLANES, (zp + 1) * SUBLANES)
        left = left_ref[zp]
        for at, size in tiles(width):
            piece = slice(at, at + size)
            source = pl.ds(pl.multiple_of(start + at, LANES), size)
            back = jnp.concatenate([backs[h * groups + d][rows, piece] for d in range(groups)], axis=0)
            high, low = split(back)
            pad = jnp.zeros((depth - 3 * count, size), BF16)
            change = dot(left, jnp.concatenate([high, low, high, pad], axis=0))
            for z in range(zb):
                buf[h, zp * zb + z, :, piece] = (
                    vol_ref[zp * zb + z, :, source] + change[z * cells:(z + 1) * cells]
                )
        leaving.append(
            pltpu.make_async_copy(buf.at[h, slices], out_ref.at[slices, :, pl.ds(start, width)], sems.at[h, zp])
        )
        leaving[-1].start()
    if last:
        for h, ref in enumerate(pieces):
            columns = pl.ds(pl.multiple_of(lax.rem(odd + h, 2) * half, LANES), half)
            leaving.append(pltpu.make_async_copy(ref, res_ref.at[:, :, columns], res_sems.at[h]))
            leaving[-1].start()
    for copy in leaving:
        copy.wait()


def update_step(dims, chunk, offset, width, left, backs, pieces, volume, out):
    per, groups, zb, cells = dims
    zdev, _, total = volume.shape
    first, last = chunk == 0, chunk == CHUNKS - 1
    args = [left, *backs[groups:], *backs[1:groups], backs[0], volume]
    shapes = [jax.ShapeDtypeStruct(volume.shape, F32)]
    scratch = [pltpu.VMEM((2, zdev, cells, width), F32), pltpu.SemaphoreType.DMA((2, zdev // zb))]
    if last:
        args += pieces
        shapes += [jax.ShapeDtypeStruct((*pieces[0].shape[:2], total), F32)]
        scratch += [pltpu.SemaphoreType.DMA((2,))]
    specs = [IN_VMEM] * len(args)
    aliases = {}
    if not first:
        aliases = {len(args): 0}
        args += [out]
        specs += [ANYWHERE]
    size = zdev * cells * width * 2
    return pl.pallas_call(
        functools.partial(update_kernel, dims, first, last, total // 2, offset, width),
        in_specs=specs,
        out_specs=[ANYWHERE] * len(shapes),
        out_shape=shapes,
        scratch_shapes=scratch,
        input_output_aliases=aliases,
        compiler_params=pltpu.CompilerParams(vmem_limit_bytes=20 * MIB),
        cost_estimate=pl.CostEstimate(flops=2 * size * 48, bytes_accessed=size * 4, transcendentals=0),
        name=f"update_{chunk}",
    )(*args)


def body(volume, measured, foot_start, foot_len, order, table):
    slabs, groups = lax.axis_size("slab"), lax.axis_size("ang")
    per, rdev, total = measured.shape
    zdev, cells, _ = volume.shape
    half = total // 2
    zb = SUBLANES // per
    dims = (per, groups, zb, cells)
    each = half // CHUNKS
    widths = [each - LANES] + [each] * (CHUNKS - 2) + [each + LANES]
    offsets = [sum(widths[:c]) for c in range(CHUNKS)]

    def along(value, to):
        pairs = [(s, to(s)) for s in range(slabs)]
        return lax.ppermute(value, "slab", pairs)

    def spread(value, other, d):
        if not (other or d):
            return value
        pairs = [
            (s * groups + a, (s ^ other) * groups + (a + d) % groups) for s in range(slabs) for a in range(groups)
        ]
        return lax.ppermute(value, ("slab", "ang"), pairs)

    def facing(s):
        return s ^ 2

    def within(to, s):
        return to if 0 <= to < slabs else facing(s)

    def beyond(s):
        return within(s - 4 if s & 2 else s + 4, s)

    def back_from_beyond(s):
        return within(s + 4 if s & 2 else s - 4, s)

    odd = lax.rem(lax.axis_index("slab"), 2)
    theirs = along(
        lax.dynamic_slice_in_dim(measured, (1 - odd) * half, half, 2).astype(F32), lambda s: s ^ 1
    )

    sums, left = [], None
    for c in range(CHUNKS):
        parts = ray_sums(
            dims, c, offsets[c], widths[c], left, (order, foot_start, foot_len), table, volume
        )
        if c == 0:
            left = parts[2 * groups]
        kept = parts[-1]
        parts = [spread(parts[h * groups + d], h, d) for h in range(2) for d in range(groups)]
        own = jnp.stack([sum(parts[:groups]), sum(parts[groups:])])
        near = along(own, facing)
        far = along(near, beyond)
        sums.append((own, near, far))
    pieces, given, mats = [], [], None
    for c in range(CHUNKS):
        mine, sent, own, near, far, *rest = residual_step(
            dims, zdev, c, offsets[c], widths[c], mats, pieces, order, table, sums[c], measured, theirs
        )
        pieces = [mine, sent]
        mats = rest if c == 0 else mats
        left = rest[0]
        near = near + along(far, back_from_beyond)
        arrived = along(near, facing)
        halves = [own[i] + arrived[i] for i in range(2)]
        given.append([spread(halves[h], h, d) for h in range(2) for d in range(groups)])
    pieces = [mine, along(sent, lambda s: s ^ 1)]
    out = None
    for c in range(CHUNKS):
        out, *res = update_step(dims, c, offsets[c], widths[c], left, given[c], pieces, kept, out)
    return out, res[0]


def solution(mesh):
    return jax.shard_map(
        body,
        mesh=mesh,
        in_specs=(
            P("slab", "ang", None),
            P("ang", "slab", None),
            P("slab", "ang"),
            P("slab", "ang"),
            P(),
            P(),
        ),
        out_specs=(P("slab", "ang", None), P("ang", "slab", None)),
        check_vma=False,
    )
```

```python
import functools

import jax
import jax.numpy as jnp
from jax import lax
from jax.experimental import pallas as pl
from jax.experimental.pallas import tpu as pltpu
from jax.sharding import PartitionSpec as P

F32, BF16 = jnp.float32, jnp.bfloat16
CHUNKS = 2
TILE = 512
LANES = 128
SUBLANES = 8
MIB = 1024 * 1024

IN_VMEM = pl.BlockSpec(memory_space=pltpu.VMEM)
IN_SMEM = pl.BlockSpec(memory_space=pltpu.SMEM)
ANYWHERE = pl.BlockSpec(memory_space=pl.ANY)


def split(value):
    high = value.astype(BF16)
    return high, (value - high.astype(F32)).astype(BF16)


def dot(a, b):
    return jnp.dot(a, b, preferred_element_type=F32)


def dot3(a, b):
    return dot(a[0], b[0]) + (dot(a[0], b[1]) + dot(a[1], b[0]))


def iota(shape, dim):
    return lax.broadcasted_iota(jnp.int32, shape, dim)


def low_bits(value, size):
    assert size & (size - 1) == 0
    return value & (size - 1)


def over(value, size):
    assert size & (size - 1) == 0
    return value >> (size.bit_length() - 1)


def pick(index, values):
    out = jnp.zeros(index.shape, values[0].dtype)
    for at, value in enumerate(values):
        out = jnp.where(index == at, value, out)
    return out


def tiles(width):
    step = min(TILE, width)
    return [(at, min(step, width - at)) for at in range(0, width, step)]


def slice_weights(dims, sign, order_ref, table_ref, rows_ref):
    per, groups, zb, cells = dims
    ang = lax.axis_index("ang")
    for d in range(groups):
        group = lax.rem(ang + sign * d + groups, groups)
        for z in range(zb):
            for a in range(per):
                at = (d * zb + z) * per + a
                rows_ref[at:at + 1, :] = table_ref[pl.ds(order_ref[group * per + a], 1), :]
    wide = rows_ref[...]
    total = wide.shape[1]
    row_slice = low_bits(over(iota(wide.shape, 0), per), zb)
    lane_slice = over(iota(wide.shape, 1), cells)
    out = jnp.zeros_like(wide)
    for z in range(zb):
        shift = lax.rem(z * cells - ang * cells + total, total)
        here = jnp.logical_and(row_slice == z, lane_slice == z)
        out = jnp.where(here, pltpu.roll(wide, shift, 1), out)
    return out


def volume_pieces(dims, zdev, half, offset):
    odd = lax.rem(lax.axis_index("slab"), 2)
    zb = dims[2]
    for h in range(2):
        start = pl.multiple_of(lax.rem(odd + h, 2) * half + offset, LANES)
        for zp in range(zdev // zb):
            yield h, zp, slice(zp * zb, (zp + 1) * zb), start


def rays_kernel(dims, first, last, half, offset, width, *refs):
    per, groups, zb, cells = dims
    count = groups * SUBLANES
    if first:
        order_ref, start_ref, len_ref, table_ref, vol_ref, *refs = refs
    else:
        given_ref, vol_ref, *refs = refs
    outs, refs = refs[:2 * groups], refs[2 * groups:]
    if first:
        left_ref, buf, sems, table_buf, order_buf, start_buf, len_buf, rows_ref, small_sems = refs
    elif last:
        kept_ref, sems, rest_sems = refs
    else:
        buf, sems = refs
    zdev = vol_ref.shape[0]
    copies, rest = [], []
    if first:
        small = [
            pltpu.make_async_copy(source, to, small_sems.at[i])
            for i, (source, to) in enumerate(
                [(order_ref, order_buf), (table_ref, table_buf), (start_ref, start_buf), (len_ref, len_buf)]
            )
        ]
        for copy in small:
            copy.start()
    for h, zp, slices, start in volume_pieces(dims, zdev, half, offset):
        columns = pl.ds(start, width)
        to = kept_ref.at[slices, :, columns] if last else buf.at[h, slices]
        copies.append((h, zp, start, pltpu.make_async_copy(vol_ref.at[slices, :, columns], to, sems.at[h, zp])))
        copies[-1][-1].start()
    if last:
        for h in range(2):
            columns = pl.ds(h * half, offset)
            rest.append(pltpu.make_async_copy(vol_ref.at[:, :, columns], kept_ref.at[:, :, columns], rest_sems.at[h]))
            rest[h].start()
    if first:
        small[0].wait()
        small[1].wait()
        both = jnp.concatenate(split(slice_weights(dims, 1, order_buf, table_buf, rows_ref)), axis=0)
        left = jnp.concatenate([both, both], axis=1)
        left_ref[...] = left
        small[2].wait()
        small[3].wait()
        shape = (zdev * per, LANES)
        angle, lane = low_bits(iota(shape, 0), per), iota(shape, 1)
        starts = pick(angle, [start_buf[0, a].astype(F32) for a in range(per)])
        lengths = pick(angle, [len_buf[0, a].astype(F32) for a in range(per)])
        for d in range(groups):
            foot = jnp.where(lane == 2 * d, starts, jnp.where(lane == 2 * d + 1, lengths, 0.0))
            for h in range(2):
                outs[h * groups + d][:, width:] = foot
    else:
        left = given_ref[...]
    for h, zp, start, copy in copies:
        copy.wait()
        for at, size in tiles(width):
            parts = []
            for z in range(zb):
                if last:
                    cells_at = kept_ref[zp * zb + z, :, pl.ds(pl.multiple_of(start + at, LANES), size)]
                else:
                    cells_at = buf[h, zp * zb + z, :, at:at + size]
                parts.append(split(cells_at))
            product = dot(left, jnp.concatenate([p[0] for p in parts] + [p[1] for p in parts], axis=0))
            sums = product[:count] + product[count:]
            for d in range(groups):
                outs[h * groups + d][zp * SUBLANES:(zp + 1) * SUBLANES, at:at + size] = (
                    sums[d * SUBLANES:(d + 1) * SUBLANES]
                )
    for copy in rest:
        copy.wait()


def ray_sums(dims, chunk, offset, width, given, small, table, volume):
    per, groups, zb, cells = dims
    zdev, _, total = volume.shape
    first, last = chunk == 0, chunk == CHUNKS - 1
    count, all_cells = groups * SUBLANES, table.shape[1]
    out = jax.ShapeDtypeStruct((zdev * per, width + (LANES if first else 0)), F32)
    left = jax.ShapeDtypeStruct((2 * count, 2 * zb * cells), BF16)
    assert zb * cells == all_cells and not (first and last)
    sems = pltpu.SemaphoreType.DMA((2, zdev // zb))
    shapes = [out] * (2 * groups)
    scratch = [pltpu.VMEM((2, zdev, cells, width), F32), sems]
    args, specs, limit = [given, volume], [IN_VMEM, ANYWHERE], 50
    if first:
        scratch += [pltpu.VMEM(table.shape, F32)] + [pltpu.SMEM(a.shape, a.dtype) for a in small]
        scratch += [pltpu.VMEM((count, all_cells), F32), pltpu.SemaphoreType.DMA((4,))]
        args, specs, limit = [*small, table, volume], [ANYWHERE] * 5, 58
        shapes += [left]
    if last:
        scratch = [sems, pltpu.SemaphoreType.DMA((2,))]
        shapes += [jax.ShapeDtypeStruct(volume.shape, F32)]
        limit = 28
    size = zdev * cells * width * 2
    return pl.pallas_call(
        functools.partial(rays_kernel, dims, first, last, total // 2, offset, width),
        in_specs=specs,
        out_specs=[IN_VMEM] * len(shapes),
        out_shape=shapes,
        scratch_shapes=scratch,
        compiler_params=pltpu.CompilerParams(vmem_limit_bytes=limit * MIB),
        cost_estimate=pl.CostEstimate(flops=2 * size * 16, bytes_accessed=size * 4, transcendentals=0),
        name=f"ray_sums_{chunk}",
    )(*args)


def hat_weights(dims, zdev, start, length, row):
    per, groups, zb, cells = dims
    at = low_bits(iota(start.shape, 0), zdev * per)
    slice_at = over(at, zb * per) * zb + low_bits(over(at, per), zb)
    span = jnp.where(length > 0.0, length, 1.0) / zdev
    centre = start + (slice_at.astype(F32) + 0.5) * span
    hat = jnp.maximum(0.0, 1.0 - jnp.abs(row + 0.5 - centre) / span)
    return jnp.where(jnp.logical_and(row >= start, row < start + length), hat, 0.0)


def footprint_matrix(dims, zdev, rdev, foot):
    per = dims[0]
    rows = 2 * per * rdev
    slab = lax.axis_index("slab")
    sibling = slab + 1 - 2 * lax.rem(slab, 2)
    row_id = iota((1, rows), 1)
    row_slab = jnp.where(row_id < per * rdev, slab, sibling)
    row = (row_slab * rdev + low_bits(row_id, rdev)).astype(F32)
    shape = (foot.shape[0], rows)
    same_angle = low_bits(iota(shape, 0), per) == low_bits(over(iota(shape, 1), rdev), per)
    beyond = slab + jnp.where(low_bits(slab, 4) < 2, -2, 2)
    there = jnp.logical_and(beyond >= 0, beyond < lax.axis_size("slab"))
    known = jnp.where(there, foot.shape[0], foot.shape[0] // 3 * 2)
    meets = jnp.logical_and(same_angle, iota(shape, 0) < known)
    return jnp.where(meets, hat_weights(dims, zdev, foot[:, 0:1], foot[:, 1:2], row), 0.0)


def update_weights(dims, zdev, rdev, foot, order_ref, table_ref, rows_ref, out_ref):
    per, groups, zb, cells = dims
    count = groups * SUBLANES
    weights = slice_weights(dims, -1, order_ref, table_ref, rows_ref)
    window = -(-5 * rdev // LANES) * LANES
    row = ((lax.axis_index("slab") - 2) * rdev + iota((1, window), 1)).astype(F32)
    sums = [
        jnp.sum(hat_weights(dims, zdev, foot[:, 2 * d:2 * d + 1], foot[:, 2 * d + 1:2 * d + 2], row), axis=1, keepdims=True)
        for d in range(groups)
    ]
    pad = jnp.zeros((out_ref.shape[2] - 3 * count, weights.shape[1]), F32)
    for zp in range(zdev // zb):
        slices = jnp.concatenate([s[zp * SUBLANES:(zp + 1) * SUBLANES] for s in sums], axis=0)
        scaled = weights / jnp.sum(weights * slices, axis=0, keepdims=True)
        high = scaled.astype(BF16).astype(F32)
        stacked = jnp.concatenate([high, high, scaled - high, pad], axis=0)
        out_ref[zp] = stacked.T.astype(BF16)


def residual_kernel(dims, first, last, half, rdev, zdev, offset, width, *refs):
    per, groups, zb, cells = dims
    block = zdev * per
    if first or last:
        order_ref, table_ref, *refs = refs
    if last:
        foot_ref, *refs = refs
    if not first:
        mats, inverse_ref, refs = refs[:4], refs[4], refs[5:]
    sums_refs, (mine_ref, theirs_ref), refs = refs[:3], refs[3:5], refs[5:]
    if not first:
        mine_before, sent_before, *refs = refs
    mine_out, sent_out, *refs = refs
    if not first:
        mine_out[:, :, :offset] = mine_before[...]
        sent_out[:, :, :offset] = sent_before[...]
    outs, refs = refs[:3], refs[3:]
    if first:
        foot = jnp.concatenate([r[i, :, width:] for r in sums_refs for i in range(2)], axis=0)
        refs[5][...] = sums_refs[0][0, :, width:]
        kernel = footprint_matrix(dims, zdev, rdev, foot)
        count, rows = kernel.shape
        kernel_t = kernel.T
        cover = jnp.sum(kernel_t, axis=1, keepdims=True)
        angle = low_bits(over(iota((rows, 1), 0), rdev), per)
        path = jnp.zeros((rows, 1), F32)
        for a in range(per):
            at = order_ref[lax.axis_index("ang") * per + a]
            path = jnp.where(angle == a, jnp.sum(table_ref[pl.ds(at, 1), :], axis=1, keepdims=True), path)
        inverse = 1.0 / jnp.maximum(path * cover, 0.25)
        ahead, back = split(kernel_t), split(kernel)
        for ref, value in zip(refs, (*ahead, *back)):
            ref[...] = value
        refs[4][...] = jnp.broadcast_to(inverse, (rows, LANES))
    else:
        ahead, back = (mats[0][...], mats[1][...]), (mats[2][...], mats[3][...])
        inverse = inverse_ref[:, 0:1]
    start = lax.rem(lax.axis_index("slab"), 2) * half + offset
    for at, size in tiles(width):
        columns = slice(at, at + size)
        mine = mine_ref[:, :, pl.ds(pl.multiple_of(start + at, LANES), size)].astype(F32)
        theirs = theirs_ref[:, :, offset + at:offset + at + size]
        measured = jnp.concatenate([m.reshape(per * rdev, size) for m in (mine, theirs)], axis=0)
        sums = jnp.concatenate([r[i, :, columns] for r in sums_refs for i in range(2)], axis=0)
        residual = (measured - dot3(ahead, split(sums))) * inverse
        placed = slice(offset + at, offset + at + size)
        mine_out[:, :, placed] = residual[:per * rdev].reshape(per, rdev, size)
        sent_out[:, :, placed] = residual[per * rdev:].reshape(per, rdev, size)
        given = dot3(back, split(residual))
        for i, ref in enumerate(outs):
            for j in range(2):
                ref[j, :, columns] = given[(2 * i + j) * block:(2 * i + j + 1) * block]
    if last:
        update_weights(dims, zdev, rdev, foot_ref[...], order_ref, table_ref, refs[1], refs[0])


def residual_step(dims, zdev, chunk, offset, width, mats, before, order, table, sums, measured, theirs):
    per, groups, zb, cells = dims
    _, rdev, total = measured.shape
    first = chunk == 0
    block = zdev * per
    count, rows = 6 * block, 2 * per * rdev
    last = chunk == CHUNKS - 1
    assert not (first and last)
    given = jax.ShapeDtypeStruct((2, block, width), F32)
    piece = jax.ShapeDtypeStruct((per, rdev, offset + width), F32)
    shapes = [piece, piece, given, given, given]
    args, specs, scratch = [], [], []
    if first or last:
        args, specs = [order, table], [IN_SMEM, IN_VMEM]
    if last:
        depth = -(-3 * groups * SUBLANES // LANES) * LANES
        shapes.append(jax.ShapeDtypeStruct((zdev // zb, zb * cells, depth), BF16))
        scratch.append(pltpu.VMEM((groups * SUBLANES, table.shape[1]), F32))
        args += [mats[5]]
        specs += [IN_VMEM]
    if first:
        ahead, back = jax.ShapeDtypeStruct((rows, count), BF16), jax.ShapeDtypeStruct((count, rows), BF16)
        shapes += [ahead, ahead, back, back, jax.ShapeDtypeStruct((rows, LANES), F32)]
        shapes += [jax.ShapeDtypeStruct((block, LANES), F32)]
    else:
        args += mats[:5]
        specs += [IN_VMEM] * 5
    args += [*sums, measured, theirs, *before]
    specs += [IN_VMEM] * (5 + len(before))
    return pl.pallas_call(
        functools.partial(residual_kernel, dims, first, last, total // 2, rdev, zdev, offset, width),
        in_specs=specs,
        out_specs=[IN_VMEM] * len(shapes),
        out_shape=shapes,
        scratch_shapes=scratch,
        compiler_params=pltpu.CompilerParams(vmem_limit_bytes=16 * MIB),
        cost_estimate=pl.CostEstimate(
            flops=12 * count * rows * width, bytes_accessed=8 * width * (count + rows), transcendentals=0
        ),
        name=f"residual_{chunk}",
    )(*args)


def update_kernel(dims, first, last, half, offset, width, *refs):
    per, groups, zb, cells = dims
    count = groups * SUBLANES
    left_ref, backs, vol_ref, refs = refs[0], refs[1:1 + 2 * groups], refs[1 + 2 * groups], refs[2 + 2 * groups:]
    backs = [backs[-1], *backs[groups:-1], *backs[:groups]]
    zdev, depth = vol_ref.shape[0], left_ref.shape[2]
    if last:
        pieces, refs = refs[:2], refs[2:]
    if not first:
        refs = refs[1:]
    if last:
        out_ref, res_ref, buf, sems, res_sems = refs
    else:
        out_ref, buf, sems = refs
    odd = lax.rem(lax.axis_index("slab"), 2)
    leaving = []
    for h, zp, slices, start in volume_pieces(dims, zdev, half, offset):
        rows = slice(zp * SUBLANES, (zp + 1) * SUBLANES)
        left = left_ref[zp]
        for at, size in tiles(width):
            piece = slice(at, at + size)
            source = pl.ds(pl.multiple_of(start + at, LANES), size)
            back = jnp.concatenate([backs[h * groups + d][rows, piece] for d in range(groups)], axis=0)
            high, low = split(back)
            pad = jnp.zeros((depth - 3 * count, size), BF16)
            change = dot(left, jnp.concatenate([high, low, high, pad], axis=0))
            for z in range(zb):
                buf[h, zp * zb + z, :, piece] = (
                    vol_ref[zp * zb + z, :, source] + change[z * cells:(z + 1) * cells]
                )
        leaving.append(
            pltpu.make_async_copy(buf.at[h, slices], out_ref.at[slices, :, pl.ds(start, width)], sems.at[h, zp])
        )
        leaving[-1].start()
    if last:
        for h, ref in enumerate(pieces):
            columns = pl.ds(pl.multiple_of(lax.rem(odd + h, 2) * half, LANES), half)
            leaving.append(pltpu.make_async_copy(ref, res_ref.at[:, :, columns], res_sems.at[h]))
            leaving[-1].start()
    for copy in leaving:
        copy.wait()


def update_step(dims, chunk, offset, width, left, backs, pieces, volume, out):
    per, groups, zb, cells = dims
    zdev, _, total = volume.shape
    first, last = chunk == 0, chunk == CHUNKS - 1
    args = [left, *backs[groups:], *backs[1:groups], backs[0], volume]
    shapes = [jax.ShapeDtypeStruct(volume.shape, F32)]
    scratch = [pltpu.VMEM((2, zdev, cells, width), F32), pltpu.SemaphoreType.DMA((2, zdev // zb))]
    if last:
        args += pieces
        shapes += [jax.ShapeDtypeStruct((*pieces[0].shape[:2], total), F32)]
        scratch += [pltpu.SemaphoreType.DMA((2,))]
    specs = [IN_VMEM] * len(args)
    aliases = {}
    if not first:
        aliases = {len(args): 0}
        args += [out]
        specs += [ANYWHERE]
    size = zdev * cells * width * 2
    return pl.pallas_call(
        functools.partial(update_kernel, dims, first, last, total // 2, offset, width),
        in_specs=specs,
        out_specs=[ANYWHERE] * len(shapes),
        out_shape=shapes,
        scratch_shapes=scratch,
        input_output_aliases=aliases,
        compiler_params=pltpu.CompilerParams(vmem_limit_bytes=20 * MIB),
        cost_estimate=pl.CostEstimate(flops=2 * size * 48, bytes_accessed=size * 4, transcendentals=0),
        name=f"update_{chunk}",
    )(*args)


def body(volume, measured, foot_start, foot_len, order, table):
    slabs, groups = lax.axis_size("slab"), lax.axis_size("ang")
    per, rdev, total = measured.shape
    zdev, cells, _ = volume.shape
    half = total // 2
    zb = SUBLANES // per
    dims = (per, groups, zb, cells)
    each = half // CHUNKS
    widths = [each - LANES] + [each] * (CHUNKS - 2) + [each + LANES]
    offsets = [sum(widths[:c]) for c in range(CHUNKS)]

    def along(value, to):
        pairs = [(s, to(s)) for s in range(slabs)]
        return lax.ppermute(value, "slab", pairs)

    def spread(value, other, d):
        if not (other or d):
            return value
        pairs = [
            (s * groups + a, (s ^ other) * groups + (a + d) % groups) for s in range(slabs) for a in range(groups)
        ]
        return lax.ppermute(value, ("slab", "ang"), pairs)

    def facing(s):
        return s ^ 2

    def step(up, busy):
        def to(s):
            there = s + 4 if up(s) else s - 4
            if 0 <= there < slabs:
                return there
            return there % slabs if busy else facing(s)
        return to

    def beyond(c):
        return step(lambda s: not s & 2, c < CHUNKS - 1)

    def back_from_beyond(c):
        return step(lambda s: s & 2, c > 0)

    odd = lax.rem(lax.axis_index("slab"), 2)
    theirs = along(
        lax.dynamic_slice_in_dim(measured, (1 - odd) * half, half, 2).astype(F32), lambda s: s ^ 1
    )

    sums, left = [], None
    for c in range(CHUNKS):
        parts = ray_sums(
            dims, c, offsets[c], widths[c], left, (order, foot_start, foot_len), table, volume
        )
        if c == 0:
            left = parts[2 * groups]
        kept = parts[-1]
        parts = [spread(parts[h * groups + d], h, d) for h in range(2) for d in range(groups)]
        own = jnp.stack([sum(parts[:groups]), sum(parts[groups:])])
        near = along(own, facing)
        far = along(near, beyond(c))
        sums.append((own, near, far))
    pieces, given, mats = [], [], None
    for c in range(CHUNKS):
        mine, sent, own, near, far, *rest = residual_step(
            dims, zdev, c, offsets[c], widths[c], mats, pieces, order, table, sums[c], measured, theirs
        )
        pieces = [mine, sent]
        mats = rest if c == 0 else mats
        left = rest[0]
        near = near + along(far, back_from_beyond(c))
        arrived = along(near, facing)
        halves = [own[i] + arrived[i] for i in range(2)]
        given.append([spread(halves[h], h, d) for h in range(2) for d in range(groups)])
    pieces = [mine, along(sent, lambda s: s ^ 1)]
    out = None
    for c in range(CHUNKS):
        out, *res = update_step(dims, c, offsets[c], widths[c], left, given[c], pieces, kept, out)
    return out, res[0]


def solution(mesh):
    return jax.shard_map(
        body,
        mesh=mesh,
        in_specs=(
            P("slab", "ang", None),
            P("ang", "slab", None),
            P("slab", "ang"),
            P("slab", "ang"),
            P(),
            P(),
        ),
        out_specs=(P("slab", "ang", None), P("ang", "slab", None)),
        check_vma=False,
    )
```

```python
import functools

import jax
import jax.numpy as jnp
from jax import lax
from jax.experimental import pallas as pl
from jax.experimental.pallas import tpu as pltpu
from jax.sharding import PartitionSpec as P

F32, BF16 = jnp.float32, jnp.bfloat16
CHUNKS = 2
TILE = 512
LANES = 128
SUBLANES = 8
MIB = 1024 * 1024

IN_VMEM = pl.BlockSpec(memory_space=pltpu.VMEM)
IN_SMEM = pl.BlockSpec(memory_space=pltpu.SMEM)
ANYWHERE = pl.BlockSpec(memory_space=pl.ANY)


def split(value):
    high = value.astype(BF16)
    return high, (value - high.astype(F32)).astype(BF16)


def dot(a, b):
    return jnp.dot(a, b, preferred_element_type=F32)


def dot3(a, b):
    return dot(a[0], b[0]) + (dot(a[0], b[1]) + dot(a[1], b[0]))


def iota(shape, dim):
    return lax.broadcasted_iota(jnp.int32, shape, dim)


def low_bits(value, size):
    assert size & (size - 1) == 0
    return value & (size - 1)


def over(value, size):
    assert size & (size - 1) == 0
    return value >> (size.bit_length() - 1)


def pick(index, values):
    out = jnp.zeros(index.shape, values[0].dtype)
    for at, value in enumerate(values):
        out = jnp.where(index == at, value, out)
    return out


def tiles(width):
    step = min(TILE, width)
    return [(at, min(step, width - at)) for at in range(0, width, step)]


def slice_weights(dims, sign, order_ref, table_ref, rows_ref):
    per, groups, zb, cells = dims
    ang = lax.axis_index("ang")
    for d in range(groups):
        group = lax.rem(ang + sign * d + groups, groups)
        for z in range(zb):
            for a in range(per):
                at = (d * zb + z) * per + a
                rows_ref[at:at + 1, :] = table_ref[pl.ds(order_ref[group * per + a], 1), :]
    wide = rows_ref[...]
    total = wide.shape[1]
    row_slice = low_bits(over(iota(wide.shape, 0), per), zb)
    lane_slice = over(iota(wide.shape, 1), cells)
    out = jnp.zeros_like(wide)
    for z in range(zb):
        shift = lax.rem(z * cells - ang * cells + total, total)
        here = jnp.logical_and(row_slice == z, lane_slice == z)
        out = jnp.where(here, pltpu.roll(wide, shift, 1), out)
    return out


def volume_pieces(dims, zdev, half, offset):
    odd = lax.rem(lax.axis_index("slab"), 2)
    zb = dims[2]
    for h in range(2):
        start = pl.multiple_of(lax.rem(odd + h, 2) * half + offset, LANES)
        for zp in range(zdev // zb):
            yield h, zp, slice(zp * zb, (zp + 1) * zb), start


def rays_kernel(dims, first, half, offset, width, *refs):
    per, groups, zb, cells = dims
    count = groups * SUBLANES
    if first:
        order_ref, start_ref, len_ref, table_ref, vol_ref, *refs = refs
    else:
        given_ref, vol_ref, *refs = refs
    outs, refs = refs[:2 * groups], refs[2 * groups:]
    if first:
        left_ref, buf, sems, table_buf, order_buf, start_buf, len_buf, rows_ref, small_sems = refs
    else:
        buf, sems = refs
    zdev = vol_ref.shape[0]
    copies = []
    if first:
        small = [
            pltpu.make_async_copy(source, to, small_sems.at[i])
            for i, (source, to) in enumerate(
                [(order_ref, order_buf), (table_ref, table_buf), (start_ref, start_buf), (len_ref, len_buf)]
            )
        ]
        for copy in small:
            copy.start()
    for h, zp, slices, start in volume_pieces(dims, zdev, half, offset):
        source = vol_ref.at[slices, :, pl.ds(start, width)]
        copies.append((h, zp, pltpu.make_async_copy(source, buf.at[h, slices], sems.at[h, zp])))
        copies[-1][-1].start()
    if first:
        small[0].wait()
        small[1].wait()
        both = jnp.concatenate(split(slice_weights(dims, 1, order_buf, table_buf, rows_ref)), axis=0)
        left = jnp.concatenate([both, both], axis=1)
        left_ref[...] = left
        small[2].wait()
        small[3].wait()
        shape = (zdev * per, LANES)
        angle, lane = low_bits(iota(shape, 0), per), iota(shape, 1)
        starts = pick(angle, [start_buf[0, a].astype(F32) for a in range(per)])
        lengths = pick(angle, [len_buf[0, a].astype(F32) for a in range(per)])
        for d in range(groups):
            foot = jnp.where(lane == 2 * d, starts, jnp.where(lane == 2 * d + 1, lengths, 0.0))
            for h in range(2):
                outs[h * groups + d][:, width:] = foot
    else:
        left = given_ref[...]
    for h, zp, copy in copies:
        copy.wait()
        for at, size in tiles(width):
            parts = [split(buf[h, zp * zb + z, :, at:at + size]) for z in range(zb)]
            product = dot(left, jnp.concatenate([p[0] for p in parts] + [p[1] for p in parts], axis=0))
            sums = product[:count] + product[count:]
            for d in range(groups):
                outs[h * groups + d][zp * SUBLANES:(zp + 1) * SUBLANES, at:at + size] = (
                    sums[d * SUBLANES:(d + 1) * SUBLANES]
                )


def ray_sums(dims, chunk, offset, width, given, small, table, volume):
    per, groups, zb, cells = dims
    zdev, _, total = volume.shape
    first = chunk == 0
    count, all_cells = groups * SUBLANES, table.shape[1]
    out = jax.ShapeDtypeStruct((zdev * per, width + (LANES if first else 0)), F32)
    left = jax.ShapeDtypeStruct((2 * count, 2 * zb * cells), BF16)
    assert zb * cells == all_cells
    sems = pltpu.SemaphoreType.DMA((2, zdev // zb))
    shapes = [out] * (2 * groups)
    scratch = [pltpu.VMEM((2, zdev, cells, width), F32), sems]
    args, specs, limit = [given, volume], [IN_VMEM, ANYWHERE], 40
    if first:
        scratch += [pltpu.VMEM(table.shape, F32)] + [pltpu.SMEM(a.shape, a.dtype) for a in small]
        scratch += [pltpu.VMEM((count, all_cells), F32), pltpu.SemaphoreType.DMA((4,))]
        args, specs, limit = [*small, table, volume], [ANYWHERE] * 5, 58
        shapes += [left]
    if not first:
        scratch = [sems]
        shapes += [jax.ShapeDtypeStruct((2, zdev, cells, width), F32)]
    size = zdev * cells * width * 2
    return pl.pallas_call(
        functools.partial(rays_kernel, dims, first, total // 2, offset, width),
        in_specs=specs,
        out_specs=[IN_VMEM] * len(shapes),
        out_shape=shapes,
        scratch_shapes=scratch,
        compiler_params=pltpu.CompilerParams(vmem_limit_bytes=limit * MIB),
        cost_estimate=pl.CostEstimate(flops=2 * size * 16, bytes_accessed=size * 4, transcendentals=0),
        name=f"ray_sums_{chunk}",
    )(*args)


def hat_weights(dims, zdev, start, length, row):
    per, groups, zb, cells = dims
    at = low_bits(iota(start.shape, 0), zdev * per)
    slice_at = over(at, zb * per) * zb + low_bits(over(at, per), zb)
    span = jnp.where(length > 0.0, length, 1.0) / zdev
    centre = start + (slice_at.astype(F32) + 0.5) * span
    hat = jnp.maximum(0.0, 1.0 - jnp.abs(row + 0.5 - centre) / span)
    return jnp.where(jnp.logical_and(row >= start, row < start + length), hat, 0.0)


def footprint_matrix(dims, zdev, rdev, foot):
    per = dims[0]
    rows = 2 * per * rdev
    slab = lax.axis_index("slab")
    sibling = slab + 1 - 2 * lax.rem(slab, 2)
    row_id = iota((1, rows), 1)
    row_slab = jnp.where(row_id < per * rdev, slab, sibling)
    row = (row_slab * rdev + low_bits(row_id, rdev)).astype(F32)
    shape = (foot.shape[0], rows)
    same_angle = low_bits(iota(shape, 0), per) == low_bits(over(iota(shape, 1), rdev), per)
    beyond = slab + jnp.where(low_bits(slab, 4) < 2, -2, 2)
    there = jnp.logical_and(beyond >= 0, beyond < lax.axis_size("slab"))
    known = jnp.where(there, foot.shape[0], foot.shape[0] // 3 * 2)
    meets = jnp.logical_and(same_angle, iota(shape, 0) < known)
    return jnp.where(meets, hat_weights(dims, zdev, foot[:, 0:1], foot[:, 1:2], row), 0.0)


def update_weights(dims, zdev, rdev, foot, order_ref, table_ref, rows_ref, out_ref):
    per, groups, zb, cells = dims
    count = groups * SUBLANES
    weights = slice_weights(dims, -1, order_ref, table_ref, rows_ref)
    window = -(-5 * rdev // LANES) * LANES
    row = ((lax.axis_index("slab") - 2) * rdev + iota((1, window), 1)).astype(F32)
    sums = [
        jnp.sum(hat_weights(dims, zdev, foot[:, 2 * d:2 * d + 1], foot[:, 2 * d + 1:2 * d + 2], row), axis=1, keepdims=True)
        for d in range(groups)
    ]
    pad = jnp.zeros((out_ref.shape[2] - 3 * count, weights.shape[1]), F32)
    for zp in range(zdev // zb):
        slices = jnp.concatenate([s[zp * SUBLANES:(zp + 1) * SUBLANES] for s in sums], axis=0)
        scaled = weights / jnp.sum(weights * slices, axis=0, keepdims=True)
        high = scaled.astype(BF16).astype(F32)
        stacked = jnp.concatenate([high, high, scaled - high, pad], axis=0)
        out_ref[zp] = stacked.T.astype(BF16)


def residual_kernel(dims, first, last, half, rdev, zdev, offset, width, *refs):
    per, groups, zb, cells = dims
    block = zdev * per
    load = None
    if first or last:
        order_ref, table_ref, vol_ref, *refs, sem = refs
    if last:
        foot_ref, *refs = refs
    if not first:
        mats, inverse_ref, refs = refs[:4], refs[4], refs[5:]
    sums_refs, (mine_ref, theirs_ref), refs = refs[:3], refs[3:5], refs[5:]
    if not first:
        mine_before, sent_before, *refs = refs
    if first or last:
        kept_ref, *refs = refs
        start = lax.rem(lax.axis_index("slab") + (0 if first else 1), 2) * half
        columns = pl.ds(pl.multiple_of(start, LANES), kept_ref.shape[2])
        load = pltpu.make_async_copy(vol_ref.at[:, :, columns], kept_ref, sem)
        load.start()
    mine_out, sent_out, *refs = refs
    if not first:
        mine_out[:, :, :offset] = mine_before[...]
        sent_out[:, :, :offset] = sent_before[...]
    outs, refs = refs[:3], refs[3:]
    if first:
        foot = jnp.concatenate([r[i, :, width:] for r in sums_refs for i in range(2)], axis=0)
        refs[5][...] = sums_refs[0][0, :, width:]
        kernel = footprint_matrix(dims, zdev, rdev, foot)
        count, rows = kernel.shape
        kernel_t = kernel.T
        cover = jnp.sum(kernel_t, axis=1, keepdims=True)
        angle = low_bits(over(iota((rows, 1), 0), rdev), per)
        path = jnp.zeros((rows, 1), F32)
        for a in range(per):
            at = order_ref[lax.axis_index("ang") * per + a]
            path = jnp.where(angle == a, jnp.sum(table_ref[pl.ds(at, 1), :], axis=1, keepdims=True), path)
        inverse = 1.0 / jnp.maximum(path * cover, 0.25)
        ahead, back = split(kernel_t), split(kernel)
        for ref, value in zip(refs, (*ahead, *back)):
            ref[...] = value
        refs[4][...] = jnp.broadcast_to(inverse, (rows, LANES))
    else:
        ahead, back = (mats[0][...], mats[1][...]), (mats[2][...], mats[3][...])
        inverse = inverse_ref[:, 0:1]
    start = lax.rem(lax.axis_index("slab"), 2) * half + offset
    for at, size in tiles(width):
        columns = slice(at, at + size)
        mine = mine_ref[:, :, pl.ds(pl.multiple_of(start + at, LANES), size)].astype(F32)
        theirs = theirs_ref[:, :, offset + at:offset + at + size]
        measured = jnp.concatenate([m.reshape(per * rdev, size) for m in (mine, theirs)], axis=0)
        sums = jnp.concatenate([r[i, :, columns] for r in sums_refs for i in range(2)], axis=0)
        residual = (measured - dot3(ahead, split(sums))) * inverse
        placed = slice(offset + at, offset + at + size)
        mine_out[:, :, placed] = residual[:per * rdev].reshape(per, rdev, size)
        sent_out[:, :, placed] = residual[per * rdev:].reshape(per, rdev, size)
        given = dot3(back, split(residual))
        for i, ref in enumerate(outs):
            for j in range(2):
                ref[j, :, columns] = given[(2 * i + j) * block:(2 * i + j + 1) * block]
    if last:
        update_weights(dims, zdev, rdev, foot_ref[...], order_ref, table_ref, refs[1], refs[0])
    if load is not None:
        load.wait()


def residual_step(dims, chunk, offset, width, load_width, mats, before, order, table, volume, sums, measured, theirs):
    per, groups, zb, cells = dims
    zdev = volume.shape[0]
    _, rdev, total = measured.shape
    first = chunk == 0
    block = zdev * per
    count, rows = 6 * block, 2 * per * rdev
    last = chunk == CHUNKS - 1
    assert not (first and last)
    given = jax.ShapeDtypeStruct((2, block, width), F32)
    piece = jax.ShapeDtypeStruct((per, rdev, offset + width), F32)
    shapes = [piece, piece, given, given, given]
    args, specs, scratch = [], [], []
    if first or last:
        args, specs = [order, table, volume], [IN_SMEM, IN_VMEM, ANYWHERE]
        shapes = [jax.ShapeDtypeStruct((zdev, cells, load_width), F32)] + shapes
    if last:
        depth = -(-3 * groups * SUBLANES // LANES) * LANES
        shapes.append(jax.ShapeDtypeStruct((zdev // zb, zb * cells, depth), BF16))
        scratch.append(pltpu.VMEM((groups * SUBLANES, table.shape[1]), F32))
        args += [mats[5]]
        specs += [IN_VMEM]
    if first:
        ahead, back = jax.ShapeDtypeStruct((rows, count), BF16), jax.ShapeDtypeStruct((count, rows), BF16)
        shapes += [ahead, ahead, back, back, jax.ShapeDtypeStruct((rows, LANES), F32)]
        shapes += [jax.ShapeDtypeStruct((block, LANES), F32)]
    else:
        args += mats[:5]
        specs += [IN_VMEM] * 5
    if first or last:
        scratch.append(pltpu.SemaphoreType.DMA)
    args += [*sums, measured, theirs, *before]
    specs += [IN_VMEM] * (5 + len(before))
    return pl.pallas_call(
        functools.partial(residual_kernel, dims, first, last, total // 2, rdev, zdev, offset, width),
        in_specs=specs,
        out_specs=[IN_VMEM] * len(shapes),
        out_shape=shapes,
        scratch_shapes=scratch,
        compiler_params=pltpu.CompilerParams(vmem_limit_bytes=30 * MIB),
        cost_estimate=pl.CostEstimate(
            flops=12 * count * rows * width, bytes_accessed=8 * width * (count + rows), transcendentals=0
        ),
        name=f"residual_{chunk}",
    )(*args)


def update_kernel(dims, first, last, half, offset, width, *refs):
    per, groups, zb, cells = dims
    count = groups * SUBLANES
    left_ref, backs, refs = refs[0], refs[1:1 + 2 * groups], refs[1 + 2 * groups:]
    backs = [backs[-1], *backs[groups:-1], *backs[:groups]]
    if first:
        vols, refs = refs[:2], refs[2:]
    else:
        vols, refs = [refs[0].at[0], refs[0].at[1]], refs[1:]
    zdev, depth = vols[0].shape[0], left_ref.shape[2]
    if last:
        pieces, refs = refs[:2], refs[2:]
    if not first:
        refs = refs[1:]
    if last:
        out_ref, res_ref, buf, sems, res_sems = refs
    else:
        out_ref, buf, sems = refs
    odd = lax.rem(lax.axis_index("slab"), 2)
    leaving = []
    for h, zp, slices, start in volume_pieces(dims, zdev, half, offset):
        rows = slice(zp * SUBLANES, (zp + 1) * SUBLANES)
        left = left_ref[zp]
        for at, size in tiles(width):
            piece = slice(at, at + size)
            back = jnp.concatenate([backs[h * groups + d][rows, piece] for d in range(groups)], axis=0)
            high, low = split(back)
            pad = jnp.zeros((depth - 3 * count, size), BF16)
            change = dot(left, jnp.concatenate([high, low, high, pad], axis=0))
            for z in range(zb):
                buf[h, zp * zb + z, :, piece] = (
                    vols[h][zp * zb + z, :, piece] + change[z * cells:(z + 1) * cells]
                )
        leaving.append(
            pltpu.make_async_copy(buf.at[h, slices], out_ref.at[slices, :, pl.ds(start, width)], sems.at[h, zp])
        )
        leaving[-1].start()
    if last:
        for h, ref in enumerate(pieces):
            columns = pl.ds(pl.multiple_of(lax.rem(odd + h, 2) * half, LANES), half)
            leaving.append(pltpu.make_async_copy(ref, res_ref.at[:, :, columns], res_sems.at[h]))
            leaving[-1].start()
    for copy in leaving:
        copy.wait()


def update_step(dims, chunk, offset, width, left, backs, pieces, kept, volume, out):
    per, groups, zb, cells = dims
    zdev, _, total = volume.shape
    first, last = chunk == 0, chunk == CHUNKS - 1
    args = [left, *backs[groups:], *backs[1:groups], backs[0], *kept]
    shapes = [jax.ShapeDtypeStruct(volume.shape, F32)]
    scratch = [pltpu.VMEM((2, zdev, cells, width), F32), pltpu.SemaphoreType.DMA((2, zdev // zb))]
    if last:
        args += pieces
        shapes += [jax.ShapeDtypeStruct((*pieces[0].shape[:2], total), F32)]
        scratch += [pltpu.SemaphoreType.DMA((2,))]
    specs = [IN_VMEM] * len(args)
    aliases = {}
    if not first:
        aliases = {len(args): 0}
        args += [out]
        specs += [ANYWHERE]
    size = zdev * cells * width * 2
    return pl.pallas_call(
        functools.partial(update_kernel, dims, first, last, total // 2, offset, width),
        in_specs=specs,
        out_specs=[ANYWHERE] * len(shapes),
        out_shape=shapes,
        scratch_shapes=scratch,
        input_output_aliases=aliases,
        compiler_params=pltpu.CompilerParams(vmem_limit_bytes=20 * MIB),
        cost_estimate=pl.CostEstimate(flops=2 * size * 48, bytes_accessed=size * 4, transcendentals=0),
        name=f"update_{chunk}",
    )(*args)


def body(volume, measured, foot_start, foot_len, order, table):
    slabs, groups = lax.axis_size("slab"), lax.axis_size("ang")
    per, rdev, total = measured.shape
    zdev, cells, _ = volume.shape
    half = total // 2
    zb = SUBLANES // per
    dims = (per, groups, zb, cells)
    each = half // CHUNKS
    widths = [each - LANES] + [each + LANES]
    offsets = [sum(widths[:c]) for c in range(CHUNKS)]

    def along(value, to):
        pairs = [(s, to(s)) for s in range(slabs)]
        return lax.ppermute(value, "slab", pairs)

    def spread(value, other, d):
        if not (other or d):
            return value
        pairs = [
            (s * groups + a, (s ^ other) * groups + (a + d) % groups) for s in range(slabs) for a in range(groups)
        ]
        return lax.ppermute(value, ("slab", "ang"), pairs)

    def facing(s):
        return s ^ 2

    def step(up, busy):
        def to(s):
            there = s + 4 if up(s) else s - 4
            if 0 <= there < slabs:
                return there
            return there % slabs if busy else facing(s)
        return to

    def beyond(c):
        return step(lambda s: not s & 2, c < CHUNKS - 1)

    def back_from_beyond(c):
        return step(lambda s: s & 2, c > 0)

    odd = lax.rem(lax.axis_index("slab"), 2)
    theirs = along(
        lax.dynamic_slice_in_dim(measured, (1 - odd) * half, half, 2).astype(F32), lambda s: s ^ 1
    )

    sums, kept, left = [], [[] for _ in range(CHUNKS)], None
    for c in range(CHUNKS):
        parts = ray_sums(
            dims, c, offsets[c], widths[c], left, (order, foot_start, foot_len), table, volume
        )
        if c == 0:
            left = parts[2 * groups]
        else:
            kept[c].append(parts[2 * groups])
        parts = [spread(parts[h * groups + d], h, d) for h in range(2) for d in range(groups)]
        if c:
            parts, _ = lax.optimization_barrier((parts, sums[-1][0]))
        own = jnp.stack([sum(parts[:groups]), sum(parts[groups:])])
        near = along(own, facing)
        far = along(near, beyond(c))
        sums.append((own, near, far))
    pieces, given, mats = [], [], None
    for c in range(CHUNKS):
        loaded, mine, sent, own, near, far, *rest = residual_step(
            dims, c, offsets[c], widths[c], widths[0], mats, pieces, order, table, volume, sums[c], measured, theirs
        )
        kept[0].append(loaded)
        pieces = [mine, sent]
        mats = rest if c == 0 else mats
        left = rest[0]
        near = near + along(far, back_from_beyond(c))
        arrived = along(near, facing)
        halves = [own[i] + arrived[i] for i in range(2)]
        given.append([spread(halves[h], h, d) for h in range(2) for d in range(groups)])
    pieces = [mine, along(sent, lambda s: s ^ 1)]
    out = None
    for c in range(CHUNKS):
        out, *res = update_step(dims, c, offsets[c], widths[c], left, given[c], pieces, kept[c], volume, out)
    return out, res[0]


def solution(mesh):
    return jax.shard_map(
        body,
        mesh=mesh,
        in_specs=(
            P("slab", "ang", None),
            P("ang", "slab", None),
            P("slab", "ang"),
            P("slab", "ang"),
            P(),
            P(),
        ),
        out_specs=(P("slab", "ang", None), P("ang", "slab", None)),
        check_vma=False,
    )
```

```python
import functools

import jax
import jax.numpy as jnp
from jax import lax
from jax.experimental import pallas as pl
from jax.experimental.pallas import tpu as pltpu
from jax.sharding import PartitionSpec as P

F32, BF16 = jnp.float32, jnp.bfloat16
CHUNKS = 2
TILE = 512
LANES = 128
SUBLANES = 8
MIB = 1024 * 1024

IN_VMEM = pl.BlockSpec(memory_space=pltpu.VMEM)
IN_SMEM = pl.BlockSpec(memory_space=pltpu.SMEM)
ANYWHERE = pl.BlockSpec(memory_space=pl.ANY)


def split(value):
    high = value.astype(BF16)
    return high, (value - high.astype(F32)).astype(BF16)


def dot(a, b):
    return jnp.dot(a, b, preferred_element_type=F32)


def dot3(a, b):
    return dot(a[0], b[0]) + (dot(a[0], b[1]) + dot(a[1], b[0]))


def iota(shape, dim):
    return lax.broadcasted_iota(jnp.int32, shape, dim)


def low_bits(value, size):
    assert size & (size - 1) == 0
    return value & (size - 1)


def over(value, size):
    assert size & (size - 1) == 0
    return value >> (size.bit_length() - 1)


def pick(index, values):
    out = jnp.zeros(index.shape, values[0].dtype)
    for at, value in enumerate(values):
        out = jnp.where(index == at, value, out)
    return out


def tiles(width):
    step = min(TILE, width)
    return [(at, min(step, width - at)) for at in range(0, width, step)]


def slice_weights(dims, sign, order_ref, table_ref, rows_ref):
    per, groups, zb, cells = dims
    ang = lax.axis_index("ang")
    for d in range(groups):
        group = lax.rem(ang + sign * d + groups, groups)
        for z in range(zb):
            for a in range(per):
                at = (d * zb + z) * per + a
                rows_ref[at:at + 1, :] = table_ref[pl.ds(order_ref[group * per + a], 1), :]
    wide = rows_ref[...]
    total = wide.shape[1]
    row_slice = low_bits(over(iota(wide.shape, 0), per), zb)
    lane_slice = over(iota(wide.shape, 1), cells)
    out = jnp.zeros_like(wide)
    for z in range(zb):
        shift = lax.rem(z * cells - ang * cells + total, total)
        here = jnp.logical_and(row_slice == z, lane_slice == z)
        out = jnp.where(here, pltpu.roll(wide, shift, 1), out)
    return out


def volume_pieces(dims, zdev, half, offset):
    odd = lax.rem(lax.axis_index("slab"), 2)
    zb = dims[2]
    for h in range(2):
        start = pl.multiple_of(lax.rem(odd + h, 2) * half + offset, LANES)
        for zp in range(zdev // zb):
            yield h, zp, slice(zp * zb, (zp + 1) * zb), start


def rays_kernel(dims, first, half, offset, width, *refs):
    per, groups, zb, cells = dims
    count = groups * SUBLANES
    if first:
        order_ref, start_ref, len_ref, table_ref, vol_ref, *refs = refs
    else:
        given_ref, vol_ref, *refs = refs
    outs, refs = refs[:2 * groups], refs[2 * groups:]
    if first:
        left_ref, buf, sems, table_buf, order_buf, start_buf, len_buf, rows_ref, small_sems = refs
    else:
        buf, sems = refs
    zdev = vol_ref.shape[0]
    copies = []
    if first:
        small = [
            pltpu.make_async_copy(source, to, small_sems.at[i])
            for i, (source, to) in enumerate(
                [(order_ref, order_buf), (table_ref, table_buf), (start_ref, start_buf), (len_ref, len_buf)]
            )
        ]
        for copy in small:
            copy.start()
    for h, zp, slices, start in volume_pieces(dims, zdev, half, offset):
        source = vol_ref.at[slices, :, pl.ds(start, width)]
        copies.append((h, zp, pltpu.make_async_copy(source, buf.at[h, slices], sems.at[h, zp])))
        copies[-1][-1].start()
    if first:
        small[0].wait()
        small[1].wait()
        both = jnp.concatenate(split(slice_weights(dims, 1, order_buf, table_buf, rows_ref)), axis=0)
        left = jnp.concatenate([both, both], axis=1)
        left_ref[...] = left
        small[2].wait()
        small[3].wait()
        shape = (zdev * per, LANES)
        angle, lane = low_bits(iota(shape, 0), per), iota(shape, 1)
        starts = pick(angle, [start_buf[0, a].astype(F32) for a in range(per)])
        lengths = pick(angle, [len_buf[0, a].astype(F32) for a in range(per)])
        for d in range(groups):
            foot = jnp.where(lane == 2 * d, starts, jnp.where(lane == 2 * d + 1, lengths, 0.0))
            for h in range(2):
                outs[h * groups + d][:, width:] = foot
    else:
        left = given_ref[...]
    for h, zp, copy in copies:
        copy.wait()
        for at, size in tiles(width):
            parts = [split(buf[h, zp * zb + z, :, at:at + size]) for z in range(zb)]
            product = dot(left, jnp.concatenate([p[0] for p in parts] + [p[1] for p in parts], axis=0))
            sums = product[:count] + product[count:]
            for d in range(groups):
                outs[h * groups + d][zp * SUBLANES:(zp + 1) * SUBLANES, at:at + size] = (
                    sums[d * SUBLANES:(d + 1) * SUBLANES]
                )


def ray_sums(dims, chunk, offset, width, given, small, table, volume):
    per, groups, zb, cells = dims
    zdev, _, total = volume.shape
    first = chunk == 0
    count, all_cells = groups * SUBLANES, table.shape[1]
    out = jax.ShapeDtypeStruct((zdev * per, width + (LANES if first else 0)), F32)
    left = jax.ShapeDtypeStruct((2 * count, 2 * zb * cells), BF16)
    assert zb * cells == all_cells
    sems = pltpu.SemaphoreType.DMA((2, zdev // zb))
    shapes = [out] * (2 * groups)
    scratch = [pltpu.VMEM((2, zdev, cells, width), F32), sems]
    args, specs, limit = [given, volume], [IN_VMEM, ANYWHERE], 40
    if first:
        scratch += [pltpu.VMEM(table.shape, F32)] + [pltpu.SMEM(a.shape, a.dtype) for a in small]
        scratch += [pltpu.VMEM((count, all_cells), F32), pltpu.SemaphoreType.DMA((4,))]
        args, specs, limit = [*small, table, volume], [ANYWHERE] * 5, 58
        shapes += [left]
    if not first:
        scratch = [sems]
        shapes += [jax.ShapeDtypeStruct((2, zdev, cells, width), F32)]
    size = zdev * cells * width * 2
    return pl.pallas_call(
        functools.partial(rays_kernel, dims, first, total // 2, offset, width),
        in_specs=specs,
        out_specs=[IN_VMEM] * len(shapes),
        out_shape=shapes,
        scratch_shapes=scratch,
        compiler_params=pltpu.CompilerParams(vmem_limit_bytes=limit * MIB),
        cost_estimate=pl.CostEstimate(flops=2 * size * 16, bytes_accessed=size * 4, transcendentals=0),
        name=f"ray_sums_{chunk}",
    )(*args)


def hat_weights(dims, zdev, start, length, row):
    per, groups, zb, cells = dims
    at = low_bits(iota(start.shape, 0), zdev * per)
    slice_at = over(at, zb * per) * zb + low_bits(over(at, per), zb)
    span = jnp.where(length > 0.0, length, 1.0) / zdev
    centre = start + (slice_at.astype(F32) + 0.5) * span
    hat = jnp.maximum(0.0, 1.0 - jnp.abs(row + 0.5 - centre) / span)
    return jnp.where(jnp.logical_and(row >= start, row < start + length), hat, 0.0)


def footprint_matrix(dims, zdev, rdev, foot):
    per = dims[0]
    rows = 2 * per * rdev
    slab = lax.axis_index("slab")
    sibling = slab + 1 - 2 * lax.rem(slab, 2)
    row_id = iota((1, rows), 1)
    row_slab = jnp.where(row_id < per * rdev, slab, sibling)
    row = (row_slab * rdev + low_bits(row_id, rdev)).astype(F32)
    shape = (foot.shape[0], rows)
    same_angle = low_bits(iota(shape, 0), per) == low_bits(over(iota(shape, 1), rdev), per)
    beyond = slab + jnp.where(low_bits(slab, 4) < 2, -2, 2)
    there = jnp.logical_and(beyond >= 0, beyond < lax.axis_size("slab"))
    known = jnp.where(there, foot.shape[0], foot.shape[0] // 3 * 2)
    meets = jnp.logical_and(same_angle, iota(shape, 0) < known)
    return jnp.where(meets, hat_weights(dims, zdev, foot[:, 0:1], foot[:, 1:2], row), 0.0)


def update_weights(dims, zdev, rdev, foot, order_ref, table_ref, rows_ref, out_ref):
    per, groups, zb, cells = dims
    count = groups * SUBLANES
    weights = slice_weights(dims, -1, order_ref, table_ref, rows_ref)
    window = -(-5 * rdev // LANES) * LANES
    row = ((lax.axis_index("slab") - 2) * rdev + iota((1, window), 1)).astype(F32)
    sums = [
        jnp.sum(hat_weights(dims, zdev, foot[:, 2 * d:2 * d + 1], foot[:, 2 * d + 1:2 * d + 2], row), axis=1, keepdims=True)
        for d in range(groups)
    ]
    pad = jnp.zeros((out_ref.shape[2] - 3 * count, weights.shape[1]), F32)
    for zp in range(zdev // zb):
        slices = jnp.concatenate([s[zp * SUBLANES:(zp + 1) * SUBLANES] for s in sums], axis=0)
        scaled = weights / jnp.sum(weights * slices, axis=0, keepdims=True)
        high = scaled.astype(BF16).astype(F32)
        stacked = jnp.concatenate([high, high, scaled - high, pad], axis=0)
        out_ref[zp] = stacked.T.astype(BF16)


def residual_kernel(dims, first, last, half, rdev, zdev, offset, width, *refs):
    per, groups, zb, cells = dims
    block = zdev * per
    loads = []
    if first or last:
        order_ref, table_ref, vol_ref, *refs, sems = refs
    if last:
        foot_ref, *refs = refs
    if not first:
        mats, inverse_ref, refs = refs[:4], refs[4], refs[5:]
    sums_refs, (mine_ref, theirs_ref), refs = refs[:3], refs[3:5], refs[5:]
    if not first:
        mine_before, sent_before, *refs = refs
    if first or last:
        kept_ref, *refs = refs
        start = lax.rem(lax.axis_index("slab") + (0 if first else 1), 2) * half
        columns = pl.ds(pl.multiple_of(start, LANES), kept_ref.shape[2])
        for z in range(zdev):
            loads.append(pltpu.make_async_copy(vol_ref.at[z, :, columns], kept_ref.at[z], sems.at[z]))
            loads[z].start()
    mine_out, sent_out, *refs = refs
    if not first:
        mine_out[:, :, :offset] = mine_before[...]
        sent_out[:, :, :offset] = sent_before[...]
    outs, refs = refs[:3], refs[3:]
    if first:
        foot = jnp.concatenate([r[i, :, width:] for r in sums_refs for i in range(2)], axis=0)
        refs[5][...] = sums_refs[0][0, :, width:]
        kernel = footprint_matrix(dims, zdev, rdev, foot)
        count, rows = kernel.shape
        kernel_t = kernel.T
        cover = jnp.sum(kernel_t, axis=1, keepdims=True)
        angle = low_bits(over(iota((rows, 1), 0), rdev), per)
        path = jnp.zeros((rows, 1), F32)
        for a in range(per):
            at = order_ref[lax.axis_index("ang") * per + a]
            path = jnp.where(angle == a, jnp.sum(table_ref[pl.ds(at, 1), :], axis=1, keepdims=True), path)
        inverse = 1.0 / jnp.maximum(path * cover, 0.25)
        ahead, back = split(kernel_t), split(kernel)
        for ref, value in zip(refs, (*ahead, *back)):
            ref[...] = value
        refs[4][...] = jnp.broadcast_to(inverse, (rows, LANES))
    else:
        ahead, back = (mats[0][...], mats[1][...]), (mats[2][...], mats[3][...])
        inverse = inverse_ref[:, 0:1]
    start = lax.rem(lax.axis_index("slab"), 2) * half + offset
    for at, size in tiles(width):
        columns = slice(at, at + size)
        mine = mine_ref[:, :, pl.ds(pl.multiple_of(start + at, LANES), size)].astype(F32)
        theirs = theirs_ref[:, :, offset + at:offset + at + size]
        measured = jnp.concatenate([m.reshape(per * rdev, size) for m in (mine, theirs)], axis=0)
        sums = jnp.concatenate([r[i, :, columns] for r in sums_refs for i in range(2)], axis=0)
        residual = (measured - dot3(ahead, split(sums))) * inverse
        placed = slice(offset + at, offset + at + size)
        mine_out[:, :, placed] = residual[:per * rdev].reshape(per, rdev, size)
        sent_out[:, :, placed] = residual[per * rdev:].reshape(per, rdev, size)
        given = dot3(back, split(residual))
        for i, ref in enumerate(outs):
            for j in range(2):
                ref[j, :, columns] = given[(2 * i + j) * block:(2 * i + j + 1) * block]
    if last:
        update_weights(dims, zdev, rdev, foot_ref[...], order_ref, table_ref, refs[1], refs[0])
    for load in loads:
        load.wait()


def residual_step(dims, chunk, offset, width, load_width, mats, before, order, table, volume, sums, measured, theirs):
    per, groups, zb, cells = dims
    zdev = volume.shape[0]
    _, rdev, total = measured.shape
    first = chunk == 0
    block = zdev * per
    count, rows = 6 * block, 2 * per * rdev
    last = chunk == CHUNKS - 1
    assert not (first and last)
    given = jax.ShapeDtypeStruct((2, block, width), F32)
    piece = jax.ShapeDtypeStruct((per, rdev, offset + width), F32)
    shapes = [piece, piece, given, given, given]
    args, specs, scratch = [], [], []
    if first or last:
        args, specs = [order, table, volume], [IN_SMEM, IN_VMEM, ANYWHERE]
        shapes = [jax.ShapeDtypeStruct((zdev, cells, load_width), F32)] + shapes
    if last:
        depth = -(-3 * groups * SUBLANES // LANES) * LANES
        shapes.append(jax.ShapeDtypeStruct((zdev // zb, zb * cells, depth), BF16))
        scratch.append(pltpu.VMEM((groups * SUBLANES, table.shape[1]), F32))
        args += [mats[5]]
        specs += [IN_VMEM]
    if first:
        ahead, back = jax.ShapeDtypeStruct((rows, count), BF16), jax.ShapeDtypeStruct((count, rows), BF16)
        shapes += [ahead, ahead, back, back, jax.ShapeDtypeStruct((rows, LANES), F32)]
        shapes += [jax.ShapeDtypeStruct((block, LANES), F32)]
    else:
        args += mats[:5]
        specs += [IN_VMEM] * 5
    if first or last:
        scratch.append(pltpu.SemaphoreType.DMA((zdev,)))
    args += [*sums, measured, theirs, *before]
    specs += [IN_VMEM] * (5 + len(before))
    return pl.pallas_call(
        functools.partial(residual_kernel, dims, first, last, total // 2, rdev, zdev, offset, width),
        in_specs=specs,
        out_specs=[IN_VMEM] * len(shapes),
        out_shape=shapes,
        scratch_shapes=scratch,
        compiler_params=pltpu.CompilerParams(vmem_limit_bytes=30 * MIB),
        cost_estimate=pl.CostEstimate(
            flops=12 * count * rows * width, bytes_accessed=8 * width * (count + rows), transcendentals=0
        ),
        name=f"residual_{chunk}",
    )(*args)


def update_kernel(dims, first, last, half, offset, width, *refs):
    per, groups, zb, cells = dims
    count = groups * SUBLANES
    left_ref, backs, refs = refs[0], refs[1:1 + 2 * groups], refs[1 + 2 * groups:]
    backs = [backs[-1], *backs[groups:-1], *backs[:groups]]
    if first:
        vols, refs = refs[:2], refs[2:]
    else:
        vols, refs = [refs[0].at[0], refs[0].at[1]], refs[1:]
    zdev, depth = vols[0].shape[0], left_ref.shape[2]
    if last:
        pieces, refs = refs[:2], refs[2:]
    if not first:
        refs = refs[1:]
    if last:
        out_ref, res_ref, buf, sems, res_sems = refs
    else:
        out_ref, buf, sems = refs
    odd = lax.rem(lax.axis_index("slab"), 2)
    leaving = []
    for h, zp, slices, start in volume_pieces(dims, zdev, half, offset):
        rows = slice(zp * SUBLANES, (zp + 1) * SUBLANES)
        left = left_ref[zp]
        for at, size in tiles(width):
            piece = slice(at, at + size)
            back = jnp.concatenate([backs[h * groups + d][rows, piece] for d in range(groups)], axis=0)
            high, low = split(back)
            pad = jnp.zeros((depth - 3 * count, size), BF16)
            change = dot(left, jnp.concatenate([high, low, high, pad], axis=0))
            for z in range(zb):
                buf[h, zp * zb + z, :, piece] = (
                    vols[h][zp * zb + z, :, piece] + change[z * cells:(z + 1) * cells]
                )
        leaving.append(
            pltpu.make_async_copy(buf.at[h, slices], out_ref.at[slices, :, pl.ds(start, width)], sems.at[h, zp])
        )
        leaving[-1].start()
    if last:
        for h, ref in enumerate(pieces):
            columns = pl.ds(pl.multiple_of(lax.rem(odd + h, 2) * half, LANES), half)
            leaving.append(pltpu.make_async_copy(ref, res_ref.at[:, :, columns], res_sems.at[h]))
            leaving[-1].start()
    for copy in leaving:
        copy.wait()


def update_step(dims, chunk, offset, width, left, backs, pieces, kept, volume, out):
    per, groups, zb, cells = dims
    zdev, _, total = volume.shape
    first, last = chunk == 0, chunk == CHUNKS - 1
    args = [left, *backs[groups:], *backs[1:groups], backs[0], *kept]
    shapes = [jax.ShapeDtypeStruct(volume.shape, F32)]
    scratch = [pltpu.VMEM((2, zdev, cells, width), F32), pltpu.SemaphoreType.DMA((2, zdev // zb))]
    if last:
        args += pieces
        shapes += [jax.ShapeDtypeStruct((*pieces[0].shape[:2], total), F32)]
        scratch += [pltpu.SemaphoreType.DMA((2,))]
    specs = [IN_VMEM] * len(args)
    aliases = {}
    if not first:
        aliases = {len(args): 0}
        args += [out]
        specs += [ANYWHERE]
    size = zdev * cells * width * 2
    return pl.pallas_call(
        functools.partial(update_kernel, dims, first, last, total // 2, offset, width),
        in_specs=specs,
        out_specs=[ANYWHERE] * len(shapes),
        out_shape=shapes,
        scratch_shapes=scratch,
        input_output_aliases=aliases,
        compiler_params=pltpu.CompilerParams(vmem_limit_bytes=20 * MIB),
        cost_estimate=pl.CostEstimate(flops=2 * size * 48, bytes_accessed=size * 4, transcendentals=0),
        name=f"update_{chunk}",
    )(*args)


def body(volume, measured, foot_start, foot_len, order, table):
    slabs, groups = lax.axis_size("slab"), lax.axis_size("ang")
    per, rdev, total = measured.shape
    zdev, cells, _ = volume.shape
    half = total // 2
    zb = SUBLANES // per
    dims = (per, groups, zb, cells)
    each = half // CHUNKS
    widths = [each] * CHUNKS
    offsets = [sum(widths[:c]) for c in range(CHUNKS)]

    def along(value, to):
        pairs = [(s, to(s)) for s in range(slabs)]
        return lax.ppermute(value, "slab", pairs)

    def spread(value, other, d):
        if not (other or d):
            return value
        pairs = [
            (s * groups + a, (s ^ other) * groups + (a + d) % groups) for s in range(slabs) for a in range(groups)
        ]
        return lax.ppermute(value, ("slab", "ang"), pairs)

    def facing(s):
        return s ^ 2

    def step(up, busy):
        def to(s):
            there = s + 4 if up(s) else s - 4
            if 0 <= there < slabs:
                return there
            return there % slabs if busy else facing(s)
        return to

    def beyond(c):
        return step(lambda s: not s & 2, c < CHUNKS - 1)

    def back_from_beyond(c):
        return step(lambda s: s & 2, c > 0)

    odd = lax.rem(lax.axis_index("slab"), 2)
    theirs = along(
        lax.dynamic_slice_in_dim(measured, (1 - odd) * half, half, 2).astype(F32), lambda s: s ^ 1
    )

    sums, kept, left = [], [[] for _ in range(CHUNKS)], None
    for c in range(CHUNKS):
        parts = ray_sums(
            dims, c, offsets[c], widths[c], left, (order, foot_start, foot_len), table, volume
        )
        if c == 0:
            left = parts[2 * groups]
        else:
            kept[c].append(parts[2 * groups])
        parts = [spread(parts[h * groups + d], h, d) for h in range(2) for d in range(groups)]
        if c:
            parts, _ = lax.optimization_barrier((parts, sums[-1][0]))
        own = jnp.stack([sum(parts[:groups]), sum(parts[groups:])])
        near = along(own, facing)
        far = along(near, beyond(c))
        sums.append((own, near, far))
    pieces, given, mats = [], [], None
    for c in range(CHUNKS):
        loaded, mine, sent, own, near, far, *rest = residual_step(
            dims, c, offsets[c], widths[c], widths[0], mats, pieces, order, table, volume, sums[c], measured, theirs
        )
        kept[0].append(loaded)
        pieces = [mine, sent]
        mats = rest if c == 0 else mats
        left = rest[0]
        near = near + along(far, back_from_beyond(c))
        arrived = along(near, facing)
        halves = [own[i] + arrived[i] for i in range(2)]
        given.append([spread(halves[h], h, d) for h in range(2) for d in range(groups)])
    pieces = [mine, along(sent, lambda s: s ^ 1)]
    out = None
    for c in range(CHUNKS):
        out, *res = update_step(dims, c, offsets[c], widths[c], left, given[c], pieces, kept[c], volume, out)
    return out, res[0]


def solution(mesh):
    return jax.shard_map(
        body,
        mesh=mesh,
        in_specs=(
            P("slab", "ang", None),
            P("ang", "slab", None),
            P("slab", "ang"),
            P("slab", "ang"),
            P(),
            P(),
        ),
        out_specs=(P("slab", "ang", None), P("ang", "slab", None)),
        check_vma=False,
    )
```

```python
import functools

import jax
import jax.numpy as jnp
from jax import lax
from jax.experimental import pallas as pl
from jax.experimental.pallas import tpu as pltpu
from jax.sharding import PartitionSpec as P

F32, BF16 = jnp.float32, jnp.bfloat16
CHUNKS = 2
TILE = 512
LANES = 128
SUBLANES = 8
MIB = 1024 * 1024

IN_VMEM = pl.BlockSpec(memory_space=pltpu.VMEM)
IN_SMEM = pl.BlockSpec(memory_space=pltpu.SMEM)
ANYWHERE = pl.BlockSpec(memory_space=pl.ANY)


def split(value):
    high = value.astype(BF16)
    return high, (value - high.astype(F32)).astype(BF16)


def dot(a, b):
    return jnp.dot(a, b, preferred_element_type=F32)


def dot3(a, b):
    return dot(a[0], b[0]) + (dot(a[0], b[1]) + dot(a[1], b[0]))


def iota(shape, dim):
    return lax.broadcasted_iota(jnp.int32, shape, dim)


def low_bits(value, size):
    assert size & (size - 1) == 0
    return value & (size - 1)


def over(value, size):
    assert size & (size - 1) == 0
    return value >> (size.bit_length() - 1)


def pick(index, values):
    out = jnp.zeros(index.shape, values[0].dtype)
    for at, value in enumerate(values):
        out = jnp.where(index == at, value, out)
    return out


def tiles(width):
    step = min(TILE, width)
    return [(at, min(step, width - at)) for at in range(0, width, step)]


def slice_weights(dims, sign, order_ref, table_ref, rows_ref):
    per, groups, zb, cells = dims
    ang = lax.axis_index("ang")
    for d in range(groups):
        group = lax.rem(ang + sign * d + groups, groups)
        for z in range(zb):
            for a in range(per):
                at = (d * zb + z) * per + a
                rows_ref[at:at + 1, :] = table_ref[pl.ds(order_ref[group * per + a], 1), :]
    wide = rows_ref[...]
    total = wide.shape[1]
    row_slice = low_bits(over(iota(wide.shape, 0), per), zb)
    lane_slice = over(iota(wide.shape, 1), cells)
    out = jnp.zeros_like(wide)
    for z in range(zb):
        shift = lax.rem(z * cells - ang * cells + total, total)
        here = jnp.logical_and(row_slice == z, lane_slice == z)
        out = jnp.where(here, pltpu.roll(wide, shift, 1), out)
    return out


def volume_pieces(dims, zdev, half, offset):
    odd = lax.rem(lax.axis_index("slab"), 2)
    zb = dims[2]
    for h in range(2):
        start = pl.multiple_of(lax.rem(odd + h, 2) * half + offset, LANES)
        for zp in range(zdev // zb):
            yield h, zp, slice(zp * zb, (zp + 1) * zb), start


def rays_kernel(dims, first, half, offset, width, *refs):
    per, groups, zb, cells = dims
    count = groups * SUBLANES
    if first:
        order_ref, start_ref, len_ref, table_ref, vol_ref, *refs = refs
    else:
        given_ref, vol_ref, *refs = refs
    outs, refs = refs[:2 * groups], refs[2 * groups:]
    if first:
        left_ref, buf, sems, table_buf, order_buf, start_buf, len_buf, rows_ref, small_sems = refs
    else:
        buf, sems = refs
    zdev = vol_ref.shape[0]
    copies = []
    if first:
        small = [
            pltpu.make_async_copy(source, to, small_sems.at[i])
            for i, (source, to) in enumerate(
                [(order_ref, order_buf), (table_ref, table_buf), (start_ref, start_buf), (len_ref, len_buf)]
            )
        ]
        for copy in small:
            copy.start()
    for h, zp, slices, start in volume_pieces(dims, zdev, half, offset):
        source = vol_ref.at[slices, :, pl.ds(start, width)]
        copies.append((h, zp, pltpu.make_async_copy(source, buf.at[h, slices], sems.at[h, zp])))
        copies[-1][-1].start()
    if first:
        small[0].wait()
        small[1].wait()
        both = jnp.concatenate(split(slice_weights(dims, 1, order_buf, table_buf, rows_ref)), axis=0)
        left = jnp.concatenate([both, both], axis=1)
        left_ref[...] = left
        small[2].wait()
        small[3].wait()
        shape = (zdev * per, LANES)
        angle, lane = low_bits(iota(shape, 0), per), iota(shape, 1)
        starts = pick(angle, [start_buf[0, a].astype(F32) for a in range(per)])
        lengths = pick(angle, [len_buf[0, a].astype(F32) for a in range(per)])
        for d in range(groups):
            foot = jnp.where(lane == 2 * d, starts, jnp.where(lane == 2 * d + 1, lengths, 0.0))
            for h in range(2):
                outs[h * groups + d][:, width:] = foot
    else:
        left = given_ref[...]
    for h, zp, copy in copies:
        copy.wait()
        for at, size in tiles(width):
            parts = [split(buf[h, zp * zb + z, :, at:at + size]) for z in range(zb)]
            product = dot(left, jnp.concatenate([p[0] for p in parts] + [p[1] for p in parts], axis=0))
            sums = product[:count] + product[count:]
            for d in range(groups):
                outs[h * groups + d][zp * SUBLANES:(zp + 1) * SUBLANES, at:at + size] = (
                    sums[d * SUBLANES:(d + 1) * SUBLANES]
                )


def ray_sums(dims, chunk, offset, width, given, small, table, volume):
    per, groups, zb, cells = dims
    zdev, _, total = volume.shape
    first = chunk == 0
    count, all_cells = groups * SUBLANES, table.shape[1]
    out = jax.ShapeDtypeStruct((zdev * per, width + (LANES if first else 0)), F32)
    left = jax.ShapeDtypeStruct((2 * count, 2 * zb * cells), BF16)
    assert zb * cells == all_cells
    sems = pltpu.SemaphoreType.DMA((2, zdev // zb))
    shapes = [out] * (2 * groups)
    scratch = [pltpu.VMEM((2, zdev, cells, width), F32), sems]
    args, specs, limit = [given, volume], [IN_VMEM, ANYWHERE], 40
    if first:
        scratch += [pltpu.VMEM(table.shape, F32)] + [pltpu.SMEM(a.shape, a.dtype) for a in small]
        scratch += [pltpu.VMEM((count, all_cells), F32), pltpu.SemaphoreType.DMA((4,))]
        args, specs, limit = [*small, table, volume], [ANYWHERE] * 5, 58
        shapes += [left]
    if not first:
        scratch = [sems]
        shapes += [jax.ShapeDtypeStruct((2, zdev, cells, width), F32)]
    size = zdev * cells * width * 2
    return pl.pallas_call(
        functools.partial(rays_kernel, dims, first, total // 2, offset, width),
        in_specs=specs,
        out_specs=[IN_VMEM] * len(shapes),
        out_shape=shapes,
        scratch_shapes=scratch,
        compiler_params=pltpu.CompilerParams(vmem_limit_bytes=limit * MIB),
        cost_estimate=pl.CostEstimate(flops=2 * size * 16, bytes_accessed=size * 4, transcendentals=0),
        name=f"ray_sums_{chunk}",
    )(*args)


def hat_weights(dims, zdev, start, length, row):
    per, groups, zb, cells = dims
    at = low_bits(iota(start.shape, 0), zdev * per)
    slice_at = over(at, zb * per) * zb + low_bits(over(at, per), zb)
    span = jnp.where(length > 0.0, length, 1.0) / zdev
    centre = start + (slice_at.astype(F32) + 0.5) * span
    hat = jnp.maximum(0.0, 1.0 - jnp.abs(row + 0.5 - centre) / span)
    return jnp.where(jnp.logical_and(row >= start, row < start + length), hat, 0.0)


def footprint_matrix(dims, zdev, rdev, foot):
    per = dims[0]
    rows = 2 * per * rdev
    slab = lax.axis_index("slab")
    sibling = slab + 1 - 2 * lax.rem(slab, 2)
    row_id = iota((1, rows), 1)
    row_slab = jnp.where(row_id < per * rdev, slab, sibling)
    row = (row_slab * rdev + low_bits(row_id, rdev)).astype(F32)
    shape = (foot.shape[0], rows)
    same_angle = low_bits(iota(shape, 0), per) == low_bits(over(iota(shape, 1), rdev), per)
    beyond = slab + jnp.where(low_bits(slab, 4) < 2, -2, 2)
    there = jnp.logical_and(beyond >= 0, beyond < lax.axis_size("slab"))
    known = jnp.where(there, foot.shape[0], foot.shape[0] // 3 * 2)
    meets = jnp.logical_and(same_angle, iota(shape, 0) < known)
    return jnp.where(meets, hat_weights(dims, zdev, foot[:, 0:1], foot[:, 1:2], row), 0.0)


def update_weights(dims, zdev, rdev, foot, order_ref, table_ref, rows_ref, out_ref):
    per, groups, zb, cells = dims
    count = groups * SUBLANES
    weights = slice_weights(dims, -1, order_ref, table_ref, rows_ref)
    window = -(-5 * rdev // LANES) * LANES
    row = ((lax.axis_index("slab") - 2) * rdev + iota((1, window), 1)).astype(F32)
    sums = [
        jnp.sum(hat_weights(dims, zdev, foot[:, 2 * d:2 * d + 1], foot[:, 2 * d + 1:2 * d + 2], row), axis=1, keepdims=True)
        for d in range(groups)
    ]
    pad = jnp.zeros((out_ref.shape[2] - 3 * count, weights.shape[1]), F32)
    for zp in range(zdev // zb):
        slices = jnp.concatenate([s[zp * SUBLANES:(zp + 1) * SUBLANES] for s in sums], axis=0)
        scaled = weights / jnp.sum(weights * slices, axis=0, keepdims=True)
        high = scaled.astype(BF16).astype(F32)
        stacked = jnp.concatenate([high, high, scaled - high, pad], axis=0)
        out_ref[zp] = stacked.T.astype(BF16)


def prepare_kernel(dims, rdev, half, width, order_ref, table_ref, foot_ref, _, vol_ref, kept_ref, left_ref, sems, rows_ref):
    zdev = vol_ref.shape[0]
    copies = []
    for h, zp, slices, start in volume_pieces(dims, zdev, half, 0):
        source = vol_ref.at[slices, :, pl.ds(start, width)]
        copies.append(pltpu.make_async_copy(source, kept_ref.at[h, slices], sems.at[h, zp]))
        copies[-1].start()
    update_weights(dims, zdev, rdev, foot_ref[0, :, width:], order_ref, table_ref, rows_ref, left_ref)
    for copy in copies:
        copy.wait()


def prepare_step(dims, rdev, width, order, table, own, after, volume):
    per, groups, zb, cells = dims
    zdev, _, total = volume.shape
    depth = -(-3 * groups * SUBLANES // LANES) * LANES
    return pl.pallas_call(
        functools.partial(prepare_kernel, dims, rdev, total // 2, width),
        in_specs=[IN_SMEM, IN_VMEM, IN_VMEM, ANYWHERE, ANYWHERE],
        out_specs=[IN_VMEM, IN_VMEM],
        out_shape=[
            jax.ShapeDtypeStruct((2, zdev, cells, width), F32),
            jax.ShapeDtypeStruct((zdev // zb, zb * cells, depth), BF16),
        ],
        scratch_shapes=[
            pltpu.SemaphoreType.DMA((2, zdev // zb)),
            pltpu.VMEM((groups * SUBLANES, table.shape[1]), F32),
        ],
        compiler_params=pltpu.CompilerParams(vmem_limit_bytes=40 * MIB),
        cost_estimate=pl.CostEstimate(flops=0, bytes_accessed=8 * zdev * cells * width, transcendentals=0),
        name="prepare",
    )(order, table, own, after, volume)


def residual_kernel(dims, first, half, rdev, zdev, offset, width, *refs):
    per, groups, zb, cells = dims
    block = zdev * per
    if first:
        order_ref, table_ref, *refs = refs
    else:
        mats, inverse_ref, refs = refs[:4], refs[4], refs[5:]
    sums_refs, (mine_ref, theirs_ref), refs = refs[:3], refs[3:5], refs[5:]
    if not first:
        mine_before, sent_before, *refs = refs
    mine_out, sent_out, *refs = refs
    if not first:
        mine_out[:, :, :offset] = mine_before[...]
        sent_out[:, :, :offset] = sent_before[...]
    outs, refs = refs[:3], refs[3:]
    if first:
        foot = jnp.concatenate([r[i, :, width:] for r in sums_refs for i in range(2)], axis=0)
        kernel = footprint_matrix(dims, zdev, rdev, foot)
        count, rows = kernel.shape
        kernel_t = kernel.T
        cover = jnp.sum(kernel_t, axis=1, keepdims=True)
        angle = low_bits(over(iota((rows, 1), 0), rdev), per)
        path = jnp.zeros((rows, 1), F32)
        for a in range(per):
            at = order_ref[lax.axis_index("ang") * per + a]
            path = jnp.where(angle == a, jnp.sum(table_ref[pl.ds(at, 1), :], axis=1, keepdims=True), path)
        inverse = 1.0 / jnp.maximum(path * cover, 0.25)
        ahead, back = split(kernel_t), split(kernel)
        for ref, value in zip(refs, (*ahead, *back)):
            ref[...] = value
        refs[4][...] = jnp.broadcast_to(inverse, (rows, LANES))
    else:
        ahead, back = (mats[0][...], mats[1][...]), (mats[2][...], mats[3][...])
        inverse = inverse_ref[:, 0:1]
    start = lax.rem(lax.axis_index("slab"), 2) * half + offset
    for at, size in tiles(width):
        columns = slice(at, at + size)
        mine = mine_ref[:, :, pl.ds(pl.multiple_of(start + at, LANES), size)].astype(F32)
        theirs = theirs_ref[:, :, offset + at:offset + at + size]
        measured = jnp.concatenate([m.reshape(per * rdev, size) for m in (mine, theirs)], axis=0)
        sums = jnp.concatenate([r[i, :, columns] for r in sums_refs for i in range(2)], axis=0)
        residual = (measured - dot3(ahead, split(sums))) * inverse
        placed = slice(offset + at, offset + at + size)
        mine_out[:, :, placed] = residual[:per * rdev].reshape(per, rdev, size)
        sent_out[:, :, placed] = residual[per * rdev:].reshape(per, rdev, size)
        given = dot3(back, split(residual))
        for i, ref in enumerate(outs):
            for j in range(2):
                ref[j, :, columns] = given[(2 * i + j) * block:(2 * i + j + 1) * block]


def residual_step(dims, zdev, chunk, offset, width, mats, before, order, table, sums, measured, theirs):
    per, groups, zb, cells = dims
    _, rdev, total = measured.shape
    first = chunk == 0
    block = zdev * per
    count, rows = 6 * block, 2 * per * rdev
    given = jax.ShapeDtypeStruct((2, block, width), F32)
    piece = jax.ShapeDtypeStruct((per, rdev, offset + width), F32)
    shapes = [piece, piece, given, given, given]
    if first:
        args, specs = [order, table], [IN_SMEM, IN_VMEM]
        ahead, back = jax.ShapeDtypeStruct((rows, count), BF16), jax.ShapeDtypeStruct((count, rows), BF16)
        shapes += [ahead, ahead, back, back, jax.ShapeDtypeStruct((rows, LANES), F32)]
    else:
        args, specs = list(mats), [IN_VMEM] * len(mats)
    args += [*sums, measured, theirs, *before]
    specs += [IN_VMEM] * (5 + len(before))
    return pl.pallas_call(
        functools.partial(residual_kernel, dims, first, total // 2, rdev, zdev, offset, width),
        in_specs=specs,
        out_specs=[IN_VMEM] * len(shapes),
        out_shape=shapes,
        compiler_params=pltpu.CompilerParams(vmem_limit_bytes=30 * MIB),
        cost_estimate=pl.CostEstimate(
            flops=12 * count * rows * width, bytes_accessed=8 * width * (count + rows), transcendentals=0
        ),
        name=f"residual_{chunk}",
    )(*args)


def update_kernel(dims, first, last, half, offset, width, *refs):
    per, groups, zb, cells = dims
    count = groups * SUBLANES
    left_ref, backs, refs = refs[0], refs[1:1 + 2 * groups], refs[1 + 2 * groups:]
    backs = [backs[-1], *backs[groups:-1], *backs[:groups]]
    vol_ref, *refs = refs
    zdev, depth = vol_ref.shape[1], left_ref.shape[2]
    if last:
        pieces, refs = refs[:2], refs[2:]
    if not first:
        refs = refs[1:]
    if last:
        out_ref, res_ref, buf, sems, res_sems = refs
    else:
        out_ref, buf, sems = refs
    odd = lax.rem(lax.axis_index("slab"), 2)
    leaving = []
    for h, zp, slices, start in volume_pieces(dims, zdev, half, offset):
        rows = slice(zp * SUBLANES, (zp + 1) * SUBLANES)
        left = left_ref[zp]
        for at, size in tiles(width):
            piece = slice(at, at + size)
            back = jnp.concatenate([backs[h * groups + d][rows, piece] for d in range(groups)], axis=0)
            high, low = split(back)
            pad = jnp.zeros((depth - 3 * count, size), BF16)
            change = dot(left, jnp.concatenate([high, low, high, pad], axis=0))
            for z in range(zb):
                buf[h, zp * zb + z, :, piece] = (
                    vol_ref[h, zp * zb + z, :, piece] + change[z * cells:(z + 1) * cells]
                )
        leaving.append(
            pltpu.make_async_copy(buf.at[h, slices], out_ref.at[slices, :, pl.ds(start, width)], sems.at[h, zp])
        )
        leaving[-1].start()
    if last:
        for h, ref in enumerate(pieces):
            columns = pl.ds(pl.multiple_of(lax.rem(odd + h, 2) * half, LANES), half)
            leaving.append(pltpu.make_async_copy(ref, res_ref.at[:, :, columns], res_sems.at[h]))
            leaving[-1].start()
    for copy in leaving:
        copy.wait()


def update_step(dims, chunk, offset, width, left, backs, pieces, kept, volume, out):
    per, groups, zb, cells = dims
    zdev, _, total = volume.shape
    first, last = chunk == 0, chunk == CHUNKS - 1
    args = [left, *backs[groups:], *backs[1:groups], backs[0], kept]
    shapes = [jax.ShapeDtypeStruct(volume.shape, F32)]
    scratch = [pltpu.VMEM((2, zdev, cells, width), F32), pltpu.SemaphoreType.DMA((2, zdev // zb))]
    if last:
        args += pieces
        shapes += [jax.ShapeDtypeStruct((*pieces[0].shape[:2], total), F32)]
        scratch += [pltpu.SemaphoreType.DMA((2,))]
    specs = [IN_VMEM] * len(args)
    aliases = {}
    if not first:
        aliases = {len(args): 0}
        args += [out]
        specs += [ANYWHERE]
    size = zdev * cells * width * 2
    return pl.pallas_call(
        functools.partial(update_kernel, dims, first, last, total // 2, offset, width),
        in_specs=specs,
        out_specs=[ANYWHERE] * len(shapes),
        out_shape=shapes,
        scratch_shapes=scratch,
        input_output_aliases=aliases,
        compiler_params=pltpu.CompilerParams(vmem_limit_bytes=20 * MIB),
        cost_estimate=pl.CostEstimate(flops=2 * size * 48, bytes_accessed=size * 4, transcendentals=0),
        name=f"update_{chunk}",
    )(*args)


def body(volume, measured, foot_start, foot_len, order, table):
    slabs, groups = lax.axis_size("slab"), lax.axis_size("ang")
    per, rdev, total = measured.shape
    zdev, cells, _ = volume.shape
    half = total // 2
    zb = SUBLANES // per
    dims = (per, groups, zb, cells)
    each = half // CHUNKS
    widths = [each] * CHUNKS
    offsets = [sum(widths[:c]) for c in range(CHUNKS)]

    def along(value, to):
        pairs = [(s, to(s)) for s in range(slabs)]
        return lax.ppermute(value, "slab", pairs)

    def spread(value, other, d):
        if not (other or d):
            return value
        pairs = [
            (s * groups + a, (s ^ other) * groups + (a + d) % groups) for s in range(slabs) for a in range(groups)
        ]
        return lax.ppermute(value, ("slab", "ang"), pairs)

    def facing(s):
        return s ^ 2

    def step(up, busy):
        def to(s):
            there = s + 4 if up(s) else s - 4
            if 0 <= there < slabs:
                return there
            return there % slabs if busy else facing(s)
        return to

    def beyond(c):
        return step(lambda s: not s & 2, c < CHUNKS - 1)

    def back_from_beyond(c):
        return step(lambda s: s & 2, c > 0)

    odd = lax.rem(lax.axis_index("slab"), 2)
    theirs = along(
        lax.dynamic_slice_in_dim(measured, (1 - odd) * half, half, 2).astype(F32), lambda s: s ^ 1
    )

    sums, kept, left = [], [], None
    for c in range(CHUNKS):
        parts = ray_sums(
            dims, c, offsets[c], widths[c], left, (order, foot_start, foot_len), table, volume
        )
        if c == 0:
            left = parts[2 * groups]
        else:
            kept.append(parts[2 * groups])
        parts = [spread(parts[h * groups + d], h, d) for h in range(2) for d in range(groups)]
        if c:
            parts, _ = lax.optimization_barrier((parts, sums[-1][0]))
        own = jnp.stack([sum(parts[:groups]), sum(parts[groups:])])
        near = along(own, facing)
        if c == 0:
            first_columns, update_left = prepare_step(dims, rdev, widths[0], order, table, own, near, volume)
            kept.append(first_columns)
        if c == 1:
            near, kept[0] = lax.optimization_barrier((near, kept[0]))
        far = along(near, beyond(c))
        sums.append((own, near, far))
    pieces, given, mats = [], [], None
    for c in range(CHUNKS):
        mine, sent, own, near, far, *rest = residual_step(
            dims, zdev, c, offsets[c], widths[c], mats, pieces, order, table, sums[c], measured, theirs
        )
        pieces = [mine, sent]
        mats = rest if c == 0 else mats
        near = near + along(far, back_from_beyond(c))
        arrived = along(near, facing)
        halves = [own[i] + arrived[i] for i in range(2)]
        given.append([spread(halves[h], h, d) for h in range(2) for d in range(groups)])
    pieces = [mine, along(sent, lambda s: s ^ 1)]
    out = None
    for c in range(CHUNKS):
        out, *res = update_step(dims, c, offsets[c], widths[c], update_left, given[c], pieces, kept[c], volume, out)
    return out, res[0]


def solution(mesh):
    return jax.shard_map(
        body,
        mesh=mesh,
        in_specs=(
            P("slab", "ang", None),
            P("ang", "slab", None),
            P("slab", "ang"),
            P("slab", "ang"),
            P(),
            P(),
        ),
        out_specs=(P("slab", "ang", None), P("ang", "slab", None)),
        check_vma=False,
    )
```

```python
import functools

import jax
import jax.numpy as jnp
from jax import lax
from jax.experimental import pallas as pl
from jax.experimental.pallas import tpu as pltpu
from jax.sharding import PartitionSpec as P

F32, BF16 = jnp.float32, jnp.bfloat16
CHUNKS = 2
RAY_HALVES = [[(0, 1)], [(0, 1)]]
UPDATE_HALVES = [[(0, 1)], [(0,), (1,)]]
TILE = 512
LANES = 128
SUBLANES = 8
MIB = 1024 * 1024

IN_VMEM = pl.BlockSpec(memory_space=pltpu.VMEM)
IN_SMEM = pl.BlockSpec(memory_space=pltpu.SMEM)
ANYWHERE = pl.BlockSpec(memory_space=pl.ANY)


def split(value):
    high = value.astype(BF16)
    return high, (value - high.astype(F32)).astype(BF16)


def dot(a, b):
    return jnp.dot(a, b, preferred_element_type=F32)


def dot3(a, b):
    return dot(a[0], b[0]) + (dot(a[0], b[1]) + dot(a[1], b[0]))


def iota(shape, dim):
    return lax.broadcasted_iota(jnp.int32, shape, dim)


def low_bits(value, size):
    assert size & (size - 1) == 0
    return value & (size - 1)


def over(value, size):
    assert size & (size - 1) == 0
    return value >> (size.bit_length() - 1)


def pick(index, values):
    out = jnp.zeros(index.shape, values[0].dtype)
    for at, value in enumerate(values):
        out = jnp.where(index == at, value, out)
    return out


def tiles(width):
    step = min(TILE, width)
    return [(at, min(step, width - at)) for at in range(0, width, step)]


def slice_weights(dims, sign, order_ref, table_ref, rows_ref):
    per, groups, zb, cells = dims
    ang = lax.axis_index("ang")
    for d in range(groups):
        group = lax.rem(ang + sign * d + groups, groups)
        for z in range(zb):
            for a in range(per):
                at = (d * zb + z) * per + a
                rows_ref[at:at + 1, :] = table_ref[pl.ds(order_ref[group * per + a], 1), :]
    wide = rows_ref[...]
    total = wide.shape[1]
    row_slice = low_bits(over(iota(wide.shape, 0), per), zb)
    lane_slice = over(iota(wide.shape, 1), cells)
    out = jnp.zeros_like(wide)
    for z in range(zb):
        shift = lax.rem(z * cells - ang * cells + total, total)
        here = jnp.logical_and(row_slice == z, lane_slice == z)
        out = jnp.where(here, pltpu.roll(wide, shift, 1), out)
    return out


def volume_pieces(dims, zdev, half, offset, halves):
    odd = lax.rem(lax.axis_index("slab"), 2)
    zb = dims[2]
    for i, h in enumerate(halves):
        start = pl.multiple_of(lax.rem(odd + h, 2) * half + offset, LANES)
        for zp in range(zdev // zb):
            yield i, zp, slice(zp * zb, (zp + 1) * zb), start


def rays_kernel(dims, first, keep, extra, halves, half, offset, width, *refs):
    per, groups, zb, cells = dims
    count = groups * SUBLANES
    if first:
        order_ref, start_ref, len_ref, table_ref, vol_ref, *refs = refs
    elif extra:
        start_buf, len_buf, given_ref, vol_ref, *refs = refs
    else:
        given_ref, vol_ref, *refs = refs
    outs, refs = refs[:len(halves) * groups], refs[len(halves) * groups:]
    if first:
        left_ref, buf, sems, table_buf, order_buf, start_buf, len_buf, rows_ref, small_sems = refs
    else:
        buf, sems = refs
    zdev = vol_ref.shape[0]
    copies = []
    if first:
        small = [
            pltpu.make_async_copy(source, to, small_sems.at[i])
            for i, (source, to) in enumerate(
                [(order_ref, order_buf), (table_ref, table_buf), (start_ref, start_buf), (len_ref, len_buf)]
            )
        ]
        for copy in small:
            copy.start()
    for h, zp, slices, start in volume_pieces(dims, zdev, half, offset, halves):
        source = vol_ref.at[slices, :, pl.ds(start, width)]
        copies.append((h, zp, pltpu.make_async_copy(source, buf.at[h, slices], sems.at[h, zp])))
        copies[-1][-1].start()
    if first:
        small[0].wait()
        small[1].wait()
        both = jnp.concatenate(split(slice_weights(dims, 1, order_buf, table_buf, rows_ref)), axis=0)
        left = jnp.concatenate([both, both], axis=1)
        left_ref[...] = left
        small[2].wait()
        small[3].wait()
    else:
        left = given_ref[...]
    if extra:
        shape = (zdev * per, LANES)
        angle, lane = low_bits(iota(shape, 0), per), iota(shape, 1)
        starts = pick(angle, [start_buf[0, a].astype(F32) for a in range(per)])
        lengths = pick(angle, [len_buf[0, a].astype(F32) for a in range(per)])
        for d in range(groups):
            foot = jnp.where(lane == 2 * d, starts, jnp.where(lane == 2 * d + 1, lengths, 0.0))
            for h in range(len(halves)):
                outs[h * groups + d][:, width:] = foot
    for h, zp, copy in copies:
        copy.wait()
        for at, size in tiles(width):
            parts = [split(buf[h, zp * zb + z, :, at:at + size]) for z in range(zb)]
            product = dot(left, jnp.concatenate([p[0] for p in parts] + [p[1] for p in parts], axis=0))
            sums = product[:count] + product[count:]
            for d in range(groups):
                outs[h * groups + d][zp * SUBLANES:(zp + 1) * SUBLANES, at:at + size] = (
                    sums[d * SUBLANES:(d + 1) * SUBLANES]
                )


def ray_sums(dims, chunk, halves, offset, width, given, small, table, volume):
    per, groups, zb, cells = dims
    zdev, _, total = volume.shape
    first, keep, extra = given is None, chunk > 0, chunk == 0
    count, all_cells = groups * SUBLANES, table.shape[1]
    out = jax.ShapeDtypeStruct((zdev * per, width + (LANES if extra else 0)), F32)
    left = jax.ShapeDtypeStruct((2 * count, 2 * zb * cells), BF16)
    columns = (len(halves), zdev, cells, width)
    assert zb * cells == all_cells
    shapes = [out] * (len(halves) * groups)
    scratch = [] if keep else [pltpu.VMEM(columns, F32)]
    scratch += [pltpu.SemaphoreType.DMA((len(halves), zdev // zb))]
    args, specs, limit = [given, volume], [IN_VMEM, ANYWHERE], 40
    if first:
        scratch += [pltpu.VMEM(table.shape, F32)] + [pltpu.SMEM(a.shape, a.dtype) for a in small]
        scratch += [pltpu.VMEM((count, all_cells), F32), pltpu.SemaphoreType.DMA((4,))]
        args, specs, limit = [*small, table, volume], [ANYWHERE] * 5, 58
        shapes += [left]
    elif extra:
        args, specs, limit = [*small[1:], *args], [IN_SMEM] * 2 + specs, 50
    if keep:
        shapes += [jax.ShapeDtypeStruct(columns, F32)]
    size = zdev * cells * width * len(halves)
    return pl.pallas_call(
        functools.partial(rays_kernel, dims, first, keep, extra, halves, total // 2, offset, width),
        in_specs=specs,
        out_specs=[IN_VMEM] * len(shapes),
        out_shape=shapes,
        scratch_shapes=scratch,
        compiler_params=pltpu.CompilerParams(vmem_limit_bytes=limit * MIB),
        cost_estimate=pl.CostEstimate(flops=2 * size * 16, bytes_accessed=size * 4, transcendentals=0),
        name=f"ray_sums_{chunk}_{halves[0]}",
    )(*args)


def hat_weights(dims, zdev, start, length, row):
    per, groups, zb, cells = dims
    at = low_bits(iota(start.shape, 0), zdev * per)
    slice_at = over(at, zb * per) * zb + low_bits(over(at, per), zb)
    span = jnp.where(length > 0.0, length, 1.0) / zdev
    centre = start + (slice_at.astype(F32) + 0.5) * span
    hat = jnp.maximum(0.0, 1.0 - jnp.abs(row + 0.5 - centre) / span)
    return jnp.where(jnp.logical_and(row >= start, row < start + length), hat, 0.0)


def footprint_matrix(dims, zdev, rdev, foot):
    per = dims[0]
    rows = 2 * per * rdev
    slab = lax.axis_index("slab")
    sibling = slab + 1 - 2 * lax.rem(slab, 2)
    row_id = iota((1, rows), 1)
    row_slab = jnp.where(row_id < per * rdev, slab, sibling)
    row = (row_slab * rdev + low_bits(row_id, rdev)).astype(F32)
    shape = (foot.shape[0], rows)
    same_angle = low_bits(iota(shape, 0), per) == low_bits(over(iota(shape, 1), rdev), per)
    beyond = slab + jnp.where(low_bits(slab, 4) < 2, -2, 2)
    there = jnp.logical_and(beyond >= 0, beyond < lax.axis_size("slab"))
    known = jnp.where(there, foot.shape[0], foot.shape[0] // 3 * 2)
    meets = jnp.logical_and(same_angle, iota(shape, 0) < known)
    return jnp.where(meets, hat_weights(dims, zdev, foot[:, 0:1], foot[:, 1:2], row), 0.0)


def update_weights(dims, zdev, rdev, foot, order_ref, table_ref, rows_ref, out_ref):
    per, groups, zb, cells = dims
    count = groups * SUBLANES
    weights = slice_weights(dims, -1, order_ref, table_ref, rows_ref)
    window = -(-5 * rdev // LANES) * LANES
    row = ((lax.axis_index("slab") - 2) * rdev + iota((1, window), 1)).astype(F32)
    sums = [
        jnp.sum(hat_weights(dims, zdev, foot[:, 2 * d:2 * d + 1], foot[:, 2 * d + 1:2 * d + 2], row), axis=1, keepdims=True)
        for d in range(groups)
    ]
    pad = jnp.zeros((out_ref.shape[2] - 3 * count, weights.shape[1]), F32)
    for zp in range(zdev // zb):
        slices = jnp.concatenate([s[zp * SUBLANES:(zp + 1) * SUBLANES] for s in sums], axis=0)
        scaled = weights / jnp.sum(weights * slices, axis=0, keepdims=True)
        high = scaled.astype(BF16).astype(F32)
        stacked = jnp.concatenate([high, high, scaled - high, pad], axis=0)
        out_ref[zp] = stacked.T.astype(BF16)


def prepare_kernel(dims, rdev, half, width, order_ref, table_ref, foot_ref, _, vol_ref, kept_ref, left_ref, sems, rows_ref):
    zdev = vol_ref.shape[0]
    copies = []
    for h, zp, slices, start in volume_pieces(dims, zdev, half, 0, (0, 1)):
        source = vol_ref.at[slices, :, pl.ds(start, width)]
        copies.append(pltpu.make_async_copy(source, kept_ref.at[h, slices], sems.at[h, zp]))
        copies[-1].start()
    update_weights(dims, zdev, rdev, foot_ref[0, :, width:], order_ref, table_ref, rows_ref, left_ref)
    for copy in copies:
        copy.wait()


def prepare_step(dims, rdev, width, order, table, own, after, volume):
    per, groups, zb, cells = dims
    zdev, _, total = volume.shape
    depth = -(-3 * groups * SUBLANES // LANES) * LANES
    return pl.pallas_call(
        functools.partial(prepare_kernel, dims, rdev, total // 2, width),
        in_specs=[IN_SMEM, IN_VMEM, IN_VMEM, ANYWHERE, ANYWHERE],
        out_specs=[IN_VMEM, IN_VMEM],
        out_shape=[
            jax.ShapeDtypeStruct((2, zdev, cells, width), F32),
            jax.ShapeDtypeStruct((zdev // zb, zb * cells, depth), BF16),
        ],
        scratch_shapes=[
            pltpu.SemaphoreType.DMA((2, zdev // zb)),
            pltpu.VMEM((groups * SUBLANES, table.shape[1]), F32),
        ],
        compiler_params=pltpu.CompilerParams(vmem_limit_bytes=40 * MIB),
        cost_estimate=pl.CostEstimate(flops=0, bytes_accessed=8 * zdev * cells * width, transcendentals=0),
        name="prepare",
    )(order, table, own, after, volume)


def residual_kernel(dims, first, half, rdev, zdev, offset, width, *refs):
    per, groups, zb, cells = dims
    block = zdev * per
    if first:
        order_ref, table_ref, *refs = refs
    else:
        mats, inverse_ref, refs = refs[:4], refs[4], refs[5:]
    sums_refs, (mine_ref, theirs_ref), refs = refs[:3], refs[3:5], refs[5:]
    if not first:
        mine_before, sent_before, *refs = refs
    mine_out, sent_out, *refs = refs
    if not first:
        mine_out[:, :, :offset] = mine_before[...]
        sent_out[:, :, :offset] = sent_before[...]
    outs, refs = refs[:3], refs[3:]
    if first:
        foot = jnp.concatenate([r[i, :, width:] for r in sums_refs for i in range(2)], axis=0)
        kernel = footprint_matrix(dims, zdev, rdev, foot)
        count, rows = kernel.shape
        kernel_t = kernel.T
        cover = jnp.sum(kernel_t, axis=1, keepdims=True)
        angle = low_bits(over(iota((rows, 1), 0), rdev), per)
        path = jnp.zeros((rows, 1), F32)
        for a in range(per):
            at = order_ref[lax.axis_index("ang") * per + a]
            path = jnp.where(angle == a, jnp.sum(table_ref[pl.ds(at, 1), :], axis=1, keepdims=True), path)
        inverse = 1.0 / jnp.maximum(path * cover, 0.25)
        ahead, back = split(kernel_t), split(kernel)
        for ref, value in zip(refs, (*ahead, *back)):
            ref[...] = value
        refs[4][...] = jnp.broadcast_to(inverse, (rows, LANES))
    else:
        ahead, back = (mats[0][...], mats[1][...]), (mats[2][...], mats[3][...])
        inverse = inverse_ref[:, 0:1]
    start = lax.rem(lax.axis_index("slab"), 2) * half + offset
    for at, size in tiles(width):
        columns = slice(at, at + size)
        mine = mine_ref[:, :, pl.ds(pl.multiple_of(start + at, LANES), size)].astype(F32)
        theirs = theirs_ref[:, :, offset + at:offset + at + size]
        measured = jnp.concatenate([m.reshape(per * rdev, size) for m in (mine, theirs)], axis=0)
        sums = jnp.concatenate([r[i, :, columns] for r in sums_refs for i in range(2)], axis=0)
        residual = (measured - dot3(ahead, split(sums))) * inverse
        placed = slice(offset + at, offset + at + size)
        mine_out[:, :, placed] = residual[:per * rdev].reshape(per, rdev, size)
        sent_out[:, :, placed] = residual[per * rdev:].reshape(per, rdev, size)
        given = dot3(back, split(residual))
        for i, ref in enumerate(outs):
            for j in range(2):
                ref[j, :, columns] = given[(2 * i + j) * block:(2 * i + j + 1) * block]


def residual_step(dims, zdev, chunk, offset, width, mats, before, order, table, sums, measured, theirs):
    per, groups, zb, cells = dims
    _, rdev, total = measured.shape
    first = chunk == 0
    block = zdev * per
    count, rows = 6 * block, 2 * per * rdev
    given = jax.ShapeDtypeStruct((2, block, width), F32)
    piece = jax.ShapeDtypeStruct((per, rdev, offset + width), F32)
    shapes = [piece, piece, given, given, given]
    if first:
        args, specs = [order, table], [IN_SMEM, IN_VMEM]
        ahead, back = jax.ShapeDtypeStruct((rows, count), BF16), jax.ShapeDtypeStruct((count, rows), BF16)
        shapes += [ahead, ahead, back, back, jax.ShapeDtypeStruct((rows, LANES), F32)]
    else:
        args, specs = list(mats), [IN_VMEM] * len(mats)
    args += [*sums, measured, theirs, *before]
    specs += [IN_VMEM] * (5 + len(before))
    return pl.pallas_call(
        functools.partial(residual_kernel, dims, first, total // 2, rdev, zdev, offset, width),
        in_specs=specs,
        out_specs=[IN_VMEM] * len(shapes),
        out_shape=shapes,
        compiler_params=pltpu.CompilerParams(vmem_limit_bytes=30 * MIB),
        cost_estimate=pl.CostEstimate(
            flops=12 * count * rows * width, bytes_accessed=8 * width * (count + rows), transcendentals=0
        ),
        name=f"residual_{chunk}",
    )(*args)


def update_kernel(dims, first, halves, half, offset, width, *refs):
    per, groups, zb, cells = dims
    count = groups * SUBLANES
    left_ref, backs, refs = refs[0], refs[len(halves) * groups:0:-1], refs[1 + len(halves) * groups:]
    vol_ref, *refs = refs
    zdev, depth = vol_ref.shape[1], left_ref.shape[2]
    if not first:
        refs = refs[1:]
    pieces = refs[:-3]
    if pieces:
        *pieces, out_ref, res_ref, buf, sems, res_sems = refs
    else:
        out_ref, buf, sems = refs
    odd = lax.rem(lax.axis_index("slab"), 2)
    leaving = []
    for h, ref in enumerate(pieces):
        columns = pl.ds(pl.multiple_of(lax.rem(odd + h, 2) * half, LANES), half)
        leaving.append(pltpu.make_async_copy(ref, res_ref.at[:, :, columns], res_sems.at[h]))
        leaving[-1].start()
    held = len(halves) < vol_ref.shape[0]
    for i, zp, slices, start in volume_pieces(dims, zdev, half, offset, halves):
        rows = slice(zp * SUBLANES, (zp + 1) * SUBLANES)
        left = left_ref[zp]
        for at, size in tiles(width):
            piece = slice(at, at + size)
            back = jnp.concatenate([backs[i * groups + d][rows, piece] for d in range(groups)], axis=0)
            high, low = split(back)
            pad = jnp.zeros((depth - 3 * count, size), BF16)
            change = dot(left, jnp.concatenate([high, low, high, pad], axis=0))
            for z in range(zb):
                buf[i, zp * zb + z, :, piece] = (
                    vol_ref[halves[i] if held else i, zp * zb + z, :, piece] + change[z * cells:(z + 1) * cells]
                )
        leaving.append(
            pltpu.make_async_copy(buf.at[i, slices], out_ref.at[slices, :, pl.ds(start, width)], sems.at[i, zp])
        )
        leaving[-1].start()
    for copy in leaving:
        copy.wait()


def update_step(dims, chunk, halves, offset, width, left, backs, pieces, kept, volume, out):
    per, groups, zb, cells = dims
    zdev, _, total = volume.shape
    first = out is None
    args = [left, *backs[::-1], kept]
    shapes = [jax.ShapeDtypeStruct(volume.shape, F32)]
    scratch = [
        pltpu.VMEM((len(halves), zdev, cells, width), F32),
        pltpu.SemaphoreType.DMA((len(halves), zdev // zb)),
    ]
    specs = [IN_VMEM] * len(args)
    aliases = {}
    if not first:
        aliases = {len(args): 0}
        args += [out]
        specs += [ANYWHERE]
    if pieces:
        args += pieces
        specs += [IN_VMEM] * 2
        shapes += [jax.ShapeDtypeStruct((*pieces[0].shape[:2], total), F32)]
        scratch += [pltpu.SemaphoreType.DMA((2,))]
    size = zdev * cells * width * len(halves)
    return pl.pallas_call(
        functools.partial(update_kernel, dims, first, halves, total // 2, offset, width),
        in_specs=specs,
        out_specs=[ANYWHERE] * len(shapes),
        out_shape=shapes,
        scratch_shapes=scratch,
        input_output_aliases=aliases,
        compiler_params=pltpu.CompilerParams(vmem_limit_bytes=20 * MIB),
        cost_estimate=pl.CostEstimate(flops=2 * size * 48, bytes_accessed=size * 4, transcendentals=0),
        name=f"update_{chunk}_{halves[0]}",
    )(*args)


def body(volume, measured, foot_start, foot_len, order, table):
    slabs, groups = lax.axis_size("slab"), lax.axis_size("ang")
    per, rdev, total = measured.shape
    zdev, cells, _ = volume.shape
    half = total // 2
    zb = SUBLANES // per
    dims = (per, groups, zb, cells)
    each = half // CHUNKS
    widths = [each] * CHUNKS
    offsets = [sum(widths[:c]) for c in range(CHUNKS)]

    def along(value, to):
        pairs = [(s, to(s)) for s in range(slabs)]
        return lax.ppermute(value, "slab", pairs)

    def spread(value, other, d):
        if not (other or d):
            return value
        pairs = [
            (s * groups + a, (s ^ other) * groups + (a + d) % groups) for s in range(slabs) for a in range(groups)
        ]
        return lax.ppermute(value, ("slab", "ang"), pairs)

    def facing(s):
        return s ^ 2

    def step(up, busy):
        def to(s):
            there = s + 4 if up(s) else s - 4
            if 0 <= there < slabs:
                return there
            return there % slabs if busy else facing(s)
        return to

    def beyond(c):
        return step(lambda s: not s & 2, c < CHUNKS - 1)

    def back_from_beyond(c):
        return step(lambda s: s & 2, c > 0)

    odd = lax.rem(lax.axis_index("slab"), 2)
    theirs = along(
        lax.dynamic_slice_in_dim(measured, (1 - odd) * half, half, 2).astype(F32), lambda s: s ^ 1
    )

    sums, kept, left = [], [[] for _ in range(CHUNKS)], None
    for c in range(CHUNKS):
        parts = []
        for halves in RAY_HALVES[c]:
            made = ray_sums(
                dims, c, halves, offsets[c], widths[c], left, (order, foot_start, foot_len), table, volume
            )
            parts += made[:len(halves) * groups]
            if left is None:
                left = made[-1]
            elif c:
                kept[c] += [(h, made[-1]) for h in halves]
        parts = [spread(parts[h * groups + d], h, d) for h in range(2) for d in range(groups)]
        if c:
            parts, _ = lax.optimization_barrier((parts, sums[-1][0]))
        own = jnp.stack([sum(parts[:groups]), sum(parts[groups:])])
        near = along(own, facing)
        if c == 0:
            first_columns, update_left = prepare_step(dims, rdev, widths[0], order, table, own, near, volume)
            kept[0] = [(h, first_columns) for h in range(2)]
        if c == 1:
            near, first_columns = lax.optimization_barrier((near, first_columns))
        far = along(near, beyond(c))
        sums.append((own, near, far))
    pieces, given, mats = [], [], None
    for c in range(CHUNKS):
        mine, sent, own, near, far, *rest = residual_step(
            dims, zdev, c, offsets[c], widths[c], mats, pieces, order, table, sums[c], measured, theirs
        )
        pieces = [mine, sent]
        mats = rest if c == 0 else mats
        near = near + along(far, back_from_beyond(c))
        arrived = along(near, facing)
        halves = [own[i] + arrived[i] for i in range(2)]
        given.append([spread(halves[h], h, d) for h in range(2) for d in range(groups)])
    pieces = [mine, along(sent, lambda s: s ^ 1)]
    out, res = None, []
    for c in range(CHUNKS):
        for halves in UPDATE_HALVES[c]:
            backs = [b for h in halves for b in given[c][h * groups:(h + 1) * groups]]
            write = c == CHUNKS - 1 and halves[0] == 0
            out, *made = update_step(
                dims, c, halves, offsets[c], widths[c], update_left, backs, pieces if write else [],
                dict(kept[c])[halves[0]], volume, out,
            )
            res += made
    return out, res[0]


def solution(mesh):
    return jax.shard_map(
        body,
        mesh=mesh,
        in_specs=(
            P("slab", "ang", None),
            P("ang", "slab", None),
            P("slab", "ang"),
            P("slab", "ang"),
            P(),
            P(),
        ),
        out_specs=(P("slab", "ang", None), P("ang", "slab", None)),
        check_vma=False,
    )
```

```python
import functools

import jax
import jax.numpy as jnp
from jax import lax
from jax.experimental import pallas as pl
from jax.experimental.pallas import tpu as pltpu
from jax.sharding import PartitionSpec as P

F32, BF16 = jnp.float32, jnp.bfloat16
CHUNKS = 2
RAY_HALVES = [[(0, 1)], [(0, 1)]]
UPDATE_HALVES = [[(0, 1)], [(0,), (1,)]]
TILE = 512
LANES = 128
SUBLANES = 8
MIB = 1024 * 1024

IN_VMEM = pl.BlockSpec(memory_space=pltpu.VMEM)
IN_SMEM = pl.BlockSpec(memory_space=pltpu.SMEM)
ANYWHERE = pl.BlockSpec(memory_space=pl.ANY)


def split(value):
    high = value.astype(BF16)
    return high, (value - high.astype(F32)).astype(BF16)


def dot(a, b):
    return jnp.dot(a, b, preferred_element_type=F32)


def dot3(a, b):
    return dot(a[0], b[0]) + (dot(a[0], b[1]) + dot(a[1], b[0]))


def iota(shape, dim):
    return lax.broadcasted_iota(jnp.int32, shape, dim)


def low_bits(value, size):
    assert size & (size - 1) == 0
    return value & (size - 1)


def over(value, size):
    assert size & (size - 1) == 0
    return value >> (size.bit_length() - 1)


def pick(index, values):
    out = jnp.zeros(index.shape, values[0].dtype)
    for at, value in enumerate(values):
        out = jnp.where(index == at, value, out)
    return out


def tiles(width):
    step = min(TILE, width)
    return [(at, min(step, width - at)) for at in range(0, width, step)]


def slice_weights(dims, sign, order_ref, table_ref, rows_ref):
    per, groups, zb, cells = dims
    ang = lax.axis_index("ang")
    for d in range(groups):
        group = lax.rem(ang + sign * d + groups, groups)
        for z in range(zb):
            for a in range(per):
                at = (d * zb + z) * per + a
                rows_ref[at:at + 1, :] = table_ref[pl.ds(order_ref[group * per + a], 1), :]
    wide = rows_ref[...]
    total = wide.shape[1]
    row_slice = low_bits(over(iota(wide.shape, 0), per), zb)
    lane_slice = over(iota(wide.shape, 1), cells)
    out = jnp.zeros_like(wide)
    for z in range(zb):
        shift = lax.rem(z * cells - ang * cells + total, total)
        here = jnp.logical_and(row_slice == z, lane_slice == z)
        out = jnp.where(here, pltpu.roll(wide, shift, 1), out)
    return out


def volume_pieces(dims, zdev, half, offset, halves):
    odd = lax.rem(lax.axis_index("slab"), 2)
    zb = dims[2]
    for i, h in enumerate(halves):
        start = pl.multiple_of(lax.rem(odd + h, 2) * half + offset, LANES)
        for zp in range(zdev // zb):
            yield i, zp, slice(zp * zb, (zp + 1) * zb), start


def rays_kernel(dims, first, keep, extra, halves, half, offset, width, *refs):
    per, groups, zb, cells = dims
    count = groups * SUBLANES
    if first:
        order_ref, start_ref, len_ref, table_ref, vol_ref, *refs = refs
    elif extra:
        start_buf, len_buf, given_ref, vol_ref, *refs = refs
    else:
        given_ref, vol_ref, *refs = refs
    outs, refs = refs[:len(halves) * groups], refs[len(halves) * groups:]
    if first:
        left_ref, buf, sems, table_buf, order_buf, start_buf, len_buf, rows_ref, small_sems = refs
    else:
        buf, sems = refs
    zdev = vol_ref.shape[0]
    copies = []
    if first:
        small = [
            pltpu.make_async_copy(source, to, small_sems.at[i])
            for i, (source, to) in enumerate(
                [(order_ref, order_buf), (table_ref, table_buf), (start_ref, start_buf), (len_ref, len_buf)]
            )
        ]
        for copy in small:
            copy.start()
    for h, zp, slices, start in volume_pieces(dims, zdev, half, offset, halves):
        source = vol_ref.at[slices, :, pl.ds(start, width)]
        copies.append((h, zp, pltpu.make_async_copy(source, buf.at[h, slices], sems.at[h, zp])))
        copies[-1][-1].start()
    if first:
        small[0].wait()
        small[1].wait()
        both = jnp.concatenate(split(slice_weights(dims, 1, order_buf, table_buf, rows_ref)), axis=0)
        left = jnp.concatenate([both, both], axis=1)
        left_ref[...] = left
        small[2].wait()
        small[3].wait()
    else:
        left = given_ref[...]
    if extra:
        shape = (SUBLANES, LANES)
        angle, lane = low_bits(iota(shape, 0), per), iota(shape, 1)
        starts = pick(angle, [start_buf[0, a].astype(F32) for a in range(per)])
        lengths = pick(angle, [len_buf[0, a].astype(F32) for a in range(per)])
        for d in range(groups):
            foot = jnp.where(lane == 2 * d, starts, jnp.where(lane == 2 * d + 1, lengths, 0.0))
            for h in range(len(halves)):
                outs[h * groups + d][:, zdev // zb * width:] = foot
    for h, zp, copy in copies:
        copy.wait()
        for at, size in tiles(width):
            parts = [split(buf[h, zp * zb + z, :, at:at + size]) for z in range(zb)]
            product = dot(left, jnp.concatenate([p[0] for p in parts] + [p[1] for p in parts], axis=0))
            sums = product[:count] + product[count:]
            for d in range(groups):
                outs[h * groups + d][:, zp * width + at:zp * width + at + size] = (
                    sums[d * SUBLANES:(d + 1) * SUBLANES]
                )


def ray_sums(dims, chunk, halves, offset, width, given, small, table, volume):
    per, groups, zb, cells = dims
    zdev, _, total = volume.shape
    first, keep, extra = given is None, chunk > 0, chunk == 0
    count, all_cells = groups * SUBLANES, table.shape[1]
    out = jax.ShapeDtypeStruct((SUBLANES, zdev // zb * width + (LANES if extra else 0)), F32)
    left = jax.ShapeDtypeStruct((2 * count, 2 * zb * cells), BF16)
    columns = (len(halves), zdev, cells, width)
    assert zb * cells == all_cells
    shapes = [out] * (len(halves) * groups)
    scratch = [] if keep else [pltpu.VMEM(columns, F32)]
    scratch += [pltpu.SemaphoreType.DMA((len(halves), zdev // zb))]
    args, specs, limit = [given, volume], [IN_VMEM, ANYWHERE], 40
    if first:
        scratch += [pltpu.VMEM(table.shape, F32)] + [pltpu.SMEM(a.shape, a.dtype) for a in small]
        scratch += [pltpu.VMEM((count, all_cells), F32), pltpu.SemaphoreType.DMA((4,))]
        args, specs, limit = [*small, table, volume], [ANYWHERE] * 5, 58
        shapes += [left]
    elif extra:
        args, specs, limit = [*small[1:], *args], [IN_SMEM] * 2 + specs, 50
    if keep:
        shapes += [jax.ShapeDtypeStruct(columns, F32)]
    size = zdev * cells * width * len(halves)
    return pl.pallas_call(
        functools.partial(rays_kernel, dims, first, keep, extra, halves, total // 2, offset, width),
        in_specs=specs,
        out_specs=[IN_VMEM] * len(shapes),
        out_shape=shapes,
        scratch_shapes=scratch,
        compiler_params=pltpu.CompilerParams(vmem_limit_bytes=limit * MIB),
        cost_estimate=pl.CostEstimate(flops=2 * size * 16, bytes_accessed=size * 4, transcendentals=0),
        name=f"ray_sums_{chunk}_{halves[0]}",
    )(*args)


def hat_weights(dims, zdev, start, length, row):
    per, groups, zb, cells = dims
    at = low_bits(iota(start.shape, 0), zdev * per)
    slice_at = over(at, zb * per) * zb + low_bits(over(at, per), zb)
    span = jnp.where(length > 0.0, length, 1.0) / zdev
    centre = start + (slice_at.astype(F32) + 0.5) * span
    hat = jnp.maximum(0.0, 1.0 - jnp.abs(row + 0.5 - centre) / span)
    return jnp.where(jnp.logical_and(row >= start, row < start + length), hat, 0.0)


def footprint_matrix(dims, zdev, rdev, foot):
    per = dims[0]
    rows = 2 * per * rdev
    slab = lax.axis_index("slab")
    sibling = slab + 1 - 2 * lax.rem(slab, 2)
    row_id = iota((1, rows), 1)
    row_slab = jnp.where(row_id < per * rdev, slab, sibling)
    row = (row_slab * rdev + low_bits(row_id, rdev)).astype(F32)
    shape = (foot.shape[0], rows)
    same_angle = low_bits(iota(shape, 0), per) == low_bits(over(iota(shape, 1), rdev), per)
    beyond = slab + jnp.where(low_bits(slab, 4) < 2, -2, 2)
    there = jnp.logical_and(beyond >= 0, beyond < lax.axis_size("slab"))
    known = jnp.where(there, foot.shape[0], foot.shape[0] // 3 * 2)
    meets = jnp.logical_and(same_angle, iota(shape, 0) < known)
    return jnp.where(meets, hat_weights(dims, zdev, foot[:, 0:1], foot[:, 1:2], row), 0.0)


def update_weights(dims, zdev, rdev, foot, order_ref, table_ref, rows_ref, out_ref):
    per, groups, zb, cells = dims
    count = groups * SUBLANES
    weights = slice_weights(dims, -1, order_ref, table_ref, rows_ref)
    window = -(-5 * rdev // LANES) * LANES
    row = ((lax.axis_index("slab") - 2) * rdev + iota((1, window), 1)).astype(F32)
    sums = [
        jnp.sum(hat_weights(dims, zdev, foot[:, 2 * d:2 * d + 1], foot[:, 2 * d + 1:2 * d + 2], row), axis=1, keepdims=True)
        for d in range(groups)
    ]
    pad = jnp.zeros((out_ref.shape[2] - 3 * count, weights.shape[1]), F32)
    for zp in range(zdev // zb):
        slices = jnp.concatenate([s[zp * SUBLANES:(zp + 1) * SUBLANES] for s in sums], axis=0)
        scaled = weights / jnp.sum(weights * slices, axis=0, keepdims=True)
        high = scaled.astype(BF16).astype(F32)
        stacked = jnp.concatenate([high, high, scaled - high, pad], axis=0)
        out_ref[zp] = stacked.T.astype(BF16)


def prepare_kernel(dims, rdev, half, width, order_ref, table_ref, foot_ref, _, vol_ref, kept_ref, left_ref, sems, rows_ref):
    zdev = vol_ref.shape[0]
    copies = []
    for h, zp, slices, start in volume_pieces(dims, zdev, half, 0, (0, 1)):
        source = vol_ref.at[slices, :, pl.ds(start, width)]
        copies.append(pltpu.make_async_copy(source, kept_ref.at[h, slices], sems.at[h, zp]))
        copies[-1].start()
    batches = zdev // dims[2]
    foot = jnp.concatenate([foot_ref[0, :, batches * width:]] * batches, axis=0)
    update_weights(dims, zdev, rdev, foot, order_ref, table_ref, rows_ref, left_ref)
    for copy in copies:
        copy.wait()


def prepare_step(dims, rdev, width, order, table, own, after, volume):
    per, groups, zb, cells = dims
    zdev, _, total = volume.shape
    depth = -(-3 * groups * SUBLANES // LANES) * LANES
    return pl.pallas_call(
        functools.partial(prepare_kernel, dims, rdev, total // 2, width),
        in_specs=[IN_SMEM, IN_VMEM, IN_VMEM, ANYWHERE, ANYWHERE],
        out_specs=[IN_VMEM, IN_VMEM],
        out_shape=[
            jax.ShapeDtypeStruct((2, zdev, cells, width), F32),
            jax.ShapeDtypeStruct((zdev // zb, zb * cells, depth), BF16),
        ],
        scratch_shapes=[
            pltpu.SemaphoreType.DMA((2, zdev // zb)),
            pltpu.VMEM((groups * SUBLANES, table.shape[1]), F32),
        ],
        compiler_params=pltpu.CompilerParams(vmem_limit_bytes=40 * MIB),
        cost_estimate=pl.CostEstimate(flops=0, bytes_accessed=8 * zdev * cells * width, transcendentals=0),
        name="prepare",
    )(order, table, own, after, volume)


def residual_kernel(dims, first, half, rdev, zdev, offset, width, *refs):
    per, groups, zb, cells = dims
    block = zdev * per
    if first:
        order_ref, table_ref, *refs = refs
    else:
        mats, inverse_ref, refs = refs[:4], refs[4], refs[5:]
    sums_refs, (mine_ref, theirs_ref), refs = refs[:3], refs[3:5], refs[5:]
    if not first:
        mine_before, sent_before, *refs = refs
    mine_out, sent_out, *refs = refs
    if not first:
        mine_out[:, :, :offset] = mine_before[...]
        sent_out[:, :, :offset] = sent_before[...]
    outs, refs = refs[:3], refs[3:]
    if first:
        foot = jnp.concatenate(
            [r[i, :, zdev // zb * width:] for r in sums_refs for i in range(2) for _ in range(zdev // zb)], axis=0
        )
        kernel = footprint_matrix(dims, zdev, rdev, foot)
        count, rows = kernel.shape
        kernel_t = kernel.T
        cover = jnp.sum(kernel_t, axis=1, keepdims=True)
        angle = low_bits(over(iota((rows, 1), 0), rdev), per)
        path = jnp.zeros((rows, 1), F32)
        for a in range(per):
            at = order_ref[lax.axis_index("ang") * per + a]
            path = jnp.where(angle == a, jnp.sum(table_ref[pl.ds(at, 1), :], axis=1, keepdims=True), path)
        inverse = 1.0 / jnp.maximum(path * cover, 0.25)
        ahead, back = split(kernel_t), split(kernel)
        for ref, value in zip(refs, (*ahead, *back)):
            ref[...] = value
        refs[4][...] = jnp.broadcast_to(inverse, (rows, LANES))
    else:
        ahead, back = (mats[0][...], mats[1][...]), (mats[2][...], mats[3][...])
        inverse = inverse_ref[:, 0:1]
    start = lax.rem(lax.axis_index("slab"), 2) * half + offset
    for at, size in tiles(width):
        columns = slice(at, at + size)
        mine = mine_ref[:, :, pl.ds(pl.multiple_of(start + at, LANES), size)].astype(F32)
        theirs = theirs_ref[:, :, offset + at:offset + at + size]
        measured = jnp.concatenate([m.reshape(per * rdev, size) for m in (mine, theirs)], axis=0)
        sums = jnp.concatenate(
            [
                r[i, :, zp * width + at:zp * width + at + size]
                for r in sums_refs for i in range(2) for zp in range(zdev // zb)
            ],
            axis=0,
        )
        residual = (measured - dot3(ahead, split(sums))) * inverse
        placed = slice(offset + at, offset + at + size)
        mine_out[:, :, placed] = residual[:per * rdev].reshape(per, rdev, size)
        sent_out[:, :, placed] = residual[per * rdev:].reshape(per, rdev, size)
        given = dot3(back, split(residual))
        for i, ref in enumerate(outs):
            for j in range(2):
                ref[j, :, columns] = given[(2 * i + j) * block:(2 * i + j + 1) * block]


def residual_step(dims, zdev, chunk, offset, width, mats, before, order, table, sums, measured, theirs):
    per, groups, zb, cells = dims
    _, rdev, total = measured.shape
    first = chunk == 0
    block = zdev * per
    count, rows = 6 * block, 2 * per * rdev
    given = jax.ShapeDtypeStruct((2, block, width), F32)
    piece = jax.ShapeDtypeStruct((per, rdev, offset + width), F32)
    shapes = [piece, piece, given, given, given]
    if first:
        args, specs = [order, table], [IN_SMEM, IN_VMEM]
        ahead, back = jax.ShapeDtypeStruct((rows, count), BF16), jax.ShapeDtypeStruct((count, rows), BF16)
        shapes += [ahead, ahead, back, back, jax.ShapeDtypeStruct((rows, LANES), F32)]
    else:
        args, specs = list(mats), [IN_VMEM] * len(mats)
    args += [*sums, measured, theirs, *before]
    specs += [IN_VMEM] * (5 + len(before))
    return pl.pallas_call(
        functools.partial(residual_kernel, dims, first, total // 2, rdev, zdev, offset, width),
        in_specs=specs,
        out_specs=[IN_VMEM] * len(shapes),
        out_shape=shapes,
        compiler_params=pltpu.CompilerParams(vmem_limit_bytes=30 * MIB),
        cost_estimate=pl.CostEstimate(
            flops=12 * count * rows * width, bytes_accessed=8 * width * (count + rows), transcendentals=0
        ),
        name=f"residual_{chunk}",
    )(*args)


def update_kernel(dims, first, halves, half, offset, width, *refs):
    per, groups, zb, cells = dims
    count = groups * SUBLANES
    left_ref, backs, refs = refs[0], refs[len(halves) * groups:0:-1], refs[1 + len(halves) * groups:]
    vol_ref, *refs = refs
    zdev, depth = vol_ref.shape[1], left_ref.shape[2]
    if not first:
        refs = refs[1:]
    pieces = refs[:-3]
    if pieces:
        *pieces, out_ref, res_ref, buf, sems, res_sems = refs
    else:
        out_ref, buf, sems = refs
    odd = lax.rem(lax.axis_index("slab"), 2)
    leaving = []
    for h, ref in enumerate(pieces):
        columns = pl.ds(pl.multiple_of(lax.rem(odd + h, 2) * half, LANES), half)
        leaving.append(pltpu.make_async_copy(ref, res_ref.at[:, :, columns], res_sems.at[h]))
        leaving[-1].start()
    held = len(halves) < vol_ref.shape[0]
    for i, zp, slices, start in volume_pieces(dims, zdev, half, offset, halves):
        rows = slice(zp * SUBLANES, (zp + 1) * SUBLANES)
        left = left_ref[zp]
        for at, size in tiles(width):
            piece = slice(at, at + size)
            back = jnp.concatenate([backs[i * groups + d][rows, piece] for d in range(groups)], axis=0)
            high, low = split(back)
            pad = jnp.zeros((depth - 3 * count, size), BF16)
            change = dot(left, jnp.concatenate([high, low, high, pad], axis=0))
            for z in range(zb):
                buf[i, zp * zb + z, :, piece] = (
                    vol_ref[halves[i] if held else i, zp * zb + z, :, piece] + change[z * cells:(z + 1) * cells]
                )
        leaving.append(
            pltpu.make_async_copy(buf.at[i, slices], out_ref.at[slices, :, pl.ds(start, width)], sems.at[i, zp])
        )
        leaving[-1].start()
    for copy in leaving:
        copy.wait()


def update_step(dims, chunk, halves, offset, width, left, backs, pieces, kept, volume, out):
    per, groups, zb, cells = dims
    zdev, _, total = volume.shape
    first = out is None
    args = [left, *backs[::-1], kept]
    shapes = [jax.ShapeDtypeStruct(volume.shape, F32)]
    scratch = [
        pltpu.VMEM((len(halves), zdev, cells, width), F32),
        pltpu.SemaphoreType.DMA((len(halves), zdev // zb)),
    ]
    specs = [IN_VMEM] * len(args)
    aliases = {}
    if not first:
        aliases = {len(args): 0}
        args += [out]
        specs += [ANYWHERE]
    if pieces:
        args += pieces
        specs += [IN_VMEM] * 2
        shapes += [jax.ShapeDtypeStruct((*pieces[0].shape[:2], total), F32)]
        scratch += [pltpu.SemaphoreType.DMA((2,))]
    size = zdev * cells * width * len(halves)
    return pl.pallas_call(
        functools.partial(update_kernel, dims, first, halves, total // 2, offset, width),
        in_specs=specs,
        out_specs=[ANYWHERE] * len(shapes),
        out_shape=shapes,
        scratch_shapes=scratch,
        input_output_aliases=aliases,
        compiler_params=pltpu.CompilerParams(vmem_limit_bytes=20 * MIB),
        cost_estimate=pl.CostEstimate(flops=2 * size * 48, bytes_accessed=size * 4, transcendentals=0),
        name=f"update_{chunk}_{halves[0]}",
    )(*args)


def body(volume, measured, foot_start, foot_len, order, table):
    slabs, groups = lax.axis_size("slab"), lax.axis_size("ang")
    per, rdev, total = measured.shape
    zdev, cells, _ = volume.shape
    half = total // 2
    zb = SUBLANES // per
    dims = (per, groups, zb, cells)
    each = half // CHUNKS
    widths = [each] * CHUNKS
    offsets = [sum(widths[:c]) for c in range(CHUNKS)]

    def along(value, to):
        pairs = [(s, to(s)) for s in range(slabs)]
        return lax.ppermute(value, "slab", pairs)

    def spread(value, other, d):
        if not (other or d):
            return value
        pairs = [
            (s * groups + a, (s ^ other) * groups + (a + d) % groups) for s in range(slabs) for a in range(groups)
        ]
        return lax.ppermute(value, ("slab", "ang"), pairs)

    def facing(s):
        return s ^ 2

    def step(up, busy):
        def to(s):
            there = s + 4 if up(s) else s - 4
            if 0 <= there < slabs:
                return there
            return there % slabs if busy else facing(s)
        return to

    def beyond(c):
        return step(lambda s: not s & 2, c < CHUNKS - 1)

    def back_from_beyond(c):
        return step(lambda s: s & 2, c > 0)

    odd = lax.rem(lax.axis_index("slab"), 2)
    theirs = along(
        lax.dynamic_slice_in_dim(measured, (1 - odd) * half, half, 2).astype(F32), lambda s: s ^ 1
    )

    sums, kept, left = [], [[] for _ in range(CHUNKS)], None
    for c in range(CHUNKS):
        parts = []
        for halves in RAY_HALVES[c]:
            made = ray_sums(
                dims, c, halves, offsets[c], widths[c], left, (order, foot_start, foot_len), table, volume
            )
            parts += made[:len(halves) * groups]
            if left is None:
                left = made[-1]
            elif c:
                kept[c] += [(h, made[-1]) for h in halves]
        parts = [spread(parts[h * groups + d], h, d) for h in range(2) for d in range(groups)]
        if c:
            parts, _ = lax.optimization_barrier((parts, sums[-1][0]))
        own = jnp.stack([sum(parts[:groups]), sum(parts[groups:])])
        near = along(own, facing)
        if c == 0:
            first_columns, update_left = prepare_step(dims, rdev, widths[0], order, table, own, near, volume)
            kept[0] = [(h, first_columns) for h in range(2)]
        if c == 1:
            near, first_columns = lax.optimization_barrier((near, first_columns))
        far = along(near, beyond(c))
        sums.append((own, near, far))
    pieces, given, mats = [], [], None
    for c in range(CHUNKS):
        mine, sent, own, near, far, *rest = residual_step(
            dims, zdev, c, offsets[c], widths[c], mats, pieces, order, table, sums[c], measured, theirs
        )
        pieces = [mine, sent]
        mats = rest if c == 0 else mats
        near = near + along(far, back_from_beyond(c))
        arrived = along(near, facing)
        halves = [own[i] + arrived[i] for i in range(2)]
        given.append([spread(halves[h], h, d) for h in range(2) for d in range(groups)])
    pieces = [mine, along(sent, lambda s: s ^ 1)]
    out, res = None, []
    for c in range(CHUNKS):
        for halves in UPDATE_HALVES[c]:
            backs = [b for h in halves for b in given[c][h * groups:(h + 1) * groups]]
            write = c == CHUNKS - 1 and halves[0] == 0
            out, *made = update_step(
                dims, c, halves, offsets[c], widths[c], update_left, backs, pieces if write else [],
                dict(kept[c])[halves[0]], volume, out,
            )
            res += made
    return out, res[0]


def solution(mesh):
    return jax.shard_map(
        body,
        mesh=mesh,
        in_specs=(
            P("slab", "ang", None),
            P("ang", "slab", None),
            P("slab", "ang"),
            P("slab", "ang"),
            P(),
            P(),
        ),
        out_specs=(P("slab", "ang", None), P("ang", "slab", None)),
        check_vma=False,
    )
```

```python
import functools

import jax
import jax.numpy as jnp
from jax import lax
from jax.experimental import pallas as pl
from jax.experimental.pallas import tpu as pltpu
from jax.sharding import PartitionSpec as P

F32, BF16 = jnp.float32, jnp.bfloat16
CHUNKS = 2
RAY_HALVES = [[(0, 1)], [(0, 1)]]
UPDATE_HALVES = [[(0, 1)], [(0,), (1,)]]
TILE = 512
LANES = 128
SUBLANES = 8
MIB = 1024 * 1024

IN_VMEM = pl.BlockSpec(memory_space=pltpu.VMEM)
IN_SMEM = pl.BlockSpec(memory_space=pltpu.SMEM)
ANYWHERE = pl.BlockSpec(memory_space=pl.ANY)


def split(value):
    high = value.astype(BF16)
    return high, (value - high.astype(F32)).astype(BF16)


def dot(a, b):
    return jnp.dot(a, b, preferred_element_type=F32)


def dot3(a, b):
    return dot(a[0], b[0]) + (dot(a[0], b[1]) + dot(a[1], b[0]))


def iota(shape, dim):
    return lax.broadcasted_iota(jnp.int32, shape, dim)


def low_bits(value, size):
    assert size & (size - 1) == 0
    return value & (size - 1)


def over(value, size):
    assert size & (size - 1) == 0
    return value >> (size.bit_length() - 1)


def pick(index, values):
    out = jnp.zeros(index.shape, values[0].dtype)
    for at, value in enumerate(values):
        out = jnp.where(index == at, value, out)
    return out


def tiles(width):
    step = min(TILE, width)
    return [(at, min(step, width - at)) for at in range(0, width, step)]


def slice_weights(dims, sign, order_ref, table_ref, rows_ref):
    per, groups, zb, cells = dims
    ang = lax.axis_index("ang")
    for d in range(groups):
        group = lax.rem(ang + sign * d + groups, groups)
        for z in range(zb):
            for a in range(per):
                at = (d * zb + z) * per + a
                rows_ref[at:at + 1, :] = table_ref[pl.ds(order_ref[group * per + a], 1), :]
    wide = rows_ref[...]
    total = wide.shape[1]
    row_slice = low_bits(over(iota(wide.shape, 0), per), zb)
    lane_slice = over(iota(wide.shape, 1), cells)
    out = jnp.zeros_like(wide)
    for z in range(zb):
        shift = lax.rem(z * cells - ang * cells + total, total)
        here = jnp.logical_and(row_slice == z, lane_slice == z)
        out = jnp.where(here, pltpu.roll(wide, shift, 1), out)
    return out


def volume_pieces(dims, zdev, half, offset, halves):
    odd = lax.rem(lax.axis_index("slab"), 2)
    zb = dims[2]
    for i, h in enumerate(halves):
        start = pl.multiple_of(lax.rem(odd + h, 2) * half + offset, LANES)
        for zp in range(zdev // zb):
            yield i, zp, slice(zp * zb, (zp + 1) * zb), start


def rays_kernel(dims, first, keep, extra, halves, half, offset, width, *refs):
    per, groups, zb, cells = dims
    count = groups * SUBLANES
    if first:
        order_ref, start_ref, len_ref, table_ref, vol_ref, *refs = refs
    elif extra:
        start_buf, len_buf, given_ref, vol_ref, *refs = refs
    else:
        given_ref, vol_ref, *refs = refs
    outs, refs = refs[:len(halves) * groups], refs[len(halves) * groups:]
    if first:
        left_ref, buf, sems, table_buf, order_buf, start_buf, len_buf, rows_ref, small_sems = refs
    else:
        buf, sems = refs
    zdev = vol_ref.shape[0]
    copies = []
    if first:
        small = [
            pltpu.make_async_copy(source, to, small_sems.at[i])
            for i, (source, to) in enumerate(
                [(order_ref, order_buf), (table_ref, table_buf), (start_ref, start_buf), (len_ref, len_buf)]
            )
        ]
        for copy in small:
            copy.start()
    for h, zp, slices, start in volume_pieces(dims, zdev, half, offset, halves):
        source = vol_ref.at[slices, :, pl.ds(start, width)]
        copies.append((h, zp, pltpu.make_async_copy(source, buf.at[h, slices], sems.at[h, zp])))
        copies[-1][-1].start()
    if first:
        small[0].wait()
        small[1].wait()
        both = jnp.concatenate(split(slice_weights(dims, 1, order_buf, table_buf, rows_ref)), axis=0)
        left = jnp.concatenate([both, both], axis=1)
        left_ref[...] = left
        small[2].wait()
        small[3].wait()
    else:
        left = given_ref[...]
    if extra:
        shape = (SUBLANES, LANES)
        angle, lane = low_bits(iota(shape, 0), per), iota(shape, 1)
        starts = pick(angle, [start_buf[0, a].astype(F32) for a in range(per)])
        lengths = pick(angle, [len_buf[0, a].astype(F32) for a in range(per)])
        for d in range(groups):
            foot = jnp.where(lane == 2 * d, starts, jnp.where(lane == 2 * d + 1, lengths, 0.0))
            for h in range(len(halves)):
                outs[h * groups + d][:, zdev // zb * width:] = foot
    for h, zp, copy in copies:
        copy.wait()
        for at, size in tiles(width):
            parts = [split(buf[h, zp * zb + z, :, at:at + size]) for z in range(zb)]
            product = dot(left, jnp.concatenate([p[0] for p in parts] + [p[1] for p in parts], axis=0))
            sums = product[:count] + product[count:]
            for d in range(groups):
                outs[h * groups + d][:, zp * width + at:zp * width + at + size] = (
                    sums[d * SUBLANES:(d + 1) * SUBLANES]
                )


def ray_sums(dims, chunk, halves, offset, width, given, small, table, volume):
    per, groups, zb, cells = dims
    zdev, _, total = volume.shape
    first, keep, extra = given is None, chunk > 0, chunk == 0
    count, all_cells = groups * SUBLANES, table.shape[1]
    out = jax.ShapeDtypeStruct((SUBLANES, zdev // zb * width + (LANES if extra else 0)), F32)
    left = jax.ShapeDtypeStruct((2 * count, 2 * zb * cells), BF16)
    columns = (len(halves), zdev, cells, width)
    assert zb * cells == all_cells
    shapes = [out] * (len(halves) * groups)
    scratch = [] if keep else [pltpu.VMEM(columns, F32)]
    scratch += [pltpu.SemaphoreType.DMA((len(halves), zdev // zb))]
    args, specs, limit = [given, volume], [IN_VMEM, ANYWHERE], 40
    if first:
        scratch += [pltpu.VMEM(table.shape, F32)] + [pltpu.SMEM(a.shape, a.dtype) for a in small]
        scratch += [pltpu.VMEM((count, all_cells), F32), pltpu.SemaphoreType.DMA((4,))]
        args, specs, limit = [*small, table, volume], [ANYWHERE] * 5, 58
        shapes += [left]
    elif extra:
        args, specs, limit = [*small[1:], *args], [IN_SMEM] * 2 + specs, 50
    if keep:
        shapes += [jax.ShapeDtypeStruct(columns, F32)]
    size = zdev * cells * width * len(halves)
    return pl.pallas_call(
        functools.partial(rays_kernel, dims, first, keep, extra, halves, total // 2, offset, width),
        in_specs=specs,
        out_specs=[IN_VMEM] * len(shapes),
        out_shape=shapes,
        scratch_shapes=scratch,
        compiler_params=pltpu.CompilerParams(vmem_limit_bytes=limit * MIB),
        cost_estimate=pl.CostEstimate(flops=2 * size * 16, bytes_accessed=size * 4, transcendentals=0),
        name=f"ray_sums_{chunk}_{halves[0]}",
    )(*args)


def hat_weights(dims, zdev, start, length, row):
    per, groups, zb, cells = dims
    at = low_bits(iota(start.shape, 0), zdev * per)
    slice_at = over(at, zb * per) * zb + low_bits(over(at, per), zb)
    span = jnp.where(length > 0.0, length, 1.0) / zdev
    centre = start + (slice_at.astype(F32) + 0.5) * span
    hat = jnp.maximum(0.0, 1.0 - jnp.abs(row + 0.5 - centre) / span)
    return jnp.where(jnp.logical_and(row >= start, row < start + length), hat, 0.0)


def footprint_matrix(dims, zdev, rdev, foot):
    per = dims[0]
    rows = 2 * per * rdev
    slab = lax.axis_index("slab")
    sibling = slab + 1 - 2 * lax.rem(slab, 2)
    row_id = iota((1, rows), 1)
    row_slab = jnp.where(row_id < per * rdev, slab, sibling)
    row = (row_slab * rdev + low_bits(row_id, rdev)).astype(F32)
    shape = (foot.shape[0], rows)
    same_angle = low_bits(iota(shape, 0), per) == low_bits(over(iota(shape, 1), rdev), per)
    beyond = slab + jnp.where(low_bits(slab, 4) < 2, -2, 2)
    there = jnp.logical_and(beyond >= 0, beyond < lax.axis_size("slab"))
    known = jnp.where(there, foot.shape[0], foot.shape[0] // 3 * 2)
    meets = jnp.logical_and(same_angle, iota(shape, 0) < known)
    return jnp.where(meets, hat_weights(dims, zdev, foot[:, 0:1], foot[:, 1:2], row), 0.0)


def update_weights(dims, zdev, rdev, foot, order_ref, table_ref, rows_ref, out_ref):
    per, groups, zb, cells = dims
    count = groups * SUBLANES
    weights = slice_weights(dims, -1, order_ref, table_ref, rows_ref)
    window = -(-5 * rdev // LANES) * LANES
    row = ((lax.axis_index("slab") - 2) * rdev + iota((1, window), 1)).astype(F32)
    sums = [
        jnp.sum(hat_weights(dims, zdev, foot[:, 2 * d:2 * d + 1], foot[:, 2 * d + 1:2 * d + 2], row), axis=1, keepdims=True)
        for d in range(groups)
    ]
    pad = jnp.zeros((out_ref.shape[2] - 3 * count, weights.shape[1]), F32)
    for zp in range(zdev // zb):
        slices = jnp.concatenate([s[zp * SUBLANES:(zp + 1) * SUBLANES] for s in sums], axis=0)
        scaled = weights / jnp.sum(weights * slices, axis=0, keepdims=True)
        high = scaled.astype(BF16).astype(F32)
        stacked = jnp.concatenate([high, high, scaled - high, pad], axis=0)
        out_ref[zp] = stacked.T.astype(BF16)


def prepare_kernel(dims, rdev, half, width, order_ref, table_ref, foot_ref, _, vol_ref, kept_ref, left_ref, sems, rows_ref):
    zdev = vol_ref.shape[0]
    copies = []
    for h, zp, slices, start in volume_pieces(dims, zdev, half, 0, (0,)):
        source = vol_ref.at[slices, :, pl.ds(start, width)]
        copies.append(pltpu.make_async_copy(source, kept_ref.at[h, slices], sems.at[h, zp]))
        copies[-1].start()
    batches = zdev // dims[2]
    foot = jnp.concatenate([foot_ref[0, :, batches * width:]] * batches, axis=0)
    update_weights(dims, zdev, rdev, foot, order_ref, table_ref, rows_ref, left_ref)
    for copy in copies:
        copy.wait()


def prepare_step(dims, rdev, width, order, table, own, after, volume):
    per, groups, zb, cells = dims
    zdev, _, total = volume.shape
    depth = -(-3 * groups * SUBLANES // LANES) * LANES
    return pl.pallas_call(
        functools.partial(prepare_kernel, dims, rdev, total // 2, width),
        in_specs=[IN_SMEM, IN_VMEM, IN_VMEM, ANYWHERE, ANYWHERE],
        out_specs=[IN_VMEM, IN_VMEM],
        out_shape=[
            jax.ShapeDtypeStruct((1, zdev, cells, width), F32),
            jax.ShapeDtypeStruct((zdev // zb, zb * cells, depth), BF16),
        ],
        scratch_shapes=[
            pltpu.SemaphoreType.DMA((1, zdev // zb)),
            pltpu.VMEM((groups * SUBLANES, table.shape[1]), F32),
        ],
        compiler_params=pltpu.CompilerParams(vmem_limit_bytes=40 * MIB),
        cost_estimate=pl.CostEstimate(flops=0, bytes_accessed=8 * zdev * cells * width, transcendentals=0),
        name="prepare",
    )(order, table, own, after, volume)


def residual_columns(half, which):
    odd = lax.rem(lax.axis_index("slab"), 2)
    return pl.ds(pl.multiple_of(lax.rem(odd + which, 2) * half, LANES), half)


def load_kernel(dims, half, width, _, vol_ref, mine_ref, kept_ref, res_ref, sems, res_sem):
    copies = []
    for h, zp, slices, start in volume_pieces(dims, vol_ref.shape[0], half, 0, (1,)):
        source = vol_ref.at[slices, :, pl.ds(start, width)]
        copies.append(pltpu.make_async_copy(source, kept_ref.at[h, slices], sems.at[h, zp]))
        copies[-1].start()
    copies.append(pltpu.make_async_copy(mine_ref, res_ref.at[:, :, residual_columns(half, 0)], res_sem))
    copies[-1].start()
    for copy in copies:
        copy.wait()


def load_step(dims, width, after, volume, mine):
    zdev, cells, total = volume.shape
    return pl.pallas_call(
        functools.partial(load_kernel, dims, total // 2, width),
        in_specs=[ANYWHERE, ANYWHERE, IN_VMEM],
        out_specs=[IN_VMEM, ANYWHERE],
        out_shape=[
            jax.ShapeDtypeStruct((1, zdev, cells, width), F32),
            jax.ShapeDtypeStruct((*mine.shape[:2], total), F32),
        ],
        scratch_shapes=[pltpu.SemaphoreType.DMA((1, zdev // dims[2])), pltpu.SemaphoreType.DMA],
        compiler_params=pltpu.CompilerParams(vmem_limit_bytes=40 * MIB),
        cost_estimate=pl.CostEstimate(flops=0, bytes_accessed=4 * zdev * cells * width, transcendentals=0),
        name="load",
    )(after, volume, mine)


def residual_kernel(dims, first, half, rdev, zdev, offset, width, *refs):
    per, groups, zb, cells = dims
    block = zdev * per
    if first:
        order_ref, table_ref, *refs = refs
    else:
        mats, inverse_ref, refs = refs[:4], refs[4], refs[5:]
    sums_refs, (mine_ref, theirs_ref), refs = refs[:3], refs[3:5], refs[5:]
    if not first:
        mine_before, sent_before, *refs = refs
    mine_out, sent_out, *refs = refs
    if not first:
        mine_out[:, :, :offset] = mine_before[...]
        sent_out[:, :, :offset] = sent_before[...]
    outs, refs = refs[:3], refs[3:]
    if first:
        foot = jnp.concatenate(
            [r[i, :, zdev // zb * width:] for r in sums_refs for i in range(2) for _ in range(zdev // zb)], axis=0
        )
        kernel = footprint_matrix(dims, zdev, rdev, foot)
        count, rows = kernel.shape
        kernel_t = kernel.T
        cover = jnp.sum(kernel_t, axis=1, keepdims=True)
        angle = low_bits(over(iota((rows, 1), 0), rdev), per)
        path = jnp.zeros((rows, 1), F32)
        for a in range(per):
            at = order_ref[lax.axis_index("ang") * per + a]
            path = jnp.where(angle == a, jnp.sum(table_ref[pl.ds(at, 1), :], axis=1, keepdims=True), path)
        inverse = 1.0 / jnp.maximum(path * cover, 0.25)
        ahead, back = split(kernel_t), split(kernel)
        for ref, value in zip(refs, (*ahead, *back)):
            ref[...] = value
        refs[4][...] = jnp.broadcast_to(inverse, (rows, LANES))
    else:
        ahead, back = (mats[0][...], mats[1][...]), (mats[2][...], mats[3][...])
        inverse = inverse_ref[:, 0:1]
    start = lax.rem(lax.axis_index("slab"), 2) * half + offset
    for at, size in tiles(width):
        columns = slice(at, at + size)
        mine = mine_ref[:, :, pl.ds(pl.multiple_of(start + at, LANES), size)].astype(F32)
        theirs = theirs_ref[:, :, offset + at:offset + at + size]
        measured = jnp.concatenate([m.reshape(per * rdev, size) for m in (mine, theirs)], axis=0)
        sums = jnp.concatenate(
            [
                r[i, :, zp * width + at:zp * width + at + size]
                for r in sums_refs for i in range(2) for zp in range(zdev // zb)
            ],
            axis=0,
        )
        residual = (measured - dot3(ahead, split(sums))) * inverse
        placed = slice(offset + at, offset + at + size)
        mine_out[:, :, placed] = residual[:per * rdev].reshape(per, rdev, size)
        sent_out[:, :, placed] = residual[per * rdev:].reshape(per, rdev, size)
        given = dot3(back, split(residual))
        for i, ref in enumerate(outs):
            for j in range(2):
                ref[j, :, columns] = given[(2 * i + j) * block:(2 * i + j + 1) * block]


def residual_step(dims, zdev, chunk, offset, width, mats, before, order, table, sums, measured, theirs):
    per, groups, zb, cells = dims
    _, rdev, total = measured.shape
    first = chunk == 0
    block = zdev * per
    count, rows = 6 * block, 2 * per * rdev
    given = jax.ShapeDtypeStruct((2, block, width), F32)
    piece = jax.ShapeDtypeStruct((per, rdev, offset + width), F32)
    shapes = [piece, piece, given, given, given]
    if first:
        args, specs = [order, table], [IN_SMEM, IN_VMEM]
        ahead, back = jax.ShapeDtypeStruct((rows, count), BF16), jax.ShapeDtypeStruct((count, rows), BF16)
        shapes += [ahead, ahead, back, back, jax.ShapeDtypeStruct((rows, LANES), F32)]
    else:
        args, specs = list(mats), [IN_VMEM] * len(mats)
    args += [*sums, measured, theirs, *before]
    specs += [IN_VMEM] * (5 + len(before))
    return pl.pallas_call(
        functools.partial(residual_kernel, dims, first, total // 2, rdev, zdev, offset, width),
        in_specs=specs,
        out_specs=[IN_VMEM] * len(shapes),
        out_shape=shapes,
        compiler_params=pltpu.CompilerParams(vmem_limit_bytes=30 * MIB),
        cost_estimate=pl.CostEstimate(
            flops=12 * count * rows * width, bytes_accessed=8 * width * (count + rows), transcendentals=0
        ),
        name=f"residual_{chunk}",
    )(*args)


def update_kernel(dims, first, parts, halves, half, offset, width, *refs):
    per, groups, zb, cells = dims
    count = groups * SUBLANES
    left_ref, backs, refs = refs[0], refs[len(halves) * groups:0:-1], refs[1 + len(halves) * groups:]
    vols, refs = refs[:parts], refs[parts:]
    zdev, depth = vols[0].shape[1], left_ref.shape[2]
    if not first:
        refs = refs[1:]
    leaving = []
    if len(refs) > 3:
        theirs_ref, _, out_ref, res_ref, buf, sems, res_sem = refs
        leaving.append(pltpu.make_async_copy(theirs_ref, res_ref.at[:, :, residual_columns(half, 1)], res_sem))
        leaving[0].start()
    else:
        out_ref, buf, sems = refs
    whole = vols[0].shape[0] == 2
    for i, zp, slices, start in volume_pieces(dims, zdev, half, offset, halves):
        rows = slice(zp * SUBLANES, (zp + 1) * SUBLANES)
        left = left_ref[zp]
        for at, size in tiles(width):
            piece = slice(at, at + size)
            back = jnp.concatenate([backs[i * groups + d][rows, piece] for d in range(groups)], axis=0)
            high, low = split(back)
            pad = jnp.zeros((depth - 3 * count, size), BF16)
            change = dot(left, jnp.concatenate([high, low, high, pad], axis=0))
            for z in range(zb):
                buf[i, zp * zb + z, :, piece] = (
                    vols[0 if whole else i][halves[i] if whole else 0, zp * zb + z, :, piece] + change[z * cells:(z + 1) * cells]
                )
        leaving.append(
            pltpu.make_async_copy(buf.at[i, slices], out_ref.at[slices, :, pl.ds(start, width)], sems.at[i, zp])
        )
        leaving[-1].start()
    for copy in leaving:
        copy.wait()


def update_step(dims, chunk, halves, offset, width, left, backs, pieces, kept, volume, out):
    per, groups, zb, cells = dims
    zdev, _, total = volume.shape
    first = out is None
    args = [left, *backs[::-1], *kept]
    shapes = [jax.ShapeDtypeStruct(volume.shape, F32)]
    scratch = [
        pltpu.VMEM((len(halves), zdev, cells, width), F32),
        pltpu.SemaphoreType.DMA((len(halves), zdev // zb)),
    ]
    specs = [IN_VMEM] * len(args)
    aliases = {}
    if not first:
        aliases = {len(args): 0}
        args += [out]
        specs += [ANYWHERE]
    if pieces:
        aliases[len(args) + 1] = 1
        args += pieces
        specs += [IN_VMEM, ANYWHERE]
        shapes += [jax.ShapeDtypeStruct(pieces[1].shape, F32)]
        scratch += [pltpu.SemaphoreType.DMA]
    size = zdev * cells * width * len(halves)
    return pl.pallas_call(
        functools.partial(update_kernel, dims, first, len(kept), halves, total // 2, offset, width),
        in_specs=specs,
        out_specs=[ANYWHERE] * len(shapes),
        out_shape=shapes,
        scratch_shapes=scratch,
        input_output_aliases=aliases,
        compiler_params=pltpu.CompilerParams(vmem_limit_bytes=20 * MIB),
        cost_estimate=pl.CostEstimate(flops=2 * size * 48, bytes_accessed=size * 4, transcendentals=0),
        name=f"update_{chunk}_{halves[0]}",
    )(*args)


def body(volume, measured, foot_start, foot_len, order, table):
    slabs, groups = lax.axis_size("slab"), lax.axis_size("ang")
    per, rdev, total = measured.shape
    zdev, cells, _ = volume.shape
    half = total // 2
    zb = SUBLANES // per
    dims = (per, groups, zb, cells)
    each = half // CHUNKS
    widths = [each] * CHUNKS
    offsets = [sum(widths[:c]) for c in range(CHUNKS)]

    def along(value, to):
        pairs = [(s, to(s)) for s in range(slabs)]
        return lax.ppermute(value, "slab", pairs)

    def spread(value, other, d):
        if not (other or d):
            return value
        pairs = [
            (s * groups + a, (s ^ other) * groups + (a + d) % groups) for s in range(slabs) for a in range(groups)
        ]
        return lax.ppermute(value, ("slab", "ang"), pairs)

    def facing(s):
        return s ^ 2

    def step(up, busy):
        def to(s):
            there = s + 4 if up(s) else s - 4
            if 0 <= there < slabs:
                return there
            return there % slabs if busy else facing(s)
        return to

    def beyond(c):
        return step(lambda s: not s & 2, c < CHUNKS - 1)

    def back_from_beyond(c):
        return step(lambda s: s & 2, c > 0)

    odd = lax.rem(lax.axis_index("slab"), 2)
    theirs = along(
        lax.dynamic_slice_in_dim(measured, (1 - odd) * half, half, 2).astype(F32), lambda s: s ^ 1
    )

    sums, kept, left = [], [[] for _ in range(CHUNKS)], None
    for c in range(CHUNKS):
        parts = []
        for halves in RAY_HALVES[c]:
            made = ray_sums(
                dims, c, halves, offsets[c], widths[c], left, (order, foot_start, foot_len), table, volume
            )
            parts += made[:len(halves) * groups]
            if left is None:
                left = made[-1]
            elif c:
                kept[c] = [made[-1]]
        parts = [spread(parts[h * groups + d], h, d) for h in range(2) for d in range(groups)]
        if c:
            parts, _ = lax.optimization_barrier((parts, sums[-1][0]))
        own = jnp.stack([sum(parts[:groups]), sum(parts[groups:])])
        near = along(own, facing)
        if c == 0:
            first_columns, update_left = prepare_step(dims, rdev, widths[0], order, table, own, near, volume)
        if c == 1:
            near, first_columns = lax.optimization_barrier((near, first_columns))
            kept[0] = [first_columns]
        far = along(near, beyond(c))
        sums.append((own, near, far))
    pieces, given, mats = [], [], None
    for c in range(CHUNKS):
        mine, sent, own, near, far, *rest = residual_step(
            dims, zdev, c, offsets[c], widths[c], mats, pieces, order, table, sums[c], measured, theirs
        )
        pieces = [mine, sent]
        mats = rest if c == 0 else mats
        returned = along(far, back_from_beyond(c))
        if c == 1:
            other_columns, res = load_step(dims, widths[0], near_before, volume, mine)
            returned, other_columns = lax.optimization_barrier((returned, other_columns))
            kept[0].append(other_columns)
        near = near + returned
        arrived = along(near, facing)
        if c == 0:
            near_before = near
        halves = [own[i] + arrived[i] for i in range(2)]
        given.append([spread(halves[h], h, d) for h in range(2) for d in range(groups)])
    pieces = [along(sent, lambda s: s ^ 1), res]
    out = None
    for c in range(CHUNKS):
        for halves in UPDATE_HALVES[c]:
            backs = [b for h in halves for b in given[c][h * groups:(h + 1) * groups]]
            write = c == CHUNKS - 1 and halves[0] == 0
            made = update_step(
                dims, c, halves, offsets[c], widths[c], update_left, backs, pieces if write else [],
                kept[c], volume, out,
            )
            out = made[0]
            res = made[1] if write else res
    return out, res


def solution(mesh):
    return jax.shard_map(
        body,
        mesh=mesh,
        in_specs=(
            P("slab", "ang", None),
            P("ang", "slab", None),
            P("slab", "ang"),
            P("slab", "ang"),
            P(),
            P(),
        ),
        out_specs=(P("slab", "ang", None), P("ang", "slab", None)),
        check_vma=False,
    )
```

```python
import functools

import jax
import jax.numpy as jnp
from jax import lax
from jax.experimental import pallas as pl
from jax.experimental.pallas import tpu as pltpu
from jax.sharding import PartitionSpec as P

F32, BF16 = jnp.float32, jnp.bfloat16
CHUNKS = 2
RAY_HALVES = [[(0, 1)], [(0, 1)]]
UPDATE_HALVES = [[(0, 1)], [(0,), (1,)]]
TILE = 512
LANES = 128
SUBLANES = 8
MIB = 1024 * 1024

IN_VMEM = pl.BlockSpec(memory_space=pltpu.VMEM)
IN_SMEM = pl.BlockSpec(memory_space=pltpu.SMEM)
ANYWHERE = pl.BlockSpec(memory_space=pl.ANY)


def split(value):
    high = value.astype(BF16)
    return high, (value - high.astype(F32)).astype(BF16)


def dot(a, b):
    return jnp.dot(a, b, preferred_element_type=F32)


def dot3(a, b):
    return dot(a[0], b[0]) + (dot(a[0], b[1]) + dot(a[1], b[0]))


def iota(shape, dim):
    return lax.broadcasted_iota(jnp.int32, shape, dim)


def low_bits(value, size):
    assert size & (size - 1) == 0
    return value & (size - 1)


def over(value, size):
    assert size & (size - 1) == 0
    return value >> (size.bit_length() - 1)


def pick(index, values):
    out = jnp.zeros(index.shape, values[0].dtype)
    for at, value in enumerate(values):
        out = jnp.where(index == at, value, out)
    return out


def tiles(width):
    step = min(TILE, width)
    return [(at, min(step, width - at)) for at in range(0, width, step)]


def slice_weights(dims, sign, order_ref, table_ref, rows_ref):
    per, groups, zb, cells = dims
    ang = lax.axis_index("ang")
    for d in range(groups):
        group = lax.rem(ang + sign * d + groups, groups)
        for z in range(zb):
            for a in range(per):
                at = (d * zb + z) * per + a
                rows_ref[at:at + 1, :] = table_ref[pl.ds(order_ref[group * per + a], 1), :]
    wide = rows_ref[...]
    total = wide.shape[1]
    row_slice = low_bits(over(iota(wide.shape, 0), per), zb)
    lane_slice = over(iota(wide.shape, 1), cells)
    out = jnp.zeros_like(wide)
    for z in range(zb):
        shift = lax.rem(z * cells - ang * cells + total, total)
        here = jnp.logical_and(row_slice == z, lane_slice == z)
        out = jnp.where(here, pltpu.roll(wide, shift, 1), out)
    return out


def volume_pieces(dims, zdev, half, offset, halves):
    odd = lax.rem(lax.axis_index("slab"), 2)
    zb = dims[2]
    for i, h in enumerate(halves):
        start = pl.multiple_of(lax.rem(odd + h, 2) * half + offset, LANES)
        for zp in range(zdev // zb):
            yield i, zp, slice(zp * zb, (zp + 1) * zb), start


def rays_kernel(dims, first, keep, extra, halves, half, offset, width, *refs):
    per, groups, zb, cells = dims
    count = groups * SUBLANES
    if first:
        order_ref, start_ref, len_ref, table_ref, vol_ref, *refs = refs
    elif extra:
        start_buf, len_buf, given_ref, vol_ref, *refs = refs
    else:
        given_ref, vol_ref, *refs = refs
    outs, refs = refs[:len(halves) * groups], refs[len(halves) * groups:]
    if first:
        left_ref, buf, sems, table_buf, order_buf, start_buf, len_buf, rows_ref, small_sems = refs
    else:
        buf, sems = refs
    zdev = vol_ref.shape[0]
    copies = []
    if first:
        small = [
            pltpu.make_async_copy(source, to, small_sems.at[i])
            for i, (source, to) in enumerate(
                [(order_ref, order_buf), (table_ref, table_buf), (start_ref, start_buf), (len_ref, len_buf)]
            )
        ]
        for copy in small:
            copy.start()
    for h, zp, slices, start in volume_pieces(dims, zdev, half, offset, halves):
        source = vol_ref.at[slices, :, pl.ds(start, width)]
        copies.append((h, zp, pltpu.make_async_copy(source, buf.at[h, slices], sems.at[h, zp])))
        copies[-1][-1].start()
    if first:
        small[0].wait()
        small[1].wait()
        both = jnp.concatenate(split(slice_weights(dims, 1, order_buf, table_buf, rows_ref)), axis=0)
        left = jnp.concatenate([both, both], axis=1)
        left_ref[...] = left
        small[2].wait()
        small[3].wait()
    else:
        left = given_ref[...]
    if extra:
        shape = (SUBLANES, LANES)
        angle, lane = low_bits(iota(shape, 0), per), iota(shape, 1)
        starts = pick(angle, [start_buf[0, a].astype(F32) for a in range(per)])
        lengths = pick(angle, [len_buf[0, a].astype(F32) for a in range(per)])
        for d in range(groups):
            foot = jnp.where(lane == 2 * d, starts, jnp.where(lane == 2 * d + 1, lengths, 0.0))
            for h in range(len(halves)):
                outs[h * groups + d][:, zdev // zb * width:] = foot
    for h, zp, copy in copies:
        copy.wait()
        for at, size in tiles(width):
            parts = [split(buf[h, zp * zb + z, :, at:at + size]) for z in range(zb)]
            product = dot(left, jnp.concatenate([p[0] for p in parts] + [p[1] for p in parts], axis=0))
            sums = product[:count] + product[count:]
            for d in range(groups):
                outs[h * groups + d][:, zp * width + at:zp * width + at + size] = (
                    sums[d * SUBLANES:(d + 1) * SUBLANES]
                )


def ray_sums(dims, chunk, halves, offset, width, given, small, table, volume):
    per, groups, zb, cells = dims
    zdev, _, total = volume.shape
    first, keep, extra = given is None, chunk > 0, chunk == 0
    count, all_cells = groups * SUBLANES, table.shape[1]
    out = jax.ShapeDtypeStruct((SUBLANES, zdev // zb * width + (LANES if extra else 0)), F32)
    left = jax.ShapeDtypeStruct((2 * count, 2 * zb * cells), BF16)
    columns = (len(halves), zdev, cells, width)
    assert zb * cells == all_cells
    shapes = [out] * (len(halves) * groups)
    scratch = [] if keep else [pltpu.VMEM(columns, F32)]
    scratch += [pltpu.SemaphoreType.DMA((len(halves), zdev // zb))]
    args, specs, limit = [given, volume], [IN_VMEM, ANYWHERE], 40
    if first:
        scratch += [pltpu.VMEM(table.shape, F32)] + [pltpu.SMEM(a.shape, a.dtype) for a in small]
        scratch += [pltpu.VMEM((count, all_cells), F32), pltpu.SemaphoreType.DMA((4,))]
        args, specs, limit = [*small, table, volume], [ANYWHERE] * 5, 58
        shapes += [left]
    elif extra:
        args, specs, limit = [*small[1:], *args], [IN_SMEM] * 2 + specs, 50
    if keep:
        shapes += [jax.ShapeDtypeStruct(columns, F32)]
    size = zdev * cells * width * len(halves)
    return pl.pallas_call(
        functools.partial(rays_kernel, dims, first, keep, extra, halves, total // 2, offset, width),
        in_specs=specs,
        out_specs=[IN_VMEM] * len(shapes),
        out_shape=shapes,
        scratch_shapes=scratch,
        compiler_params=pltpu.CompilerParams(vmem_limit_bytes=limit * MIB),
        cost_estimate=pl.CostEstimate(flops=2 * size * 16, bytes_accessed=size * 4, transcendentals=0),
        name=f"ray_sums_{chunk}_{halves[0]}",
    )(*args)


def hat_weights(dims, zdev, start, length, row):
    per, groups, zb, cells = dims
    at = low_bits(iota(start.shape, 0), zdev * per)
    slice_at = over(at, zb * per) * zb + low_bits(over(at, per), zb)
    span = jnp.where(length > 0.0, length, 1.0) / zdev
    centre = start + (slice_at.astype(F32) + 0.5) * span
    hat = jnp.maximum(0.0, 1.0 - jnp.abs(row + 0.5 - centre) / span)
    return jnp.where(jnp.logical_and(row >= start, row < start + length), hat, 0.0)


def footprint_matrix(dims, zdev, rdev, foot):
    per = dims[0]
    rows = 2 * per * rdev
    slab = lax.axis_index("slab")
    sibling = slab + 1 - 2 * lax.rem(slab, 2)
    row_id = iota((1, rows), 1)
    row_slab = jnp.where(row_id < per * rdev, slab, sibling)
    row = (row_slab * rdev + low_bits(row_id, rdev)).astype(F32)
    shape = (foot.shape[0], rows)
    same_angle = low_bits(iota(shape, 0), per) == low_bits(over(iota(shape, 1), rdev), per)
    beyond = slab + jnp.where(low_bits(slab, 4) < 2, -2, 2)
    there = jnp.logical_and(beyond >= 0, beyond < lax.axis_size("slab"))
    known = jnp.where(there, foot.shape[0], foot.shape[0] // 3 * 2)
    meets = jnp.logical_and(same_angle, iota(shape, 0) < known)
    return jnp.where(meets, hat_weights(dims, zdev, foot[:, 0:1], foot[:, 1:2], row), 0.0)


def update_weights(dims, zdev, rdev, foot, order_ref, table_ref, rows_ref, out_ref):
    per, groups, zb, cells = dims
    count = groups * SUBLANES
    weights = slice_weights(dims, -1, order_ref, table_ref, rows_ref)
    window = -(-5 * rdev // LANES) * LANES
    row = ((lax.axis_index("slab") - 2) * rdev + iota((1, window), 1)).astype(F32)
    sums = [
        jnp.sum(hat_weights(dims, zdev, foot[:, 2 * d:2 * d + 1], foot[:, 2 * d + 1:2 * d + 2], row), axis=1, keepdims=True)
        for d in range(groups)
    ]
    pad = jnp.zeros((out_ref.shape[2] - 3 * count, weights.shape[1]), F32)
    for zp in range(zdev // zb):
        slices = jnp.concatenate([s[zp * SUBLANES:(zp + 1) * SUBLANES] for s in sums], axis=0)
        scaled = weights / jnp.sum(weights * slices, axis=0, keepdims=True)
        high = scaled.astype(BF16).astype(F32)
        stacked = jnp.concatenate([high, high, scaled - high, pad], axis=0)
        out_ref[zp] = stacked.T.astype(BF16)


def prepare_kernel(dims, rdev, half, width, order_ref, table_ref, foot_ref, _, vol_ref, kept_ref, left_ref, sems, rows_ref):
    zdev = vol_ref.shape[0]
    copies = []
    for h, zp, slices, start in volume_pieces(dims, zdev, half, 0, (0,)):
        source = vol_ref.at[slices, :, pl.ds(start, width)]
        copies.append(pltpu.make_async_copy(source, kept_ref.at[h, slices], sems.at[h, zp]))
        copies[-1].start()
    batches = zdev // dims[2]
    foot = jnp.concatenate([foot_ref[0, :, batches * width:]] * batches, axis=0)
    update_weights(dims, zdev, rdev, foot, order_ref, table_ref, rows_ref, left_ref)
    for copy in copies:
        copy.wait()


def prepare_step(dims, rdev, width, order, table, own, after, volume):
    per, groups, zb, cells = dims
    zdev, _, total = volume.shape
    depth = -(-3 * groups * SUBLANES // LANES) * LANES
    return pl.pallas_call(
        functools.partial(prepare_kernel, dims, rdev, total // 2, width),
        in_specs=[IN_SMEM, IN_VMEM, IN_VMEM, ANYWHERE, ANYWHERE],
        out_specs=[IN_VMEM, IN_VMEM],
        out_shape=[
            jax.ShapeDtypeStruct((1, zdev, cells, width), F32),
            jax.ShapeDtypeStruct((zdev // zb, zb * cells, depth), BF16),
        ],
        scratch_shapes=[
            pltpu.SemaphoreType.DMA((1, zdev // zb)),
            pltpu.VMEM((groups * SUBLANES, table.shape[1]), F32),
        ],
        compiler_params=pltpu.CompilerParams(vmem_limit_bytes=36 * MIB),
        cost_estimate=pl.CostEstimate(flops=0, bytes_accessed=8 * zdev * cells * width, transcendentals=0),
        name="prepare",
    )(order, table, own, after, volume)


def residual_columns(half, which):
    odd = lax.rem(lax.axis_index("slab"), 2)
    return pl.ds(pl.multiple_of(lax.rem(odd + which, 2) * half, LANES), half)


def load_kernel(dims, half, width, _, vol_ref, mine_ref, kept_ref, res_ref, sems, res_sem):
    copies = []
    for h, zp, slices, start in volume_pieces(dims, vol_ref.shape[0], half, 0, (1,)):
        source = vol_ref.at[slices, :, pl.ds(start, width)]
        copies.append(pltpu.make_async_copy(source, kept_ref.at[h, slices], sems.at[h, zp]))
        copies[-1].start()
    copies.append(pltpu.make_async_copy(mine_ref, res_ref.at[:, :, residual_columns(half, 0)], res_sem))
    copies[-1].start()
    for copy in copies:
        copy.wait()


def load_step(dims, width, after, volume, mine):
    zdev, cells, total = volume.shape
    return pl.pallas_call(
        functools.partial(load_kernel, dims, total // 2, width),
        in_specs=[ANYWHERE, ANYWHERE, IN_VMEM],
        out_specs=[IN_VMEM, ANYWHERE],
        out_shape=[
            jax.ShapeDtypeStruct((1, zdev, cells, width), F32),
            jax.ShapeDtypeStruct((*mine.shape[:2], total), F32),
        ],
        scratch_shapes=[pltpu.SemaphoreType.DMA((1, zdev // dims[2])), pltpu.SemaphoreType.DMA],
        compiler_params=pltpu.CompilerParams(vmem_limit_bytes=33 * MIB),
        cost_estimate=pl.CostEstimate(flops=0, bytes_accessed=4 * zdev * cells * width, transcendentals=0),
        name="load",
    )(after, volume, mine)


def residual_kernel(dims, first, half, rdev, zdev, offset, width, *refs):
    per, groups, zb, cells = dims
    block = zdev * per
    if first:
        order_ref, table_ref, *refs = refs
    else:
        mats, inverse_ref, refs = refs[:4], refs[4], refs[5:]
    sums_refs, (mine_ref, theirs_ref), refs = refs[:3], refs[3:5], refs[5:]
    if not first:
        mine_before, sent_before, *refs = refs
    mine_out, sent_out, *refs = refs
    if not first:
        mine_out[:, :, :offset] = mine_before[...]
        sent_out[:, :, :offset] = sent_before[...]
    outs, refs = refs[:3], refs[3:]
    if first:
        foot = jnp.concatenate(
            [r[i, :, zdev // zb * width:] for r in sums_refs for i in range(2) for _ in range(zdev // zb)], axis=0
        )
        kernel = footprint_matrix(dims, zdev, rdev, foot)
        count, rows = kernel.shape
        kernel_t = kernel.T
        cover = jnp.sum(kernel_t, axis=1, keepdims=True)
        angle = low_bits(over(iota((rows, 1), 0), rdev), per)
        path = jnp.zeros((rows, 1), F32)
        for a in range(per):
            at = order_ref[lax.axis_index("ang") * per + a]
            path = jnp.where(angle == a, jnp.sum(table_ref[pl.ds(at, 1), :], axis=1, keepdims=True), path)
        inverse = 1.0 / jnp.maximum(path * cover, 0.25)
        ahead, back = split(kernel_t), split(kernel)
        for ref, value in zip(refs, (*ahead, *back)):
            ref[...] = value
        refs[4][...] = jnp.broadcast_to(inverse, (rows, LANES))
    else:
        ahead, back = (mats[0][...], mats[1][...]), (mats[2][...], mats[3][...])
        inverse = inverse_ref[:, 0:1]
    start = lax.rem(lax.axis_index("slab"), 2) * half + offset
    for at, size in tiles(width):
        columns = slice(at, at + size)
        mine = mine_ref[:, :, pl.ds(pl.multiple_of(start + at, LANES), size)].astype(F32)
        theirs = theirs_ref[:, :, offset + at:offset + at + size]
        measured = jnp.concatenate([m.reshape(per * rdev, size) for m in (mine, theirs)], axis=0)
        sums = jnp.concatenate(
            [
                r[i, :, zp * width + at:zp * width + at + size]
                for r in sums_refs for i in range(2) for zp in range(zdev // zb)
            ],
            axis=0,
        )
        residual = (measured - dot3(ahead, split(sums))) * inverse
        placed = slice(offset + at, offset + at + size)
        mine_out[:, :, placed] = residual[:per * rdev].reshape(per, rdev, size)
        sent_out[:, :, placed] = residual[per * rdev:].reshape(per, rdev, size)
        given = dot3(back, split(residual))
        for i, ref in enumerate(outs):
            for j in range(2):
                ref[j, :, columns] = given[(2 * i + j) * block:(2 * i + j + 1) * block]


def residual_step(dims, zdev, chunk, offset, width, mats, before, order, table, sums, measured, theirs):
    per, groups, zb, cells = dims
    _, rdev, total = measured.shape
    first = chunk == 0
    block = zdev * per
    count, rows = 6 * block, 2 * per * rdev
    given = jax.ShapeDtypeStruct((2, block, width), F32)
    piece = jax.ShapeDtypeStruct((per, rdev, offset + width), F32)
    shapes = [piece, piece, given, given, given]
    if first:
        args, specs = [order, table], [IN_SMEM, IN_VMEM]
        ahead, back = jax.ShapeDtypeStruct((rows, count), BF16), jax.ShapeDtypeStruct((count, rows), BF16)
        shapes += [ahead, ahead, back, back, jax.ShapeDtypeStruct((rows, LANES), F32)]
    else:
        args, specs = list(mats), [IN_VMEM] * len(mats)
    args += [*sums, measured, theirs, *before]
    specs += [IN_VMEM] * (5 + len(before))
    return pl.pallas_call(
        functools.partial(residual_kernel, dims, first, total // 2, rdev, zdev, offset, width),
        in_specs=specs,
        out_specs=[IN_VMEM] * len(shapes),
        out_shape=shapes,
        compiler_params=pltpu.CompilerParams(vmem_limit_bytes=30 * MIB),
        cost_estimate=pl.CostEstimate(
            flops=12 * count * rows * width, bytes_accessed=8 * width * (count + rows), transcendentals=0
        ),
        name=f"residual_{chunk}",
    )(*args)


def update_kernel(dims, first, parts, halves, half, offset, width, *refs):
    per, groups, zb, cells = dims
    count = groups * SUBLANES
    left_ref, backs, refs = refs[0], refs[len(halves) * groups:0:-1], refs[1 + len(halves) * groups:]
    vols, refs = refs[:parts], refs[parts:]
    zdev, depth = vols[0].shape[1], left_ref.shape[2]
    if not first:
        refs = refs[1:]
    leaving = []
    if len(refs) > 3:
        theirs_ref, _, out_ref, res_ref, buf, sems, res_sem = refs
        leaving.append(pltpu.make_async_copy(theirs_ref, res_ref.at[:, :, residual_columns(half, 1)], res_sem))
        leaving[0].start()
    else:
        out_ref, buf, sems = refs
    whole = vols[0].shape[0] == 2
    for i, zp, slices, start in volume_pieces(dims, zdev, half, offset, halves):
        rows = slice(zp * SUBLANES, (zp + 1) * SUBLANES)
        left = left_ref[zp]
        for at, size in tiles(width):
            piece = slice(at, at + size)
            back = jnp.concatenate([backs[i * groups + d][rows, piece] for d in range(groups)], axis=0)
            high, low = split(back)
            pad = jnp.zeros((depth - 3 * count, size), BF16)
            change = dot(left, jnp.concatenate([high, low, high, pad], axis=0))
            for z in range(zb):
                buf[i, zp * zb + z, :, piece] = (
                    vols[0 if whole else i][halves[i] if whole else 0, zp * zb + z, :, piece] + change[z * cells:(z + 1) * cells]
                )
        leaving.append(
            pltpu.make_async_copy(buf.at[i, slices], out_ref.at[slices, :, pl.ds(start, width)], sems.at[i, zp])
        )
        leaving[-1].start()
    for copy in leaving:
        copy.wait()


def update_step(dims, chunk, halves, offset, width, left, backs, pieces, kept, volume, out):
    per, groups, zb, cells = dims
    zdev, _, total = volume.shape
    first = out is None
    args = [left, *backs[::-1], *kept]
    shapes = [jax.ShapeDtypeStruct(volume.shape, F32)]
    scratch = [
        pltpu.VMEM((len(halves), zdev, cells, width), F32),
        pltpu.SemaphoreType.DMA((len(halves), zdev // zb)),
    ]
    specs = [IN_VMEM] * len(args)
    aliases = {}
    if not first:
        aliases = {len(args): 0}
        args += [out]
        specs += [ANYWHERE]
    if pieces:
        aliases[len(args) + 1] = 1
        args += pieces
        specs += [IN_VMEM, ANYWHERE]
        shapes += [jax.ShapeDtypeStruct(pieces[1].shape, F32)]
        scratch += [pltpu.SemaphoreType.DMA]
    size = zdev * cells * width * len(halves)
    return pl.pallas_call(
        functools.partial(update_kernel, dims, first, len(kept), halves, total // 2, offset, width),
        in_specs=specs,
        out_specs=[ANYWHERE] * len(shapes),
        out_shape=shapes,
        scratch_shapes=scratch,
        input_output_aliases=aliases,
        compiler_params=pltpu.CompilerParams(vmem_limit_bytes=20 * MIB),
        cost_estimate=pl.CostEstimate(flops=2 * size * 48, bytes_accessed=size * 4, transcendentals=0),
        name=f"update_{chunk}_{halves[0]}",
    )(*args)


def body(volume, measured, foot_start, foot_len, order, table):
    slabs, groups = lax.axis_size("slab"), lax.axis_size("ang")
    per, rdev, total = measured.shape
    zdev, cells, _ = volume.shape
    half = total // 2
    zb = SUBLANES // per
    dims = (per, groups, zb, cells)
    each = half // CHUNKS
    widths = [each] * CHUNKS
    offsets = [sum(widths[:c]) for c in range(CHUNKS)]

    def along(value, to):
        pairs = [(s, to(s)) for s in range(slabs) if to(s) is not None]
        return lax.ppermute(value, "slab", pairs)

    def spread(value, other, d):
        if not (other or d):
            return value
        pairs = [
            (s * groups + a, (s ^ other) * groups + (a + d) % groups) for s in range(slabs) for a in range(groups)
        ]
        return lax.ppermute(value, ("slab", "ang"), pairs)

    def facing(s):
        return s ^ 2

    def step(up, busy):
        def to(s):
            there = s + 4 if up(s) else s - 4
            if 0 <= there < slabs:
                return there
            return None if busy else facing(s)
        return to

    def beyond(c):
        return step(lambda s: not s & 2, c < CHUNKS - 1)

    def back_from_beyond(c):
        return step(lambda s: s & 2, c > 0)

    odd = lax.rem(lax.axis_index("slab"), 2)
    theirs = along(
        lax.dynamic_slice_in_dim(measured, (1 - odd) * half, half, 2).astype(F32), lambda s: s ^ 1
    )

    sums, kept, left = [], [[] for _ in range(CHUNKS)], None
    for c in range(CHUNKS):
        parts = []
        for halves in RAY_HALVES[c]:
            made = ray_sums(
                dims, c, halves, offsets[c], widths[c], left, (order, foot_start, foot_len), table, volume
            )
            parts += made[:len(halves) * groups]
            if left is None:
                left = made[-1]
            elif c:
                kept[c] = [made[-1]]
        parts = [spread(parts[h * groups + d], h, d) for h in range(2) for d in range(groups)]
        if c:
            parts, _ = lax.optimization_barrier((parts, sums[-1][0]))
        own = jnp.stack([sum(parts[:groups]), sum(parts[groups:])])
        near = along(own, facing)
        if c == 0:
            first_columns, update_left = prepare_step(dims, rdev, widths[0], order, table, own, near, volume)
        if c == 1:
            near, first_columns = lax.optimization_barrier((near, first_columns))
            kept[0] = [first_columns]
        far = along(near, beyond(c))
        sums.append((own, near, far))
    pieces, given, mats = [], [], None
    for c in range(CHUNKS):
        mine, sent, own, near, far, *rest = residual_step(
            dims, zdev, c, offsets[c], widths[c], mats, pieces, order, table, sums[c], measured, theirs
        )
        pieces = [mine, sent]
        mats = rest if c == 0 else mats
        returned = along(far, back_from_beyond(c))
        if c == 1:
            other_columns, res = load_step(dims, widths[0], near_before, volume, mine)
            returned, other_columns = lax.optimization_barrier((returned, other_columns))
            kept[0].append(other_columns)
        near = near + returned
        arrived = along(near, facing)
        if c == 0:
            near_before = near
        halves = [own[i] + arrived[i] for i in range(2)]
        given.append([spread(halves[h], h, d) for h in range(2) for d in range(groups)])
    pieces = [along(sent, lambda s: s ^ 1), res]
    out = None
    for c in range(CHUNKS):
        for halves in UPDATE_HALVES[c]:
            backs = [b for h in halves for b in given[c][h * groups:(h + 1) * groups]]
            write = c == CHUNKS - 1 and halves[0] == 0
            made = update_step(
                dims, c, halves, offsets[c], widths[c], update_left, backs, pieces if write else [],
                kept[c], volume, out,
            )
            out = made[0]
            res = made[1] if write else res
    return out, res


def solution(mesh):
    return jax.shard_map(
        body,
        mesh=mesh,
        in_specs=(
            P("slab", "ang", None),
            P("ang", "slab", None),
            P("slab", "ang"),
            P("slab", "ang"),
            P(),
            P(),
        ),
        out_specs=(P("slab", "ang", None), P("ang", "slab", None)),
        check_vma=False,
    )
```

```python
import functools

import jax
import jax.numpy as jnp
from jax import lax
from jax.experimental import pallas as pl
from jax.experimental.pallas import tpu as pltpu
from jax.sharding import PartitionSpec as P

F32, BF16 = jnp.float32, jnp.bfloat16
CHUNKS = 2
RAY_HALVES = [[(0, 1)], [(0, 1)]]
UPDATE_HALVES = [[(0, 1)], [(0,), (1,)]]
TILE = 512
LANES = 128
SUBLANES = 8
MIB = 1024 * 1024

IN_VMEM = pl.BlockSpec(memory_space=pltpu.VMEM)
IN_SMEM = pl.BlockSpec(memory_space=pltpu.SMEM)
ANYWHERE = pl.BlockSpec(memory_space=pl.ANY)


def split(value):
    high = value.astype(BF16)
    return high, (value - high.astype(F32)).astype(BF16)


def dot(a, b):
    return jnp.dot(a, b, preferred_element_type=F32)


def dot3(a, b):
    return dot(a[0], b[0]) + (dot(a[0], b[1]) + dot(a[1], b[0]))


def iota(shape, dim):
    return lax.broadcasted_iota(jnp.int32, shape, dim)


def low_bits(value, size):
    assert size & (size - 1) == 0
    return value & (size - 1)


def over(value, size):
    assert size & (size - 1) == 0
    return value >> (size.bit_length() - 1)


def pick(index, values):
    out = jnp.zeros(index.shape, values[0].dtype)
    for at, value in enumerate(values):
        out = jnp.where(index == at, value, out)
    return out


def tiles(width):
    step = min(TILE, width)
    return [(at, min(step, width - at)) for at in range(0, width, step)]


def slice_weights(dims, sign, order_ref, table_ref, rows_ref):
    per, groups, zb, cells = dims
    ang = lax.axis_index("ang")
    for d in range(groups):
        group = lax.rem(ang + sign * d + groups, groups)
        for z in range(zb):
            for a in range(per):
                at = (d * zb + z) * per + a
                rows_ref[at:at + 1, :] = table_ref[pl.ds(order_ref[group * per + a], 1), :]
    wide = rows_ref[...]
    total = wide.shape[1]
    row_slice = low_bits(over(iota(wide.shape, 0), per), zb)
    lane_slice = over(iota(wide.shape, 1), cells)
    out = jnp.zeros_like(wide)
    for z in range(zb):
        shift = lax.rem(z * cells - ang * cells + total, total)
        here = jnp.logical_and(row_slice == z, lane_slice == z)
        out = jnp.where(here, pltpu.roll(wide, shift, 1), out)
    return out


def volume_pieces(dims, zdev, half, offset, halves):
    odd = lax.rem(lax.axis_index("slab"), 2)
    zb = dims[2]
    for i, h in enumerate(halves):
        start = pl.multiple_of(lax.rem(odd + h, 2) * half + offset, LANES)
        for zp in range(zdev // zb):
            yield i, zp, slice(zp * zb, (zp + 1) * zb), start


def rays_kernel(dims, first, keep, extra, halves, half, offset, width, *refs):
    per, groups, zb, cells = dims
    count = groups * SUBLANES
    if first:
        order_ref, start_ref, len_ref, table_ref, vol_ref, *refs = refs
    elif extra:
        start_buf, len_buf, given_ref, vol_ref, *refs = refs
    else:
        given_ref, vol_ref, *refs = refs
    outs, refs = refs[:len(halves) * groups], refs[len(halves) * groups:]
    if first:
        left_ref, buf, sems, table_buf, order_buf, start_buf, len_buf, rows_ref, small_sems = refs
    else:
        buf, sems = refs
    zdev = vol_ref.shape[0]
    copies = []
    if first:
        small = [
            pltpu.make_async_copy(source, to, small_sems.at[i])
            for i, (source, to) in enumerate(
                [(order_ref, order_buf), (table_ref, table_buf), (start_ref, start_buf), (len_ref, len_buf)]
            )
        ]
        for copy in small:
            copy.start()
    for h, zp, slices, start in volume_pieces(dims, zdev, half, offset, halves):
        source = vol_ref.at[slices, :, pl.ds(start, width)]
        copies.append((h, zp, pltpu.make_async_copy(source, buf.at[h, slices], sems.at[h, zp])))
        copies[-1][-1].start()
    if first:
        small[0].wait()
        small[1].wait()
        both = jnp.concatenate(split(slice_weights(dims, 1, order_buf, table_buf, rows_ref)), axis=0)
        left = jnp.concatenate([both, both], axis=1)
        left_ref[...] = left
        small[2].wait()
        small[3].wait()
    else:
        left = given_ref[...]
    if extra:
        shape = (SUBLANES, LANES)
        angle, lane = low_bits(iota(shape, 0), per), iota(shape, 1)
        starts = pick(angle, [start_buf[0, a].astype(F32) for a in range(per)])
        lengths = pick(angle, [len_buf[0, a].astype(F32) for a in range(per)])
        for d in range(groups):
            foot = jnp.where(lane == 2 * d, starts, jnp.where(lane == 2 * d + 1, lengths, 0.0))
            for h in range(len(halves)):
                outs[h * groups + d][:, zdev // zb * width:] = foot
    for h, zp, copy in copies:
        copy.wait()
        for at, size in tiles(width):
            parts = [split(buf[h, zp * zb + z, :, at:at + size]) for z in range(zb)]
            product = dot(left, jnp.concatenate([p[0] for p in parts] + [p[1] for p in parts], axis=0))
            sums = product[:count] + product[count:]
            for d in range(groups):
                outs[h * groups + d][:, zp * width + at:zp * width + at + size] = (
                    sums[d * SUBLANES:(d + 1) * SUBLANES]
                )


def ray_sums(dims, chunk, halves, offset, width, given, small, table, volume):
    per, groups, zb, cells = dims
    zdev, _, total = volume.shape
    first, keep, extra = given is None, chunk > 0, chunk == 0
    count, all_cells = groups * SUBLANES, table.shape[1]
    out = jax.ShapeDtypeStruct((SUBLANES, zdev // zb * width + (LANES if extra else 0)), F32)
    left = jax.ShapeDtypeStruct((2 * count, 2 * zb * cells), BF16)
    columns = (len(halves), zdev, cells, width)
    assert zb * cells == all_cells
    shapes = [out] * (len(halves) * groups)
    scratch = [] if keep else [pltpu.VMEM(columns, F32)]
    scratch += [pltpu.SemaphoreType.DMA((len(halves), zdev // zb))]
    args, specs, limit = [given, volume], [IN_VMEM, ANYWHERE], 40
    if first:
        scratch += [pltpu.VMEM(table.shape, F32)] + [pltpu.SMEM(a.shape, a.dtype) for a in small]
        scratch += [pltpu.VMEM((count, all_cells), F32), pltpu.SemaphoreType.DMA((4,))]
        args, specs, limit = [*small, table, volume], [ANYWHERE] * 5, 58
        shapes += [left]
    elif extra:
        args, specs, limit = [*small[1:], *args], [IN_SMEM] * 2 + specs, 50
    if keep:
        shapes += [jax.ShapeDtypeStruct(columns, F32)]
    size = zdev * cells * width * len(halves)
    return pl.pallas_call(
        functools.partial(rays_kernel, dims, first, keep, extra, halves, total // 2, offset, width),
        in_specs=specs,
        out_specs=[IN_VMEM] * len(shapes),
        out_shape=shapes,
        scratch_shapes=scratch,
        compiler_params=pltpu.CompilerParams(vmem_limit_bytes=limit * MIB),
        cost_estimate=pl.CostEstimate(flops=2 * size * 16, bytes_accessed=size * 4, transcendentals=0),
        name=f"ray_sums_{chunk}_{halves[0]}",
    )(*args)


def hat_weights(dims, zdev, start, length, row):
    per, groups, zb, cells = dims
    at = low_bits(iota(start.shape, 0), zdev * per)
    slice_at = over(at, zb * per) * zb + low_bits(over(at, per), zb)
    span = jnp.where(length > 0.0, length, 1.0) / zdev
    centre = start + (slice_at.astype(F32) + 0.5) * span
    hat = jnp.maximum(0.0, 1.0 - jnp.abs(row + 0.5 - centre) / span)
    return jnp.where(jnp.logical_and(row >= start, row < start + length), hat, 0.0)


def footprint_matrix(dims, zdev, rdev, foot):
    per = dims[0]
    rows = 2 * per * rdev
    slab = lax.axis_index("slab")
    sibling = slab + 1 - 2 * lax.rem(slab, 2)
    row_id = iota((1, rows), 1)
    row_slab = jnp.where(row_id < per * rdev, slab, sibling)
    row = (row_slab * rdev + low_bits(row_id, rdev)).astype(F32)
    shape = (foot.shape[0], rows)
    same_angle = low_bits(iota(shape, 0), per) == low_bits(over(iota(shape, 1), rdev), per)
    return jnp.where(same_angle, hat_weights(dims, zdev, foot[:, 0:1], foot[:, 1:2], row), 0.0)


def footprints(ref, batches, width):
    return jnp.concatenate([ref[i, :, batches * width:] for i in range(2) for _ in range(batches)], axis=0)


def update_weights(dims, zdev, rdev, foot, order_ref, table_ref, rows_ref, out_ref):
    per, groups, zb, cells = dims
    count = groups * SUBLANES
    weights = slice_weights(dims, -1, order_ref, table_ref, rows_ref)
    window = -(-5 * rdev // LANES) * LANES
    row = ((lax.axis_index("slab") - 2) * rdev + iota((1, window), 1)).astype(F32)
    sums = [
        jnp.sum(hat_weights(dims, zdev, foot[:, 2 * d:2 * d + 1], foot[:, 2 * d + 1:2 * d + 2], row), axis=1, keepdims=True)
        for d in range(groups)
    ]
    pad = jnp.zeros((out_ref.shape[2] - 3 * count, weights.shape[1]), F32)
    for zp in range(zdev // zb):
        slices = jnp.concatenate([s[zp * SUBLANES:(zp + 1) * SUBLANES] for s in sums], axis=0)
        scaled = weights / jnp.sum(weights * slices, axis=0, keepdims=True)
        high = scaled.astype(BF16).astype(F32)
        stacked = jnp.concatenate([high, high, scaled - high, pad], axis=0)
        out_ref[zp] = stacked.T.astype(BF16)


def prepare_kernel(
    dims, rdev, half, width, order_ref, table_ref, own_ref, near_ref, vol_ref,
    kept_ref, left_ref, ahead_high, ahead_low, back_high, back_low, cover_ref, sems, rows_ref,
):
    zdev = vol_ref.shape[0]
    copies = []
    for h, zp, slices, start in volume_pieces(dims, zdev, half, 0, (0, 1)):
        source = vol_ref.at[slices, :, pl.ds(start, width)]
        copies.append(pltpu.make_async_copy(source, kept_ref.at[h, slices], sems.at[h, zp]))
        copies[-1].start()
    batches = zdev // dims[2]
    own = footprints(own_ref, batches, width)
    kernel = footprint_matrix(dims, zdev, rdev, jnp.concatenate([own, footprints(near_ref, batches, width)], axis=0))
    back_high[...], back_low[...] = split(kernel)
    kernel_t = kernel.T
    ahead_high[...], ahead_low[...] = split(kernel_t)
    cover_ref[...] = jnp.broadcast_to(jnp.sum(kernel_t, axis=1, keepdims=True), cover_ref.shape)
    update_weights(dims, zdev, rdev, own[:own.shape[0] // 2], order_ref, table_ref, rows_ref, left_ref)
    for copy in copies:
        copy.wait()


def prepare_step(dims, rdev, width, order, table, own, after, volume):
    per, groups, zb, cells = dims
    zdev, _, total = volume.shape
    depth = -(-3 * groups * SUBLANES // LANES) * LANES
    count, rows = 4 * zdev * per, 2 * per * rdev
    return pl.pallas_call(
        functools.partial(prepare_kernel, dims, rdev, total // 2, width),
        in_specs=[IN_SMEM, IN_VMEM, IN_VMEM, IN_VMEM, ANYWHERE],
        out_specs=[IN_VMEM] * 7,
        out_shape=[
            jax.ShapeDtypeStruct((2, zdev, cells, width), F32),
            jax.ShapeDtypeStruct((zdev // zb, zb * cells, depth), BF16),
            jax.ShapeDtypeStruct((rows, count), BF16),
            jax.ShapeDtypeStruct((rows, count), BF16),
            jax.ShapeDtypeStruct((count, rows), BF16),
            jax.ShapeDtypeStruct((count, rows), BF16),
            jax.ShapeDtypeStruct((rows, LANES), F32),
        ],
        scratch_shapes=[
            pltpu.SemaphoreType.DMA((2, zdev // zb)),
            pltpu.VMEM((groups * SUBLANES, table.shape[1]), F32),
        ],
        compiler_params=pltpu.CompilerParams(vmem_limit_bytes=40 * MIB),
        cost_estimate=pl.CostEstimate(flops=0, bytes_accessed=8 * zdev * cells * width, transcendentals=0),
        name="prepare",
    )(order, table, own, after, volume)


def residual_kernel(dims, first, half, rdev, zdev, offset, width, *refs):
    per, groups, zb, cells = dims
    block = zdev * per
    if first:
        order_ref, table_ref, *refs = refs
        known, known_cover, refs = refs[:4], refs[4], refs[5:]
    else:
        mats, inverse_ref, refs = refs[:4], refs[4], refs[5:]
    sums_refs, (mine_ref, theirs_ref), refs = refs[:3], refs[3:5], refs[5:]
    if not first:
        mine_before, sent_before, *refs = refs
    mine_out, sent_out, *refs = refs
    if not first:
        mine_out[:, :, :offset] = mine_before[...]
        sent_out[:, :, :offset] = sent_before[...]
    outs = refs[:1 if first else 3]
    refs = refs[len(outs):]
    if first:
        slab = lax.axis_index("slab")
        beyond = slab + jnp.where(low_bits(slab, 4) < 2, -2, 2)
        there = jnp.logical_and(beyond >= 0, beyond < lax.axis_size("slab"))
        kernel = footprint_matrix(dims, zdev, rdev, footprints(sums_refs[2], zdev // zb, width))
        kernel = jnp.where(there, kernel, 0.0)
        rows = kernel.shape[1]
        kernel_t = kernel.T
        cover = known_cover[:, 0:1] + jnp.sum(kernel_t, axis=1, keepdims=True)
        angle = low_bits(over(iota((rows, 1), 0), rdev), per)
        path = jnp.zeros((rows, 1), F32)
        for a in range(per):
            at = order_ref[lax.axis_index("ang") * per + a]
            path = jnp.where(angle == a, jnp.sum(table_ref[pl.ds(at, 1), :], axis=1, keepdims=True), path)
        inverse = 1.0 / jnp.maximum(path * cover, 0.25)
        ahead = [jnp.concatenate([k[...], far], axis=1) for k, far in zip(known[:2], split(kernel_t))]
        back = [jnp.concatenate([k[...], far], axis=0) for k, far in zip(known[2:], split(kernel))]
        for ref, value in zip(refs, (*ahead, *back)):
            ref[...] = value
        back = split(kernel)
        refs[4][...] = jnp.broadcast_to(inverse, (rows, LANES))
    else:
        ahead, back = (mats[0][...], mats[1][...]), (mats[2][...], mats[3][...])
        inverse = inverse_ref[:, 0:1]
    start = lax.rem(lax.axis_index("slab"), 2) * half + offset
    for at, size in tiles(width):
        columns = slice(at, at + size)
        mine = mine_ref[:, :, pl.ds(pl.multiple_of(start + at, LANES), size)].astype(F32)
        theirs = theirs_ref[:, :, offset + at:offset + at + size]
        measured = jnp.concatenate([m.reshape(per * rdev, size) for m in (mine, theirs)], axis=0)
        sums = jnp.concatenate(
            [
                r[i, :, zp * width + at:zp * width + at + size]
                for r in sums_refs for i in range(2) for zp in range(zdev // zb)
            ],
            axis=0,
        )
        residual = (measured - dot3(ahead, split(sums))) * inverse
        placed = slice(offset + at, offset + at + size)
        mine_out[:, :, placed] = residual[:per * rdev].reshape(per, rdev, size)
        sent_out[:, :, placed] = residual[per * rdev:].reshape(per, rdev, size)
        given = dot3(back, split(residual))
        for i, ref in enumerate(outs):
            for j in range(2):
                ref[j, :, columns] = given[(2 * i + j) * block:(2 * i + j + 1) * block]


def residual_step(dims, zdev, chunk, offset, width, mats, before, order, table, sums, measured, theirs):
    per, groups, zb, cells = dims
    _, rdev, total = measured.shape
    first = chunk == 0
    block = zdev * per
    count, rows = 6 * block, 2 * per * rdev
    given = jax.ShapeDtypeStruct((2, block, width), F32)
    piece = jax.ShapeDtypeStruct((per, rdev, offset + width), F32)
    shapes = [piece, piece] + [given] * (1 if first else 3)
    if first:
        args, specs = [order, table, *mats], [IN_SMEM] + [IN_VMEM] * (1 + len(mats))
        ahead, back = jax.ShapeDtypeStruct((rows, count), BF16), jax.ShapeDtypeStruct((count, rows), BF16)
        shapes += [ahead, ahead, back, back, jax.ShapeDtypeStruct((rows, LANES), F32)]
    else:
        args, specs = list(mats), [IN_VMEM] * len(mats)
    args += [*sums, measured, theirs, *before]
    specs += [IN_VMEM] * (5 + len(before))
    return pl.pallas_call(
        functools.partial(residual_kernel, dims, first, total // 2, rdev, zdev, offset, width),
        in_specs=specs,
        out_specs=[IN_VMEM] * len(shapes),
        out_shape=shapes,
        compiler_params=pltpu.CompilerParams(vmem_limit_bytes=30 * MIB),
        cost_estimate=pl.CostEstimate(
            flops=12 * count * rows * width, bytes_accessed=8 * width * (count + rows), transcendentals=0
        ),
        name=f"residual_{chunk}",
    )(*args)


def back_kernel(high_ref, low_ref, mine_ref, sent_ref, *outs):
    block, width = outs[0].shape[1:]
    back = high_ref[:4 * block], low_ref[:4 * block]
    for at, size in tiles(width):
        columns = slice(at, at + size)
        rows = mine_ref.shape[0] * mine_ref.shape[1]
        residual = jnp.concatenate([r[:, :, columns].reshape(rows, size) for r in (mine_ref, sent_ref)], axis=0)
        given = dot3(back, split(residual))
        for i, ref in enumerate(outs):
            for j in range(2):
                ref[j, :, columns] = given[(2 * i + j) * block:(2 * i + j + 1) * block]


def back_step(high, low, mine, sent, far):
    given = jax.ShapeDtypeStruct(far.shape, F32)
    return pl.pallas_call(
        back_kernel,
        in_specs=[IN_VMEM] * 4,
        out_specs=[IN_VMEM] * 2,
        out_shape=[given, given],
        compiler_params=pltpu.CompilerParams(vmem_limit_bytes=30 * MIB),
        cost_estimate=pl.CostEstimate(
            flops=6 * high.size * far.shape[2], bytes_accessed=8 * mine.size, transcendentals=0
        ),
        name="back_0",
    )(high, low, mine, sent)


def update_kernel(dims, first, halves, half, offset, width, *refs):
    per, groups, zb, cells = dims
    count = groups * SUBLANES
    left_ref, backs, refs = refs[0], refs[len(halves) * groups:0:-1], refs[1 + len(halves) * groups:]
    vol_ref, *refs = refs
    zdev, depth = vol_ref.shape[1], left_ref.shape[2]
    if not first:
        refs = refs[1:]
    pieces = refs[:-3]
    if pieces:
        *pieces, out_ref, res_ref, buf, sems, res_sems = refs
    else:
        out_ref, buf, sems = refs
    odd = lax.rem(lax.axis_index("slab"), 2)
    leaving = []
    for h, ref in enumerate(pieces):
        columns = pl.ds(pl.multiple_of(lax.rem(odd + h, 2) * half, LANES), half)
        leaving.append(pltpu.make_async_copy(ref, res_ref.at[:, :, columns], res_sems.at[h]))
        leaving[-1].start()
    held = len(halves) < vol_ref.shape[0]
    for i, zp, slices, start in volume_pieces(dims, zdev, half, offset, halves):
        rows = slice(zp * SUBLANES, (zp + 1) * SUBLANES)
        left = left_ref[zp]
        for at, size in tiles(width):
            piece = slice(at, at + size)
            back = jnp.concatenate([backs[i * groups + d][rows, piece] for d in range(groups)], axis=0)
            high, low = split(back)
            pad = jnp.zeros((depth - 3 * count, size), BF16)
            change = dot(left, jnp.concatenate([high, low, high, pad], axis=0))
            for z in range(zb):
                buf[i, zp * zb + z, :, piece] = (
                    vol_ref[halves[i] if held else i, zp * zb + z, :, piece] + change[z * cells:(z + 1) * cells]
                )
        leaving.append(
            pltpu.make_async_copy(buf.at[i, slices], out_ref.at[slices, :, pl.ds(start, width)], sems.at[i, zp])
        )
        leaving[-1].start()
    for copy in leaving:
        copy.wait()


def update_step(dims, chunk, halves, offset, width, left, backs, pieces, kept, volume, out):
    per, groups, zb, cells = dims
    zdev, _, total = volume.shape
    first = out is None
    args = [left, *backs[::-1], kept]
    shapes = [jax.ShapeDtypeStruct(volume.shape, F32)]
    scratch = [
        pltpu.VMEM((len(halves), zdev, cells, width), F32),
        pltpu.SemaphoreType.DMA((len(halves), zdev // zb)),
    ]
    specs = [IN_VMEM] * len(args)
    aliases = {}
    if not first:
        aliases = {len(args): 0}
        args += [out]
        specs += [ANYWHERE]
    if pieces:
        args += pieces
        specs += [IN_VMEM] * 2
        shapes += [jax.ShapeDtypeStruct((*pieces[0].shape[:2], total), F32)]
        scratch += [pltpu.SemaphoreType.DMA((2,))]
    size = zdev * cells * width * len(halves)
    return pl.pallas_call(
        functools.partial(update_kernel, dims, first, halves, total // 2, offset, width),
        in_specs=specs,
        out_specs=[ANYWHERE] * len(shapes),
        out_shape=shapes,
        scratch_shapes=scratch,
        input_output_aliases=aliases,
        compiler_params=pltpu.CompilerParams(vmem_limit_bytes=20 * MIB),
        cost_estimate=pl.CostEstimate(flops=2 * size * 48, bytes_accessed=size * 4, transcendentals=0),
        name=f"update_{chunk}_{halves[0]}",
    )(*args)


def body(volume, measured, foot_start, foot_len, order, table):
    slabs, groups = lax.axis_size("slab"), lax.axis_size("ang")
    per, rdev, total = measured.shape
    zdev, cells, _ = volume.shape
    half = total // 2
    zb = SUBLANES // per
    dims = (per, groups, zb, cells)
    each = half // CHUNKS
    widths = [each] * CHUNKS
    offsets = [sum(widths[:c]) for c in range(CHUNKS)]

    def along(value, to):
        pairs = [(s, to(s)) for s in range(slabs)]
        return lax.ppermute(value, "slab", pairs)

    def spread(value, other, d):
        if not (other or d):
            return value
        pairs = [
            (s * groups + a, (s ^ other) * groups + (a + d) % groups) for s in range(slabs) for a in range(groups)
        ]
        return lax.ppermute(value, ("slab", "ang"), pairs)

    def facing(s):
        return s ^ 2

    def step(up, busy):
        def to(s):
            there = s + 4 if up(s) else s - 4
            if 0 <= there < slabs:
                return there
            return there % slabs if busy else facing(s)
        return to

    def beyond(c):
        return step(lambda s: not s & 2, c < CHUNKS - 1)

    def back_from_beyond(c):
        return step(lambda s: s & 2, c > 0)

    odd = lax.rem(lax.axis_index("slab"), 2)
    theirs = along(
        lax.dynamic_slice_in_dim(measured, (1 - odd) * half, half, 2).astype(F32), lambda s: s ^ 1
    )

    sums, kept, left = [], [[] for _ in range(CHUNKS)], None
    for c in range(CHUNKS):
        parts = []
        for halves in RAY_HALVES[c]:
            made = ray_sums(
                dims, c, halves, offsets[c], widths[c], left, (order, foot_start, foot_len), table, volume
            )
            parts += made[:len(halves) * groups]
            if left is None:
                left = made[-1]
            elif c:
                kept[c] += [(h, made[-1]) for h in halves]
        parts = [spread(parts[h * groups + d], h, d) for h in range(2) for d in range(groups)]
        if c:
            parts, _ = lax.optimization_barrier((parts, sums[-1][0]))
        own = jnp.stack([sum(parts[:groups]), sum(parts[groups:])])
        near = along(own, facing)
        if c == 0:
            first_columns, update_left, *mats = prepare_step(dims, rdev, widths[0], order, table, own, near, volume)
            kept[0] = [(h, first_columns) for h in range(2)]
        if c == 1:
            near, first_columns = lax.optimization_barrier((near, first_columns))
        far = along(near, beyond(c))
        sums.append((own, near, far))
    pieces, given = [], []
    for c in range(CHUNKS):
        mine, sent, *made = residual_step(
            dims, zdev, c, offsets[c], widths[c], mats, pieces, order, table, sums[c], measured, theirs
        )
        if c == 0:
            far, *mats = made
            own, near = back_step(mats[2], mats[3], mine, sent, far)
        else:
            own, near, far = made
        pieces = [mine, sent]
        near = near + along(far, back_from_beyond(c))
        arrived = along(near, facing)
        halves = [own[i] + arrived[i] for i in range(2)]
        given.append([spread(halves[h], h, d) for h in range(2) for d in range(groups)])
    pieces = [mine, along(sent, lambda s: s ^ 1)]
    out, res = None, []
    for c in range(CHUNKS):
        for halves in UPDATE_HALVES[c]:
            backs = [b for h in halves for b in given[c][h * groups:(h + 1) * groups]]
            write = c == CHUNKS - 1 and halves[0] == 0
            out, *made = update_step(
                dims, c, halves, offsets[c], widths[c], update_left, backs, pieces if write else [],
                dict(kept[c])[halves[0]], volume, out,
            )
            res += made
    return out, res[0]


def solution(mesh):
    return jax.shard_map(
        body,
        mesh=mesh,
        in_specs=(
            P("slab", "ang", None),
            P("ang", "slab", None),
            P("slab", "ang"),
            P("slab", "ang"),
            P(),
            P(),
        ),
        out_specs=(P("slab", "ang", None), P("ang", "slab", None)),
        check_vma=False,
    )
```

```python
import functools

import jax
import jax.numpy as jnp
from jax import lax
from jax.experimental import pallas as pl
from jax.experimental.pallas import tpu as pltpu
from jax.sharding import PartitionSpec as P

F32, BF16 = jnp.float32, jnp.bfloat16
CHUNKS = 2
RAY_HALVES = [[(0, 1)], [(0, 1)]]
UPDATE_HALVES = [[(0, 1)], [(0,), (1,)]]
TILE = 512
LANES = 128
SUBLANES = 8
MIB = 1024 * 1024

IN_VMEM = pl.BlockSpec(memory_space=pltpu.VMEM)
IN_SMEM = pl.BlockSpec(memory_space=pltpu.SMEM)
ANYWHERE = pl.BlockSpec(memory_space=pl.ANY)


def split(value):
    high = value.astype(BF16)
    return high, (value - high.astype(F32)).astype(BF16)


def dot(a, b):
    return jnp.dot(a, b, preferred_element_type=F32)


def dot3(a, b):
    return dot(a[0], b[0]) + (dot(a[0], b[1]) + dot(a[1], b[0]))


def iota(shape, dim):
    return lax.broadcasted_iota(jnp.int32, shape, dim)


def low_bits(value, size):
    assert size & (size - 1) == 0
    return value & (size - 1)


def over(value, size):
    assert size & (size - 1) == 0
    return value >> (size.bit_length() - 1)


def pick(index, values):
    out = jnp.zeros(index.shape, values[0].dtype)
    for at, value in enumerate(values):
        out = jnp.where(index == at, value, out)
    return out


def tiles(width):
    step = min(TILE, width)
    return [(at, min(step, width - at)) for at in range(0, width, step)]


def slice_weights(dims, sign, order_ref, table_ref, rows_ref):
    per, groups, zb, cells = dims
    ang = lax.axis_index("ang")
    for d in range(groups):
        group = lax.rem(ang + sign * d + groups, groups)
        for z in range(zb):
            for a in range(per):
                at = (d * zb + z) * per + a
                rows_ref[at:at + 1, :] = table_ref[pl.ds(order_ref[group * per + a], 1), :]
    wide = rows_ref[...]
    total = wide.shape[1]
    row_slice = low_bits(over(iota(wide.shape, 0), per), zb)
    lane_slice = over(iota(wide.shape, 1), cells)
    out = jnp.zeros_like(wide)
    for z in range(zb):
        shift = lax.rem(z * cells - ang * cells + total, total)
        here = jnp.logical_and(row_slice == z, lane_slice == z)
        out = jnp.where(here, pltpu.roll(wide, shift, 1), out)
    return out


def volume_pieces(dims, zdev, half, offset, halves):
    odd = lax.rem(lax.axis_index("slab"), 2)
    zb = dims[2]
    for i, h in enumerate(halves):
        start = pl.multiple_of(lax.rem(odd + h, 2) * half + offset, LANES)
        for zp in range(zdev // zb):
            yield i, zp, slice(zp * zb, (zp + 1) * zb), start


def rays_kernel(dims, first, keep, extra, halves, half, offset, width, *refs):
    per, groups, zb, cells = dims
    count = groups * SUBLANES
    if first:
        order_ref, start_ref, len_ref, table_ref, vol_ref, *refs = refs
    elif extra:
        start_buf, len_buf, given_ref, vol_ref, *refs = refs
    else:
        given_ref, vol_ref, *refs = refs
    outs, refs = refs[:len(halves) * groups], refs[len(halves) * groups:]
    if first:
        left_ref, buf, sems, table_buf, order_buf, start_buf, len_buf, rows_ref, small_sems = refs
    else:
        buf, sems = refs
    zdev = vol_ref.shape[0]
    copies = []
    if first:
        small = [
            pltpu.make_async_copy(source, to, small_sems.at[i])
            for i, (source, to) in enumerate(
                [(order_ref, order_buf), (table_ref, table_buf), (start_ref, start_buf), (len_ref, len_buf)]
            )
        ]
        for copy in small:
            copy.start()
    for h, zp, slices, start in volume_pieces(dims, zdev, half, offset, halves):
        source = vol_ref.at[slices, :, pl.ds(start, width)]
        copies.append((h, zp, pltpu.make_async_copy(source, buf.at[h, slices], sems.at[h, zp])))
        copies[-1][-1].start()
    if first:
        small[0].wait()
        small[1].wait()
        both = jnp.concatenate(split(slice_weights(dims, 1, order_buf, table_buf, rows_ref)), axis=0)
        left = jnp.concatenate([both, both], axis=1)
        left_ref[...] = left
        small[2].wait()
        small[3].wait()
    else:
        left = given_ref[...]
    if extra:
        shape = (SUBLANES, LANES)
        angle, lane = low_bits(iota(shape, 0), per), iota(shape, 1)
        starts = pick(angle, [start_buf[0, a].astype(F32) for a in range(per)])
        lengths = pick(angle, [len_buf[0, a].astype(F32) for a in range(per)])
        for d in range(groups):
            foot = jnp.where(lane == 2 * d, starts, jnp.where(lane == 2 * d + 1, lengths, 0.0))
            for h in range(len(halves)):
                outs[h * groups + d][:, zdev // zb * width:] = foot
    for h, zp, copy in copies:
        copy.wait()
        for at, size in tiles(width):
            parts = [split(buf[h, zp * zb + z, :, at:at + size]) for z in range(zb)]
            product = dot(left, jnp.concatenate([p[0] for p in parts] + [p[1] for p in parts], axis=0))
            sums = product[:count] + product[count:]
            for d in range(groups):
                outs[h * groups + d][:, zp * width + at:zp * width + at + size] = (
                    sums[d * SUBLANES:(d + 1) * SUBLANES]
                )


def ray_sums(dims, chunk, halves, offset, width, given, small, table, volume):
    per, groups, zb, cells = dims
    zdev, _, total = volume.shape
    first, keep, extra = given is None, chunk > 0, chunk == 0
    count, all_cells = groups * SUBLANES, table.shape[1]
    out = jax.ShapeDtypeStruct((SUBLANES, zdev // zb * width + (LANES if extra else 0)), F32)
    left = jax.ShapeDtypeStruct((2 * count, 2 * zb * cells), BF16)
    columns = (len(halves), zdev, cells, width)
    assert zb * cells == all_cells
    shapes = [out] * (len(halves) * groups)
    scratch = [] if keep else [pltpu.VMEM(columns, F32)]
    scratch += [pltpu.SemaphoreType.DMA((len(halves), zdev // zb))]
    args, specs, limit = [given, volume], [IN_VMEM, ANYWHERE], 40
    if first:
        scratch += [pltpu.VMEM(table.shape, F32)] + [pltpu.SMEM(a.shape, a.dtype) for a in small]
        scratch += [pltpu.VMEM((count, all_cells), F32), pltpu.SemaphoreType.DMA((4,))]
        args, specs, limit = [*small, table, volume], [ANYWHERE] * 5, 58
        shapes += [left]
    elif extra:
        args, specs, limit = [*small[1:], *args], [IN_SMEM] * 2 + specs, 50
    if keep:
        shapes += [jax.ShapeDtypeStruct(columns, F32)]
    size = zdev * cells * width * len(halves)
    return pl.pallas_call(
        functools.partial(rays_kernel, dims, first, keep, extra, halves, total // 2, offset, width),
        in_specs=specs,
        out_specs=[IN_VMEM] * len(shapes),
        out_shape=shapes,
        scratch_shapes=scratch,
        compiler_params=pltpu.CompilerParams(vmem_limit_bytes=limit * MIB),
        cost_estimate=pl.CostEstimate(flops=2 * size * 16, bytes_accessed=size * 4, transcendentals=0),
        name=f"ray_sums_{chunk}_{halves[0]}",
    )(*args)


def hat_weights(dims, zdev, start, length, row):
    per, groups, zb, cells = dims
    at = low_bits(iota(start.shape, 0), zdev * per)
    slice_at = over(at, zb * per) * zb + low_bits(over(at, per), zb)
    span = jnp.where(length > 0.0, length, 1.0) / zdev
    centre = start + (slice_at.astype(F32) + 0.5) * span
    hat = jnp.maximum(0.0, 1.0 - jnp.abs(row + 0.5 - centre) / span)
    return jnp.where(jnp.logical_and(row >= start, row < start + length), hat, 0.0)


def footprint_matrix(dims, zdev, rdev, foot):
    per = dims[0]
    rows = 2 * per * rdev
    slab = lax.axis_index("slab")
    sibling = slab + 1 - 2 * lax.rem(slab, 2)
    row_id = iota((1, rows), 1)
    row_slab = jnp.where(row_id < per * rdev, slab, sibling)
    row = (row_slab * rdev + low_bits(row_id, rdev)).astype(F32)
    shape = (foot.shape[0], rows)
    same_angle = low_bits(iota(shape, 0), per) == low_bits(over(iota(shape, 1), rdev), per)
    beyond = slab + jnp.where(low_bits(slab, 4) < 2, -2, 2)
    there = jnp.logical_and(beyond >= 0, beyond < lax.axis_size("slab"))
    known = jnp.where(there, foot.shape[0], foot.shape[0] // 3 * 2)
    meets = jnp.logical_and(same_angle, iota(shape, 0) < known)
    return jnp.where(meets, hat_weights(dims, zdev, foot[:, 0:1], foot[:, 1:2], row), 0.0)


def update_weights(dims, zdev, rdev, foot, order_ref, table_ref, rows_ref, out_ref):
    per, groups, zb, cells = dims
    count = groups * SUBLANES
    weights = slice_weights(dims, -1, order_ref, table_ref, rows_ref)
    window = -(-5 * rdev // LANES) * LANES
    row = ((lax.axis_index("slab") - 2) * rdev + iota((1, window), 1)).astype(F32)
    sums = [
        jnp.sum(hat_weights(dims, zdev, foot[:, 2 * d:2 * d + 1], foot[:, 2 * d + 1:2 * d + 2], row), axis=1, keepdims=True)
        for d in range(groups)
    ]
    pad = jnp.zeros((out_ref.shape[2] - 3 * count, weights.shape[1]), F32)
    for zp in range(zdev // zb):
        slices = jnp.concatenate([s[zp * SUBLANES:(zp + 1) * SUBLANES] for s in sums], axis=0)
        scaled = weights / jnp.sum(weights * slices, axis=0, keepdims=True)
        high = scaled.astype(BF16).astype(F32)
        stacked = jnp.concatenate([high, high, scaled - high, pad], axis=0)
        out_ref[zp] = stacked.T.astype(BF16)


def prepare_kernel(dims, rdev, half, width, order_ref, table_ref, foot_ref, _, vol_ref, kept_ref, left_ref, sems, rows_ref):
    zdev = vol_ref.shape[0]
    copies = []
    for h, zp, slices, start in volume_pieces(dims, zdev, half, 0, (0, 1)):
        source = vol_ref.at[slices, :, pl.ds(start, width)]
        copies.append(pltpu.make_async_copy(source, kept_ref.at[h, slices], sems.at[h, zp]))
        copies[-1].start()
    batches = zdev // dims[2]
    foot = jnp.concatenate([foot_ref[0, :, batches * width:]] * batches, axis=0)
    update_weights(dims, zdev, rdev, foot, order_ref, table_ref, rows_ref, left_ref)
    for copy in copies:
        copy.wait()


def prepare_step(dims, rdev, width, order, table, own, after, volume):
    per, groups, zb, cells = dims
    zdev, _, total = volume.shape
    depth = -(-3 * groups * SUBLANES // LANES) * LANES
    return pl.pallas_call(
        functools.partial(prepare_kernel, dims, rdev, total // 2, width),
        in_specs=[IN_SMEM, IN_VMEM, IN_VMEM, ANYWHERE, ANYWHERE],
        out_specs=[IN_VMEM, IN_VMEM],
        out_shape=[
            jax.ShapeDtypeStruct((2, zdev, cells, width), F32),
            jax.ShapeDtypeStruct((zdev // zb, zb * cells, depth), BF16),
        ],
        scratch_shapes=[
            pltpu.SemaphoreType.DMA((2, zdev // zb)),
            pltpu.VMEM((groups * SUBLANES, table.shape[1]), F32),
        ],
        compiler_params=pltpu.CompilerParams(vmem_limit_bytes=32 * MIB),
        cost_estimate=pl.CostEstimate(flops=0, bytes_accessed=8 * zdev * cells * width, transcendentals=0),
        name="prepare",
    )(order, table, own, after, volume)


def residual_kernel(dims, first, half, rdev, zdev, offset, width, *refs):
    per, groups, zb, cells = dims
    block = zdev * per
    if first:
        order_ref, table_ref, *refs = refs
    else:
        mats, inverse_ref, refs = refs[:4], refs[4], refs[5:]
    sums_refs, (mine_ref, theirs_ref), refs = refs[:3], refs[3:5], refs[5:]
    if not first:
        mine_before, sent_before, *refs = refs
    mine_out, sent_out, *refs = refs
    if not first:
        mine_out[:, :, :offset] = mine_before[...]
        sent_out[:, :, :offset] = sent_before[...]
    outs, refs = refs[:3], refs[3:]
    if first:
        foot = jnp.concatenate(
            [r[i, :, zdev // zb * width:] for r in sums_refs for i in range(2) for _ in range(zdev // zb)], axis=0
        )
        kernel = footprint_matrix(dims, zdev, rdev, foot)
        count, rows = kernel.shape
        kernel_t = kernel.T
        cover = jnp.sum(kernel_t, axis=1, keepdims=True)
        angle = low_bits(over(iota((rows, 1), 0), rdev), per)
        path = jnp.zeros((rows, 1), F32)
        for a in range(per):
            at = order_ref[lax.axis_index("ang") * per + a]
            path = jnp.where(angle == a, jnp.sum(table_ref[pl.ds(at, 1), :], axis=1, keepdims=True), path)
        inverse = 1.0 / jnp.maximum(path * cover, 0.25)
        ahead, back = split(kernel_t), split(kernel)
        for ref, value in zip(refs, (*ahead, *back)):
            ref[...] = value
        refs[4][...] = jnp.broadcast_to(inverse, (rows, LANES))
    else:
        ahead, back = (mats[0][...], mats[1][...]), (mats[2][...], mats[3][...])
        inverse = inverse_ref[:, 0:1]
    start = lax.rem(lax.axis_index("slab"), 2) * half + offset
    for at, size in tiles(width):
        columns = slice(at, at + size)
        mine = mine_ref[:, :, pl.ds(pl.multiple_of(start + at, LANES), size)].astype(F32)
        theirs = theirs_ref[:, :, offset + at:offset + at + size]
        measured = jnp.concatenate([m.reshape(per * rdev, size) for m in (mine, theirs)], axis=0)
        sums = jnp.concatenate(
            [
                r[i, :, zp * width + at:zp * width + at + size]
                for r in sums_refs for i in range(2) for zp in range(zdev // zb)
            ],
            axis=0,
        )
        residual = (measured - dot3(ahead, split(sums))) * inverse
        placed = slice(offset + at, offset + at + size)
        mine_out[:, :, placed] = residual[:per * rdev].reshape(per, rdev, size)
        sent_out[:, :, placed] = residual[per * rdev:].reshape(per, rdev, size)
        given = dot3(back, split(residual))
        for i, ref in enumerate(outs):
            for j in range(2):
                ref[j, :, columns] = given[(2 * i + j) * block:(2 * i + j + 1) * block]


def residual_step(dims, zdev, chunk, offset, width, mats, before, order, table, sums, measured, theirs):
    per, groups, zb, cells = dims
    _, rdev, total = measured.shape
    first = chunk == 0
    block = zdev * per
    count, rows = 6 * block, 2 * per * rdev
    given = jax.ShapeDtypeStruct((2, block, width), F32)
    piece = jax.ShapeDtypeStruct((per, rdev, offset + width), F32)
    shapes = [piece, piece, given, given, given]
    if first:
        args, specs = [order, table], [IN_SMEM, IN_VMEM]
        ahead, back = jax.ShapeDtypeStruct((rows, count), BF16), jax.ShapeDtypeStruct((count, rows), BF16)
        shapes += [ahead, ahead, back, back, jax.ShapeDtypeStruct((rows, LANES), F32)]
    else:
        args, specs = list(mats), [IN_VMEM] * len(mats)
    args += [*sums, measured, theirs, *before]
    specs += [IN_VMEM] * (5 + len(before))
    return pl.pallas_call(
        functools.partial(residual_kernel, dims, first, total // 2, rdev, zdev, offset, width),
        in_specs=specs,
        out_specs=[IN_VMEM] * len(shapes),
        out_shape=shapes,
        compiler_params=pltpu.CompilerParams(vmem_limit_bytes=30 * MIB),
        cost_estimate=pl.CostEstimate(
            flops=12 * count * rows * width, bytes_accessed=8 * width * (count + rows), transcendentals=0
        ),
        name=f"residual_{chunk}",
    )(*args)


def update_kernel(dims, first, halves, half, offset, width, *refs):
    per, groups, zb, cells = dims
    count = groups * SUBLANES
    left_ref, backs, refs = refs[0], refs[len(halves) * groups:0:-1], refs[1 + len(halves) * groups:]
    vol_ref, *refs = refs
    zdev, depth = vol_ref.shape[1], left_ref.shape[2]
    if not first:
        refs = refs[1:]
    pieces = refs[:-3]
    if pieces:
        *pieces, out_ref, res_ref, buf, sems, res_sems = refs
    else:
        out_ref, buf, sems = refs
    odd = lax.rem(lax.axis_index("slab"), 2)
    leaving = []
    for h, ref in enumerate(pieces):
        columns = pl.ds(pl.multiple_of(lax.rem(odd + h, 2) * half, LANES), half)
        leaving.append(pltpu.make_async_copy(ref, res_ref.at[:, :, columns], res_sems.at[h]))
        leaving[-1].start()
    held = len(halves) < vol_ref.shape[0]
    for i, zp, slices, start in volume_pieces(dims, zdev, half, offset, halves):
        rows = slice(zp * SUBLANES, (zp + 1) * SUBLANES)
        left = left_ref[zp]
        for at, size in tiles(width):
            piece = slice(at, at + size)
            back = jnp.concatenate([backs[i * groups + d][rows, piece] for d in range(groups)], axis=0)
            high, low = split(back)
            pad = jnp.zeros((depth - 3 * count, size), BF16)
            change = dot(left, jnp.concatenate([high, low, high, pad], axis=0))
            for z in range(zb):
                buf[i, zp * zb + z, :, piece] = (
                    vol_ref[halves[i] if held else i, zp * zb + z, :, piece] + change[z * cells:(z + 1) * cells]
                )
        leaving.append(
            pltpu.make_async_copy(buf.at[i, slices], out_ref.at[slices, :, pl.ds(start, width)], sems.at[i, zp])
        )
        leaving[-1].start()
    for copy in leaving:
        copy.wait()


def update_step(dims, chunk, halves, offset, width, left, backs, pieces, kept, volume, out):
    per, groups, zb, cells = dims
    zdev, _, total = volume.shape
    first = out is None
    args = [left, *backs[::-1], kept]
    shapes = [jax.ShapeDtypeStruct(volume.shape, F32)]
    scratch = [
        pltpu.VMEM((len(halves), zdev, cells, width), F32),
        pltpu.SemaphoreType.DMA((len(halves), zdev // zb)),
    ]
    specs = [IN_VMEM] * len(args)
    aliases = {}
    if not first:
        aliases = {len(args): 0}
        args += [out]
        specs += [ANYWHERE]
    if pieces:
        args += pieces
        specs += [IN_VMEM] * 2
        shapes += [jax.ShapeDtypeStruct((*pieces[0].shape[:2], total), F32)]
        scratch += [pltpu.SemaphoreType.DMA((2,))]
    size = zdev * cells * width * len(halves)
    return pl.pallas_call(
        functools.partial(update_kernel, dims, first, halves, total // 2, offset, width),
        in_specs=specs,
        out_specs=[ANYWHERE] * len(shapes),
        out_shape=shapes,
        scratch_shapes=scratch,
        input_output_aliases=aliases,
        compiler_params=pltpu.CompilerParams(vmem_limit_bytes=20 * MIB),
        cost_estimate=pl.CostEstimate(flops=2 * size * 48, bytes_accessed=size * 4, transcendentals=0),
        name=f"update_{chunk}_{halves[0]}",
    )(*args)


def body(volume, measured, foot_start, foot_len, order, table):
    slabs, groups = lax.axis_size("slab"), lax.axis_size("ang")
    per, rdev, total = measured.shape
    zdev, cells, _ = volume.shape
    half = total // 2
    zb = SUBLANES // per
    dims = (per, groups, zb, cells)
    each = half // CHUNKS
    widths = [each] * CHUNKS
    offsets = [sum(widths[:c]) for c in range(CHUNKS)]

    def along(value, to):
        pairs = [(s, to(s)) for s in range(slabs)]
        return lax.ppermute(value, "slab", pairs)

    def spread(value, other, d):
        if not (other or d):
            return value
        pairs = [
            (s * groups + a, (s ^ other) * groups + (a + d) % groups) for s in range(slabs) for a in range(groups)
        ]
        return lax.ppermute(value, ("slab", "ang"), pairs)

    def facing(s):
        return s ^ 2

    def step(up, busy):
        def to(s):
            there = s + 4 if up(s) else s - 4
            if 0 <= there < slabs:
                return there
            return there % slabs if busy else facing(s)
        return to

    def beyond(c):
        return step(lambda s: not s & 2, c < CHUNKS - 1)

    def back_from_beyond(c):
        return step(lambda s: s & 2, c > 0)

    odd = lax.rem(lax.axis_index("slab"), 2)
    theirs = along(
        lax.dynamic_slice_in_dim(measured, (1 - odd) * half, half, 2).astype(F32), lambda s: s ^ 1
    )

    sums, kept, left = [], [[] for _ in range(CHUNKS)], None
    for c in range(CHUNKS):
        parts = []
        for halves in RAY_HALVES[c]:
            made = ray_sums(
                dims, c, halves, offsets[c], widths[c], left, (order, foot_start, foot_len), table, volume
            )
            parts += made[:len(halves) * groups]
            if left is None:
                left = made[-1]
            elif c:
                kept[c] += [(h, made[-1]) for h in halves]
        parts = [spread(parts[h * groups + d], h, d) for h in range(2) for d in range(groups)]
        if c:
            parts, _ = lax.optimization_barrier((parts, sums[-1][0]))
        own = jnp.stack([sum(parts[:groups]), sum(parts[groups:])])
        near = along(own, facing)
        far = along(near, beyond(c))
        sums.append((own, near, far))
    pieces, given, mats = [], [], None
    for c in range(CHUNKS):
        mine, sent, own, near, far, *rest = residual_step(
            dims, zdev, c, offsets[c], widths[c], mats, pieces, order, table, sums[c], measured, theirs
        )
        pieces = [mine, sent]
        mats = rest if c == 0 else mats
        returned = along(far, back_from_beyond(c))
        if c == 1:
            first_columns, update_left = prepare_step(
                dims, rdev, widths[0], order, table, sums[0][0], near_before, volume
            )
            returned, first_columns = lax.optimization_barrier((returned, first_columns))
            kept[0] = [(h, first_columns) for h in range(2)]
        near = near + returned
        near_before = near
        arrived = along(near, facing)
        halves = [own[i] + arrived[i] for i in range(2)]
        given.append([spread(halves[h], h, d) for h in range(2) for d in range(groups)])
    pieces = [mine, along(sent, lambda s: s ^ 1)]
    out, res = None, []
    for c in range(CHUNKS):
        for halves in UPDATE_HALVES[c]:
            backs = [b for h in halves for b in given[c][h * groups:(h + 1) * groups]]
            write = c == CHUNKS - 1 and halves[0] == 0
            out, *made = update_step(
                dims, c, halves, offsets[c], widths[c], update_left, backs, pieces if write else [],
                dict(kept[c])[halves[0]], volume, out,
            )
            res += made
    return out, res[0]


def solution(mesh):
    return jax.shard_map(
        body,
        mesh=mesh,
        in_specs=(
            P("slab", "ang", None),
            P("ang", "slab", None),
            P("slab", "ang"),
            P("slab", "ang"),
            P(),
            P(),
        ),
        out_specs=(P("slab", "ang", None), P("ang", "slab", None)),
        check_vma=False,
    )
```

```python
import functools

import jax
import jax.numpy as jnp
from jax import lax
from jax.experimental import pallas as pl
from jax.experimental.pallas import tpu as pltpu
from jax.sharding import PartitionSpec as P

F32, BF16 = jnp.float32, jnp.bfloat16
CHUNKS = 2
RAY_HALVES = [[(0, 1)], [(0, 1)]]
UPDATE_HALVES = [[(0, 1)], [(0,), (1,)]]
TILE = 512
LANES = 128
SUBLANES = 8
MIB = 1024 * 1024

IN_VMEM = pl.BlockSpec(memory_space=pltpu.VMEM)
IN_SMEM = pl.BlockSpec(memory_space=pltpu.SMEM)
ANYWHERE = pl.BlockSpec(memory_space=pl.ANY)


def split(value):
    high = value.astype(BF16)
    return high, (value - high.astype(F32)).astype(BF16)


def dot(a, b):
    return jnp.dot(a, b, preferred_element_type=F32)


def dot3(a, b):
    return dot(a[0], b[0]) + (dot(a[0], b[1]) + dot(a[1], b[0]))


def iota(shape, dim):
    return lax.broadcasted_iota(jnp.int32, shape, dim)


def low_bits(value, size):
    assert size & (size - 1) == 0
    return value & (size - 1)


def over(value, size):
    assert size & (size - 1) == 0
    return value >> (size.bit_length() - 1)


def pick(index, values):
    out = jnp.zeros(index.shape, values[0].dtype)
    for at, value in enumerate(values):
        out = jnp.where(index == at, value, out)
    return out


def tiles(width):
    step = min(TILE, width)
    return [(at, min(step, width - at)) for at in range(0, width, step)]


def slice_weights(dims, sign, order_ref, table_ref, rows_ref):
    per, groups, zb, cells = dims
    ang = lax.axis_index("ang")
    for d in range(groups):
        group = lax.rem(ang + sign * d + groups, groups)
        for z in range(zb):
            for a in range(per):
                at = (d * zb + z) * per + a
                rows_ref[at:at + 1, :] = table_ref[pl.ds(order_ref[group * per + a], 1), :]
    wide = rows_ref[...]
    total = wide.shape[1]
    row_slice = low_bits(over(iota(wide.shape, 0), per), zb)
    lane_slice = over(iota(wide.shape, 1), cells)
    out = jnp.zeros_like(wide)
    for z in range(zb):
        shift = lax.rem(z * cells - ang * cells + total, total)
        here = jnp.logical_and(row_slice == z, lane_slice == z)
        out = jnp.where(here, pltpu.roll(wide, shift, 1), out)
    return out


def volume_pieces(dims, zdev, half, offset, halves):
    odd = lax.rem(lax.axis_index("slab"), 2)
    zb = dims[2]
    for i, h in enumerate(halves):
        start = pl.multiple_of(lax.rem(odd + h, 2) * half + offset, LANES)
        for zp in range(zdev // zb):
            yield i, zp, slice(zp * zb, (zp + 1) * zb), start


def rays_kernel(dims, first, keep, extra, halves, half, offset, width, *refs):
    per, groups, zb, cells = dims
    count = groups * SUBLANES
    if first:
        order_ref, start_ref, len_ref, table_ref, vol_ref, *refs = refs
    elif extra:
        start_buf, len_buf, given_ref, vol_ref, *refs = refs
    else:
        given_ref, vol_ref, *refs = refs
    outs, refs = refs[:len(halves) * groups], refs[len(halves) * groups:]
    if first:
        left_ref, buf, sems, table_buf, order_buf, start_buf, len_buf, rows_ref, small_sems = refs
    else:
        buf, sems = refs
    zdev = vol_ref.shape[0]
    copies = []
    if first:
        small = [
            pltpu.make_async_copy(source, to, small_sems.at[i])
            for i, (source, to) in enumerate(
                [(order_ref, order_buf), (table_ref, table_buf), (start_ref, start_buf), (len_ref, len_buf)]
            )
        ]
        for copy in small:
            copy.start()
    for h, zp, slices, start in volume_pieces(dims, zdev, half, offset, halves):
        source = vol_ref.at[slices, :, pl.ds(start, width)]
        copies.append((h, zp, pltpu.make_async_copy(source, buf.at[h, slices], sems.at[h, zp])))
        copies[-1][-1].start()
    if first:
        small[0].wait()
        small[1].wait()
        both = jnp.concatenate(split(slice_weights(dims, 1, order_buf, table_buf, rows_ref)), axis=0)
        left = jnp.concatenate([both, both], axis=1)
        left_ref[...] = left
        small[2].wait()
        small[3].wait()
    else:
        left = given_ref[...]
    if extra:
        shape = (zdev * per, LANES)
        angle, lane = low_bits(iota(shape, 0), per), iota(shape, 1)
        starts = pick(angle, [start_buf[0, a].astype(F32) for a in range(per)])
        lengths = pick(angle, [len_buf[0, a].astype(F32) for a in range(per)])
        for d in range(groups):
            foot = jnp.where(lane == 2 * d, starts, jnp.where(lane == 2 * d + 1, lengths, 0.0))
            for h in range(len(halves)):
                outs[h * groups + d][:, width:] = foot
    for h, zp, copy in copies:
        copy.wait()
        for at, size in tiles(width):
            parts = [split(buf[h, zp * zb + z, :, at:at + size]) for z in range(zb)]
            product = dot(left, jnp.concatenate([p[0] for p in parts] + [p[1] for p in parts], axis=0))
            sums = product[:count] + product[count:]
            for d in range(groups):
                outs[h * groups + d][zp * SUBLANES:(zp + 1) * SUBLANES, at:at + size] = (
                    sums[d * SUBLANES:(d + 1) * SUBLANES]
                )


def ray_sums(dims, chunk, halves, offset, width, given, small, table, volume):
    per, groups, zb, cells = dims
    zdev, _, total = volume.shape
    first, keep, extra = given is None, chunk > 0, chunk == 0
    count, all_cells = groups * SUBLANES, table.shape[1]
    out = jax.ShapeDtypeStruct((zdev * per, width + (LANES if extra else 0)), F32)
    left = jax.ShapeDtypeStruct((2 * count, 2 * zb * cells), BF16)
    columns = (len(halves), zdev, cells, width)
    assert zb * cells == all_cells
    shapes = [out] * (len(halves) * groups)
    scratch = [] if keep else [pltpu.VMEM(columns, F32)]
    scratch += [pltpu.SemaphoreType.DMA((len(halves), zdev // zb))]
    args, specs, limit = [given, volume], [IN_VMEM, ANYWHERE], 40
    if first:
        scratch += [pltpu.VMEM(table.shape, F32)] + [pltpu.SMEM(a.shape, a.dtype) for a in small]
        scratch += [pltpu.VMEM((count, all_cells), F32), pltpu.SemaphoreType.DMA((4,))]
        args, specs, limit = [*small, table, volume], [ANYWHERE] * 5, 58
        shapes += [left]
    elif extra:
        args, specs, limit = [*small[1:], *args], [IN_SMEM] * 2 + specs, 50
    if keep:
        shapes += [jax.ShapeDtypeStruct(columns, F32)]
    size = zdev * cells * width * len(halves)
    return pl.pallas_call(
        functools.partial(rays_kernel, dims, first, keep, extra, halves, total // 2, offset, width),
        in_specs=specs,
        out_specs=[IN_VMEM] * len(shapes),
        out_shape=shapes,
        scratch_shapes=scratch,
        compiler_params=pltpu.CompilerParams(vmem_limit_bytes=limit * MIB),
        cost_estimate=pl.CostEstimate(flops=2 * size * 16, bytes_accessed=size * 4, transcendentals=0),
        name=f"ray_sums_{chunk}_{halves[0]}",
    )(*args)


def hat_weights(dims, zdev, start, length, row):
    per, groups, zb, cells = dims
    at = low_bits(iota(start.shape, 0), zdev * per)
    slice_at = over(at, zb * per) * zb + low_bits(over(at, per), zb)
    span = jnp.where(length > 0.0, length, 1.0) / zdev
    centre = start + (slice_at.astype(F32) + 0.5) * span
    hat = jnp.maximum(0.0, 1.0 - jnp.abs(row + 0.5 - centre) / span)
    return jnp.where(jnp.logical_and(row >= start, row < start + length), hat, 0.0)


def footprint_matrix(dims, zdev, rdev, foot):
    per = dims[0]
    rows = 2 * per * rdev
    slab = lax.axis_index("slab")
    sibling = slab + 1 - 2 * lax.rem(slab, 2)
    row_id = iota((1, rows), 1)
    row_slab = jnp.where(row_id < per * rdev, slab, sibling)
    row = (row_slab * rdev + low_bits(row_id, rdev)).astype(F32)
    shape = (foot.shape[0], rows)
    same_angle = low_bits(iota(shape, 0), per) == low_bits(over(iota(shape, 1), rdev), per)
    beyond = slab + jnp.where(low_bits(slab, 4) < 2, -2, 2)
    there = jnp.logical_and(beyond >= 0, beyond < lax.axis_size("slab"))
    known = jnp.where(there, foot.shape[0], foot.shape[0] // 3 * 2)
    meets = jnp.logical_and(same_angle, iota(shape, 0) < known)
    return jnp.where(meets, hat_weights(dims, zdev, foot[:, 0:1], foot[:, 1:2], row), 0.0)


def update_weights(dims, zdev, rdev, foot, order_ref, table_ref, rows_ref, out_ref):
    per, groups, zb, cells = dims
    count = groups * SUBLANES
    weights = slice_weights(dims, -1, order_ref, table_ref, rows_ref)
    window = -(-5 * rdev // LANES) * LANES
    row = ((lax.axis_index("slab") - 2) * rdev + iota((1, window), 1)).astype(F32)
    sums = [
        jnp.sum(hat_weights(dims, zdev, foot[:, 2 * d:2 * d + 1], foot[:, 2 * d + 1:2 * d + 2], row), axis=1, keepdims=True)
        for d in range(groups)
    ]
    pad = jnp.zeros((out_ref.shape[2] - 3 * count, weights.shape[1]), F32)
    for zp in range(zdev // zb):
        slices = jnp.concatenate([s[zp * SUBLANES:(zp + 1) * SUBLANES] for s in sums], axis=0)
        scaled = weights / jnp.sum(weights * slices, axis=0, keepdims=True)
        high = scaled.astype(BF16).astype(F32)
        stacked = jnp.concatenate([high, high, scaled - high, pad], axis=0)
        out_ref[zp] = stacked.T.astype(BF16)


def prepare_kernel(dims, rdev, half, width, order_ref, table_ref, foot_ref, _, vol_ref, kept_ref, left_ref, sems, rows_ref):
    zdev = vol_ref.shape[0]
    copies = []
    for h, zp, slices, start in volume_pieces(dims, zdev, half, 0, (0, 1)):
        source = vol_ref.at[slices, :, pl.ds(start, width)]
        copies.append(pltpu.make_async_copy(source, kept_ref.at[h, slices], sems.at[h, zp]))
        copies[-1].start()
    update_weights(dims, zdev, rdev, foot_ref[0, :, width:], order_ref, table_ref, rows_ref, left_ref)
    for copy in copies:
        copy.wait()


def prepare_step(dims, rdev, width, order, table, own, after, volume):
    per, groups, zb, cells = dims
    zdev, _, total = volume.shape
    depth = -(-3 * groups * SUBLANES // LANES) * LANES
    return pl.pallas_call(
        functools.partial(prepare_kernel, dims, rdev, total // 2, width),
        in_specs=[IN_SMEM, IN_VMEM, IN_VMEM, ANYWHERE, ANYWHERE],
        out_specs=[IN_VMEM, IN_VMEM],
        out_shape=[
            jax.ShapeDtypeStruct((2, zdev, cells, width), F32),
            jax.ShapeDtypeStruct((zdev // zb, zb * cells, depth), BF16),
        ],
        scratch_shapes=[
            pltpu.SemaphoreType.DMA((2, zdev // zb)),
            pltpu.VMEM((groups * SUBLANES, table.shape[1]), F32),
        ],
        compiler_params=pltpu.CompilerParams(vmem_limit_bytes=40 * MIB),
        cost_estimate=pl.CostEstimate(flops=0, bytes_accessed=8 * zdev * cells * width, transcendentals=0),
        name="prepare",
    )(order, table, own, after, volume)


def residual_kernel(dims, first, half, rdev, zdev, offset, width, *refs):
    per, groups, zb, cells = dims
    block = zdev * per
    if first:
        order_ref, table_ref, *refs = refs
    else:
        mats, inverse_ref, refs = refs[:4], refs[4], refs[5:]
    sums_refs, (mine_ref, theirs_ref), refs = refs[:3], refs[3:5], refs[5:]
    if not first:
        mine_before, sent_before, *refs = refs
    mine_out, sent_out, *refs = refs
    if not first:
        mine_out[:, :, :offset] = mine_before[...]
        sent_out[:, :, :offset] = sent_before[...]
    outs, refs = refs[:3], refs[3:]
    if first:
        foot = jnp.concatenate([r[i, :, width:] for r in sums_refs for i in range(2)], axis=0)
        kernel = footprint_matrix(dims, zdev, rdev, foot)
        count, rows = kernel.shape
        kernel_t = kernel.T
        cover = jnp.sum(kernel_t, axis=1, keepdims=True)
        angle = low_bits(over(iota((rows, 1), 0), rdev), per)
        path = jnp.zeros((rows, 1), F32)
        for a in range(per):
            at = order_ref[lax.axis_index("ang") * per + a]
            path = jnp.where(angle == a, jnp.sum(table_ref[pl.ds(at, 1), :], axis=1, keepdims=True), path)
        inverse = 1.0 / jnp.maximum(path * cover, 0.25)
        ahead, back = split(kernel_t), split(kernel)
        for ref, value in zip(refs, (*ahead, *back)):
            ref[...] = value
        refs[4][...] = jnp.broadcast_to(inverse, (rows, LANES))
    else:
        ahead, back = (mats[0][...], mats[1][...]), (mats[2][...], mats[3][...])
        inverse = inverse_ref[:, 0:1]
    start = lax.rem(lax.axis_index("slab"), 2) * half + offset
    for at, size in tiles(width):
        columns = slice(at, at + size)
        mine = mine_ref[:, :, pl.ds(pl.multiple_of(start + at, LANES), size)].astype(F32)
        theirs = theirs_ref[:, :, offset + at:offset + at + size]
        measured = jnp.concatenate([m.reshape(per * rdev, size) for m in (mine, theirs)], axis=0)
        sums = jnp.concatenate([r[i, :, columns] for r in sums_refs for i in range(2)], axis=0)
        residual = (measured - dot3(ahead, split(sums))) * inverse
        placed = slice(offset + at, offset + at + size)
        mine_out[:, :, placed] = residual[:per * rdev].reshape(per, rdev, size)
        sent_out[:, :, placed] = residual[per * rdev:].reshape(per, rdev, size)
        given = dot3(back, split(residual))
        for i, ref in enumerate(outs):
            for j in range(2):
                ref[j, :, columns] = given[(2 * i + j) * block:(2 * i + j + 1) * block]


def residual_step(dims, zdev, chunk, offset, width, mats, before, order, table, sums, measured, theirs):
    per, groups, zb, cells = dims
    _, rdev, total = measured.shape
    first = chunk == 0
    block = zdev * per
    count, rows = 6 * block, 2 * per * rdev
    given = jax.ShapeDtypeStruct((2, block, width), F32)
    piece = jax.ShapeDtypeStruct((per, rdev, offset + width), F32)
    shapes = [piece, piece, given, given, given]
    if first:
        args, specs = [order, table], [IN_SMEM, IN_VMEM]
        ahead, back = jax.ShapeDtypeStruct((rows, count), BF16), jax.ShapeDtypeStruct((count, rows), BF16)
        shapes += [ahead, ahead, back, back, jax.ShapeDtypeStruct((rows, LANES), F32)]
    else:
        args, specs = list(mats), [IN_VMEM] * len(mats)
    args += [*sums, measured, theirs, *before]
    specs += [IN_VMEM] * (5 + len(before))
    return pl.pallas_call(
        functools.partial(residual_kernel, dims, first, total // 2, rdev, zdev, offset, width),
        in_specs=specs,
        out_specs=[IN_VMEM] * len(shapes),
        out_shape=shapes,
        compiler_params=pltpu.CompilerParams(vmem_limit_bytes=30 * MIB),
        cost_estimate=pl.CostEstimate(
            flops=12 * count * rows * width, bytes_accessed=8 * width * (count + rows), transcendentals=0
        ),
        name=f"residual_{chunk}",
    )(*args)


def operand_order(halves, groups):
    at = list(range(len(halves) * groups))
    return at[1:groups] + at[groups + 1:] + at[groups:groups + 1] + at[:1]


def update_kernel(dims, first, halves, half, offset, width, *refs):
    per, groups, zb, cells = dims
    count = groups * SUBLANES
    left_ref, given, refs = refs[0], refs[1:1 + len(halves) * groups], refs[1 + len(halves) * groups:]
    backs = dict(zip(operand_order(halves, groups), given))
    vol_ref, *refs = refs
    zdev, depth = vol_ref.shape[1], left_ref.shape[2]
    if not first:
        refs = refs[1:]
    pieces = refs[:-3]
    if pieces:
        *pieces, out_ref, res_ref, buf, sems, res_sems = refs
    else:
        out_ref, buf, sems = refs
    odd = lax.rem(lax.axis_index("slab"), 2)
    leaving = []
    for h, ref in enumerate(pieces):
        columns = pl.ds(pl.multiple_of(lax.rem(odd + h, 2) * half, LANES), half)
        leaving.append(pltpu.make_async_copy(ref, res_ref.at[:, :, columns], res_sems.at[h]))
        leaving[-1].start()
    held = len(halves) < vol_ref.shape[0]
    for i, zp, slices, start in volume_pieces(dims, zdev, half, offset, halves):
        rows = slice(zp * SUBLANES, (zp + 1) * SUBLANES)
        left = left_ref[zp]
        for at, size in tiles(width):
            piece = slice(at, at + size)
            back = jnp.concatenate([backs[i * groups + d][rows, piece] for d in range(groups)], axis=0)
            high, low = split(back)
            pad = jnp.zeros((depth - 3 * count, size), BF16)
            change = dot(left, jnp.concatenate([high, low, high, pad], axis=0))
            for z in range(zb):
                buf[i, zp * zb + z, :, piece] = (
                    vol_ref[halves[i] if held else i, zp * zb + z, :, piece] + change[z * cells:(z + 1) * cells]
                )
        leaving.append(
            pltpu.make_async_copy(buf.at[i, slices], out_ref.at[slices, :, pl.ds(start, width)], sems.at[i, zp])
        )
        leaving[-1].start()
    for copy in leaving:
        copy.wait()


def update_step(dims, chunk, halves, offset, width, left, backs, pieces, kept, volume, out):
    per, groups, zb, cells = dims
    zdev, _, total = volume.shape
    first = out is None
    args = [left, *(backs[i] for i in operand_order(halves, groups)), kept]
    shapes = [jax.ShapeDtypeStruct(volume.shape, F32)]
    scratch = [
        pltpu.VMEM((len(halves), zdev, cells, width), F32),
        pltpu.SemaphoreType.DMA((len(halves), zdev // zb)),
    ]
    specs = [IN_VMEM] * len(args)
    aliases = {}
    if not first:
        aliases = {len(args): 0}
        args += [out]
        specs += [ANYWHERE]
    if pieces:
        args += pieces
        specs += [IN_VMEM] * 2
        shapes += [jax.ShapeDtypeStruct((*pieces[0].shape[:2], total), F32)]
        scratch += [pltpu.SemaphoreType.DMA((2,))]
    size = zdev * cells * width * len(halves)
    return pl.pallas_call(
        functools.partial(update_kernel, dims, first, halves, total // 2, offset, width),
        in_specs=specs,
        out_specs=[ANYWHERE] * len(shapes),
        out_shape=shapes,
        scratch_shapes=scratch,
        input_output_aliases=aliases,
        compiler_params=pltpu.CompilerParams(vmem_limit_bytes=20 * MIB),
        cost_estimate=pl.CostEstimate(flops=2 * size * 48, bytes_accessed=size * 4, transcendentals=0),
        name=f"update_{chunk}_{halves[0]}",
    )(*args)


def body(volume, measured, foot_start, foot_len, order, table):
    slabs, groups = lax.axis_size("slab"), lax.axis_size("ang")
    per, rdev, total = measured.shape
    zdev, cells, _ = volume.shape
    half = total // 2
    zb = SUBLANES // per
    dims = (per, groups, zb, cells)
    each = half // CHUNKS
    widths = [each - LANES] + [each] * (CHUNKS - 2) + [each + LANES]
    offsets = [sum(widths[:c]) for c in range(CHUNKS)]

    def along(value, to):
        pairs = [(s, to(s)) for s in range(slabs)]
        return lax.ppermute(value, "slab", pairs)

    def spread(value, other, d):
        if not (other or d):
            return value
        pairs = [
            (s * groups + a, (s ^ other) * groups + (a + d) % groups) for s in range(slabs) for a in range(groups)
        ]
        return lax.ppermute(value, ("slab", "ang"), pairs)

    def facing(s):
        return s ^ 2

    def step(up, busy):
        def to(s):
            there = s + 4 if up(s) else s - 4
            if 0 <= there < slabs:
                return there
            return there % slabs if busy else facing(s)
        return to

    def beyond(c):
        return step(lambda s: not s & 2, c < CHUNKS - 1)

    def back_from_beyond(c):
        return step(lambda s: s & 2, c > 0)

    odd = lax.rem(lax.axis_index("slab"), 2)
    theirs = along(
        lax.dynamic_slice_in_dim(measured, (1 - odd) * half, half, 2).astype(F32), lambda s: s ^ 1
    )

    sums, kept, left = [], [[] for _ in range(CHUNKS)], None
    for c in range(CHUNKS):
        parts = []
        for halves in RAY_HALVES[c]:
            made = ray_sums(
                dims, c, halves, offsets[c], widths[c], left, (order, foot_start, foot_len), table, volume
            )
            parts += made[:len(halves) * groups]
            if left is None:
                left = made[-1]
            elif c:
                kept[c] += [(h, made[-1]) for h in halves]
        parts = [spread(parts[h * groups + d], h, d) for h in range(2) for d in range(groups)]
        if c:
            parts, _ = lax.optimization_barrier((parts, sums[-1][0]))
        own = jnp.stack([sum(parts[:groups]), sum(parts[groups:])])
        near = along(own, facing)
        if c == 0:
            first_columns, update_left = prepare_step(dims, rdev, widths[0], order, table, own, near, volume)
            kept[0] = [(h, first_columns) for h in range(2)]
        if c == 1:
            near, first_columns = lax.optimization_barrier((near, first_columns))
        far = along(near, beyond(c))
        sums.append((own, near, far))
    pieces, given, mats = [], [], None
    for c in range(CHUNKS):
        mine, sent, own, near, far, *rest = residual_step(
            dims, zdev, c, offsets[c], widths[c], mats, pieces, order, table, sums[c], measured, theirs
        )
        pieces = [mine, sent]
        mats = rest if c == 0 else mats
        near = near + along(far, back_from_beyond(c))
        arrived = along(near, facing)
        halves = [own[i] + arrived[i] for i in range(2)]
        given.append([spread(halves[h], h, d) for h in range(2) for d in range(groups)])
    pieces = [mine, along(sent, lambda s: s ^ 1)]
    out, res = None, []
    for c in range(CHUNKS):
        for halves in UPDATE_HALVES[c]:
            backs = [b for h in halves for b in given[c][h * groups:(h + 1) * groups]]
            write = c == CHUNKS - 1 and halves[0] == 0
            out, *made = update_step(
                dims, c, halves, offsets[c], widths[c], update_left, backs, pieces if write else [],
                dict(kept[c])[halves[0]], volume, out,
            )
            res += made
    return out, res[0]


def solution(mesh):
    return jax.shard_map(
        body,
        mesh=mesh,
        in_specs=(
            P("slab", "ang", None),
            P("ang", "slab", None),
            P("slab", "ang"),
            P("slab", "ang"),
            P(),
            P(),
        ),
        out_specs=(P("slab", "ang", None), P("ang", "slab", None)),
        check_vma=False,
    )
```

```python
import functools

import jax
import jax.numpy as jnp
from jax import lax
from jax.experimental import pallas as pl
from jax.experimental.pallas import tpu as pltpu
from jax.sharding import PartitionSpec as P

F32, BF16 = jnp.float32, jnp.bfloat16
CHUNKS = 2
RAY_HALVES = [[(0, 1)], [(0, 1)]]
UPDATE_HALVES = [[(0, 1)], [(0,), (1,)]]
TILE = 512
LANES = 128
SUBLANES = 8
MIB = 1024 * 1024

IN_VMEM = pl.BlockSpec(memory_space=pltpu.VMEM)
IN_SMEM = pl.BlockSpec(memory_space=pltpu.SMEM)
ANYWHERE = pl.BlockSpec(memory_space=pl.ANY)


def split(value):
    high = value.astype(BF16)
    return high, (value - high.astype(F32)).astype(BF16)


def dot(a, b):
    return jnp.dot(a, b, preferred_element_type=F32)


def dot3(a, b):
    return dot(a[0], b[0]) + (dot(a[0], b[1]) + dot(a[1], b[0]))


def iota(shape, dim):
    return lax.broadcasted_iota(jnp.int32, shape, dim)


def low_bits(value, size):
    assert size & (size - 1) == 0
    return value & (size - 1)


def over(value, size):
    assert size & (size - 1) == 0
    return value >> (size.bit_length() - 1)


def pick(index, values):
    out = jnp.zeros(index.shape, values[0].dtype)
    for at, value in enumerate(values):
        out = jnp.where(index == at, value, out)
    return out


def tiles(width):
    step = min(TILE, width)
    return [(at, min(step, width - at)) for at in range(0, width, step)]


def slice_weights(dims, sign, order_ref, table_ref, rows_ref):
    per, groups, zb, cells = dims
    ang = lax.axis_index("ang")
    for d in range(groups):
        group = lax.rem(ang + sign * d + groups, groups)
        for z in range(zb):
            for a in range(per):
                at = (d * zb + z) * per + a
                rows_ref[at:at + 1, :] = table_ref[pl.ds(order_ref[group * per + a], 1), :]
    wide = rows_ref[...]
    total = wide.shape[1]
    row_slice = low_bits(over(iota(wide.shape, 0), per), zb)
    lane_slice = over(iota(wide.shape, 1), cells)
    out = jnp.zeros_like(wide)
    for z in range(zb):
        shift = lax.rem(z * cells - ang * cells + total, total)
        here = jnp.logical_and(row_slice == z, lane_slice == z)
        out = jnp.where(here, pltpu.roll(wide, shift, 1), out)
    return out


def volume_pieces(dims, zdev, half, offset, halves):
    odd = lax.rem(lax.axis_index("slab"), 2)
    zb = dims[2]
    for i, h in enumerate(halves):
        start = pl.multiple_of(lax.rem(odd + h, 2) * half + offset, LANES)
        for zp in range(zdev // zb):
            yield i, zp, slice(zp * zb, (zp + 1) * zb), start


def rays_kernel(dims, first, keep, extra, halves, half, offset, width, *refs):
    per, groups, zb, cells = dims
    count = groups * SUBLANES
    if first:
        order_ref, start_ref, len_ref, table_ref, vol_ref, *refs = refs
    else:
        order_ref, table_ref, vol_ref, *refs, rows_ref = refs
    outs, refs = refs[:len(halves) * groups], refs[len(halves) * groups:]
    if first:
        left_ref, buf, sems, table_buf, order_buf, start_buf, len_buf, rows_ref, small_sems = refs
    else:
        buf, sems = refs
    zdev = vol_ref.shape[0]
    copies = []
    if first:
        small = [
            pltpu.make_async_copy(source, to, small_sems.at[i])
            for i, (source, to) in enumerate(
                [(order_ref, order_buf), (table_ref, table_buf), (start_ref, start_buf), (len_ref, len_buf)]
            )
        ]
        for copy in small:
            copy.start()
    for h, zp, slices, start in volume_pieces(dims, zdev, half, offset, halves):
        source = vol_ref.at[slices, :, pl.ds(start, width)]
        copies.append((h, zp, pltpu.make_async_copy(source, buf.at[h, slices], sems.at[h, zp])))
        copies[-1][-1].start()
    if first:
        small[0].wait()
        small[1].wait()
        both = jnp.concatenate(split(slice_weights(dims, 1, order_buf, table_buf, rows_ref)), axis=0)
        left = jnp.concatenate([both, both], axis=1)
        left_ref[...] = left
        small[2].wait()
        small[3].wait()
    else:
        both = jnp.concatenate(split(slice_weights(dims, 1, order_ref, table_ref, rows_ref)), axis=0)
        left = jnp.concatenate([both, both], axis=1)
    if extra:
        shape = (SUBLANES, LANES)
        angle, lane = low_bits(iota(shape, 0), per), iota(shape, 1)
        starts = pick(angle, [start_buf[0, a].astype(F32) for a in range(per)])
        lengths = pick(angle, [len_buf[0, a].astype(F32) for a in range(per)])
        for d in range(groups):
            foot = jnp.where(lane == 2 * d, starts, jnp.where(lane == 2 * d + 1, lengths, 0.0))
            for h in range(len(halves)):
                outs[h * groups + d][:, zdev // zb * width:] = foot
    for h, zp, copy in copies:
        copy.wait()
        for at, size in tiles(width):
            parts = [split(buf[h, zp * zb + z, :, at:at + size]) for z in range(zb)]
            product = dot(left, jnp.concatenate([p[0] for p in parts] + [p[1] for p in parts], axis=0))
            sums = product[:count] + product[count:]
            for d in range(groups):
                outs[h * groups + d][:, zp * width + at:zp * width + at + size] = (
                    sums[d * SUBLANES:(d + 1) * SUBLANES]
                )


def ray_sums(dims, chunk, halves, offset, width, given, small, table, volume):
    per, groups, zb, cells = dims
    zdev, _, total = volume.shape
    first, keep, extra = given is None, chunk > 0, chunk == 0
    count, all_cells = groups * SUBLANES, table.shape[1]
    out = jax.ShapeDtypeStruct((SUBLANES, zdev // zb * width + (LANES if extra else 0)), F32)
    left = jax.ShapeDtypeStruct((2 * count, 2 * zb * cells), BF16)
    columns = (len(halves), zdev, cells, width)
    assert zb * cells == all_cells
    shapes = [out] * (len(halves) * groups)
    scratch = [] if keep else [pltpu.VMEM(columns, F32)]
    scratch += [pltpu.SemaphoreType.DMA((len(halves), zdev // zb))]
    if first:
        scratch += [pltpu.VMEM(table.shape, F32)] + [pltpu.SMEM(a.shape, a.dtype) for a in small]
        scratch += [pltpu.VMEM((count, all_cells), F32), pltpu.SemaphoreType.DMA((4,))]
        args, specs, limit = [*small, table, volume], [ANYWHERE] * 5, 58
        shapes += [left]
    else:
        scratch += [pltpu.VMEM((count, all_cells), F32)]
        args, specs, limit = [small[0], table, volume], [IN_SMEM, IN_VMEM, ANYWHERE], 40
    if keep:
        shapes += [jax.ShapeDtypeStruct(columns, F32)]
    size = zdev * cells * width * len(halves)
    return pl.pallas_call(
        functools.partial(rays_kernel, dims, first, keep, extra, halves, total // 2, offset, width),
        in_specs=specs,
        out_specs=[IN_VMEM] * len(shapes),
        out_shape=shapes,
        scratch_shapes=scratch,
        compiler_params=pltpu.CompilerParams(vmem_limit_bytes=limit * MIB),
        cost_estimate=pl.CostEstimate(flops=2 * size * 16, bytes_accessed=size * 4, transcendentals=0),
        name=f"ray_sums_{chunk}_{halves[0]}",
    )(*args)


def hat_weights(dims, zdev, start, length, row):
    per, groups, zb, cells = dims
    at = low_bits(iota(start.shape, 0), zdev * per)
    slice_at = over(at, zb * per) * zb + low_bits(over(at, per), zb)
    span = jnp.where(length > 0.0, length, 1.0) / zdev
    centre = start + (slice_at.astype(F32) + 0.5) * span
    hat = jnp.maximum(0.0, 1.0 - jnp.abs(row + 0.5 - centre) / span)
    return jnp.where(jnp.logical_and(row >= start, row < start + length), hat, 0.0)


def footprint_matrix(dims, zdev, rdev, foot):
    per = dims[0]
    rows = 2 * per * rdev
    slab = lax.axis_index("slab")
    sibling = slab + 1 - 2 * lax.rem(slab, 2)
    row_id = iota((1, rows), 1)
    row_slab = jnp.where(row_id < per * rdev, slab, sibling)
    row = (row_slab * rdev + low_bits(row_id, rdev)).astype(F32)
    shape = (foot.shape[0], rows)
    same_angle = low_bits(iota(shape, 0), per) == low_bits(over(iota(shape, 1), rdev), per)
    beyond = slab + jnp.where(low_bits(slab, 4) < 2, -2, 2)
    there = jnp.logical_and(beyond >= 0, beyond < lax.axis_size("slab"))
    known = jnp.where(there, foot.shape[0], foot.shape[0] // 3 * 2)
    meets = jnp.logical_and(same_angle, iota(shape, 0) < known)
    return jnp.where(meets, hat_weights(dims, zdev, foot[:, 0:1], foot[:, 1:2], row), 0.0)


def update_weights(dims, zdev, rdev, foot, order_ref, table_ref, rows_ref, out_ref):
    per, groups, zb, cells = dims
    count = groups * SUBLANES
    weights = slice_weights(dims, -1, order_ref, table_ref, rows_ref)
    window = -(-5 * rdev // LANES) * LANES
    row = ((lax.axis_index("slab") - 2) * rdev + iota((1, window), 1)).astype(F32)
    sums = [
        jnp.sum(hat_weights(dims, zdev, foot[:, 2 * d:2 * d + 1], foot[:, 2 * d + 1:2 * d + 2], row), axis=1, keepdims=True)
        for d in range(groups)
    ]
    pad = jnp.zeros((out_ref.shape[2] - 3 * count, weights.shape[1]), F32)
    for zp in range(zdev // zb):
        slices = jnp.concatenate([s[zp * SUBLANES:(zp + 1) * SUBLANES] for s in sums], axis=0)
        scaled = weights / jnp.sum(weights * slices, axis=0, keepdims=True)
        high = scaled.astype(BF16).astype(F32)
        stacked = jnp.concatenate([high, high, scaled - high, pad], axis=0)
        out_ref[zp] = stacked.T.astype(BF16)


def prepare_kernel(dims, rdev, half, width, order_ref, table_ref, foot_ref, _, vol_ref, kept_ref, left_ref, sems, rows_ref):
    zdev = vol_ref.shape[0]
    copies = []
    for h, zp, slices, start in volume_pieces(dims, zdev, half, 0, (0, 1)):
        source = vol_ref.at[slices, :, pl.ds(start, width)]
        copies.append(pltpu.make_async_copy(source, kept_ref.at[h, slices], sems.at[h, zp]))
        copies[-1].start()
    batches = zdev // dims[2]
    foot = jnp.concatenate([foot_ref[0, :, batches * width:]] * batches, axis=0)
    update_weights(dims, zdev, rdev, foot, order_ref, table_ref, rows_ref, left_ref)
    for copy in copies:
        copy.wait()


def prepare_step(dims, rdev, width, order, table, own, after, volume):
    per, groups, zb, cells = dims
    zdev, _, total = volume.shape
    depth = -(-3 * groups * SUBLANES // LANES) * LANES
    return pl.pallas_call(
        functools.partial(prepare_kernel, dims, rdev, total // 2, width),
        in_specs=[IN_SMEM, IN_VMEM, IN_VMEM, ANYWHERE, ANYWHERE],
        out_specs=[IN_VMEM, IN_VMEM],
        out_shape=[
            jax.ShapeDtypeStruct((2, zdev, cells, width), F32),
            jax.ShapeDtypeStruct((zdev // zb, zb * cells, depth), BF16),
        ],
        scratch_shapes=[
            pltpu.SemaphoreType.DMA((2, zdev // zb)),
            pltpu.VMEM((groups * SUBLANES, table.shape[1]), F32),
        ],
        compiler_params=pltpu.CompilerParams(vmem_limit_bytes=40 * MIB),
        cost_estimate=pl.CostEstimate(flops=0, bytes_accessed=8 * zdev * cells * width, transcendentals=0),
        name="prepare",
    )(order, table, own, after, volume)


def residual_kernel(dims, first, half, rdev, zdev, offset, width, *refs):
    per, groups, zb, cells = dims
    block = zdev * per
    if first:
        order_ref, table_ref, *refs = refs
    else:
        mats, inverse_ref, refs = refs[:4], refs[4], refs[5:]
    sums_refs, (mine_ref, theirs_ref), refs = refs[:3], refs[3:5], refs[5:]
    if not first:
        mine_before, sent_before, *refs = refs
    mine_out, sent_out, *refs = refs
    if not first:
        mine_out[:, :, :offset] = mine_before[...]
        sent_out[:, :, :offset] = sent_before[...]
    outs, refs = refs[:3], refs[3:]
    if first:
        foot = jnp.concatenate(
            [r[i, :, zdev // zb * width:] for r in sums_refs for i in range(2) for _ in range(zdev // zb)], axis=0
        )
        kernel = footprint_matrix(dims, zdev, rdev, foot)
        count, rows = kernel.shape
        kernel_t = kernel.T
        cover = jnp.sum(kernel_t, axis=1, keepdims=True)
        angle = low_bits(over(iota((rows, 1), 0), rdev), per)
        path = jnp.zeros((rows, 1), F32)
        for a in range(per):
            at = order_ref[lax.axis_index("ang") * per + a]
            path = jnp.where(angle == a, jnp.sum(table_ref[pl.ds(at, 1), :], axis=1, keepdims=True), path)
        inverse = 1.0 / jnp.maximum(path * cover, 0.25)
        ahead, back = split(kernel_t), split(kernel)
        for ref, value in zip(refs, (*ahead, *back)):
            ref[...] = value
        refs[4][...] = jnp.broadcast_to(inverse, (rows, LANES))
    else:
        ahead, back = (mats[0][...], mats[1][...]), (mats[2][...], mats[3][...])
        inverse = inverse_ref[:, 0:1]
    start = lax.rem(lax.axis_index("slab"), 2) * half + offset
    for at, size in tiles(width):
        columns = slice(at, at + size)
        mine = mine_ref[:, :, pl.ds(pl.multiple_of(start + at, LANES), size)].astype(F32)
        theirs = theirs_ref[:, :, offset + at:offset + at + size]
        measured = jnp.concatenate([m.reshape(per * rdev, size) for m in (mine, theirs)], axis=0)
        sums = jnp.concatenate(
            [
                r[i, :, zp * width + at:zp * width + at + size]
                for r in sums_refs for i in range(2) for zp in range(zdev // zb)
            ],
            axis=0,
        )
        residual = (measured - dot3(ahead, split(sums))) * inverse
        placed = slice(offset + at, offset + at + size)
        mine_out[:, :, placed] = residual[:per * rdev].reshape(per, rdev, size)
        sent_out[:, :, placed] = residual[per * rdev:].reshape(per, rdev, size)
        given = dot3(back, split(residual))
        for i, ref in enumerate(outs):
            for j in range(2):
                ref[j, :, columns] = given[(2 * i + j) * block:(2 * i + j + 1) * block]


def residual_step(dims, zdev, chunk, offset, width, mats, before, order, table, sums, measured, theirs):
    per, groups, zb, cells = dims
    _, rdev, total = measured.shape
    first = chunk == 0
    block = zdev * per
    count, rows = 6 * block, 2 * per * rdev
    given = jax.ShapeDtypeStruct((2, block, width), F32)
    piece = jax.ShapeDtypeStruct((per, rdev, offset + width), F32)
    shapes = [piece, piece, given, given, given]
    if first:
        args, specs = [order, table], [IN_SMEM, IN_VMEM]
        ahead, back = jax.ShapeDtypeStruct((rows, count), BF16), jax.ShapeDtypeStruct((count, rows), BF16)
        shapes += [ahead, ahead, back, back, jax.ShapeDtypeStruct((rows, LANES), F32)]
    else:
        args, specs = list(mats), [IN_VMEM] * len(mats)
    args += [*sums, measured, theirs, *before]
    specs += [IN_VMEM] * (5 + len(before))
    return pl.pallas_call(
        functools.partial(residual_kernel, dims, first, total // 2, rdev, zdev, offset, width),
        in_specs=specs,
        out_specs=[IN_VMEM] * len(shapes),
        out_shape=shapes,
        compiler_params=pltpu.CompilerParams(vmem_limit_bytes=30 * MIB),
        cost_estimate=pl.CostEstimate(
            flops=12 * count * rows * width, bytes_accessed=8 * width * (count + rows), transcendentals=0
        ),
        name=f"residual_{chunk}",
    )(*args)


def update_kernel(dims, first, halves, half, offset, width, *refs):
    per, groups, zb, cells = dims
    count = groups * SUBLANES
    left_ref, backs, refs = refs[0], refs[len(halves) * groups:0:-1], refs[1 + len(halves) * groups:]
    vol_ref, *refs = refs
    zdev, depth = vol_ref.shape[1], left_ref.shape[2]
    if not first:
        refs = refs[1:]
    pieces = refs[:-3]
    if pieces:
        *pieces, out_ref, res_ref, buf, sems, res_sems = refs
    else:
        out_ref, buf, sems = refs
    odd = lax.rem(lax.axis_index("slab"), 2)
    leaving = []
    for h, ref in enumerate(pieces):
        columns = pl.ds(pl.multiple_of(lax.rem(odd + h, 2) * half, LANES), half)
        leaving.append(pltpu.make_async_copy(ref, res_ref.at[:, :, columns], res_sems.at[h]))
        leaving[-1].start()
    held = len(halves) < vol_ref.shape[0]
    for i, zp, slices, start in volume_pieces(dims, zdev, half, offset, halves):
        rows = slice(zp * SUBLANES, (zp + 1) * SUBLANES)
        left = left_ref[zp]
        for at, size in tiles(width):
            piece = slice(at, at + size)
            back = jnp.concatenate([backs[i * groups + d][rows, piece] for d in range(groups)], axis=0)
            high, low = split(back)
            pad = jnp.zeros((depth - 3 * count, size), BF16)
            change = dot(left, jnp.concatenate([high, low, high, pad], axis=0))
            for z in range(zb):
                buf[i, zp * zb + z, :, piece] = (
                    vol_ref[halves[i] if held else i, zp * zb + z, :, piece] + change[z * cells:(z + 1) * cells]
                )
        leaving.append(
            pltpu.make_async_copy(buf.at[i, slices], out_ref.at[slices, :, pl.ds(start, width)], sems.at[i, zp])
        )
        leaving[-1].start()
    for copy in leaving:
        copy.wait()


def update_step(dims, chunk, halves, offset, width, left, backs, pieces, kept, volume, out):
    per, groups, zb, cells = dims
    zdev, _, total = volume.shape
    first = out is None
    args = [left, *backs[::-1], kept]
    shapes = [jax.ShapeDtypeStruct(volume.shape, F32)]
    scratch = [
        pltpu.VMEM((len(halves), zdev, cells, width), F32),
        pltpu.SemaphoreType.DMA((len(halves), zdev // zb)),
    ]
    specs = [IN_VMEM] * len(args)
    aliases = {}
    if not first:
        aliases = {len(args): 0}
        args += [out]
        specs += [ANYWHERE]
    if pieces:
        args += pieces
        specs += [IN_VMEM] * 2
        shapes += [jax.ShapeDtypeStruct((*pieces[0].shape[:2], total), F32)]
        scratch += [pltpu.SemaphoreType.DMA((2,))]
    size = zdev * cells * width * len(halves)
    return pl.pallas_call(
        functools.partial(update_kernel, dims, first, halves, total // 2, offset, width),
        in_specs=specs,
        out_specs=[ANYWHERE] * len(shapes),
        out_shape=shapes,
        scratch_shapes=scratch,
        input_output_aliases=aliases,
        compiler_params=pltpu.CompilerParams(vmem_limit_bytes=20 * MIB),
        cost_estimate=pl.CostEstimate(flops=2 * size * 48, bytes_accessed=size * 4, transcendentals=0),
        name=f"update_{chunk}_{halves[0]}",
    )(*args)


def body(volume, measured, foot_start, foot_len, order, table):
    slabs, groups = lax.axis_size("slab"), lax.axis_size("ang")
    per, rdev, total = measured.shape
    zdev, cells, _ = volume.shape
    half = total // 2
    zb = SUBLANES // per
    dims = (per, groups, zb, cells)
    each = half // CHUNKS
    widths = [each] * CHUNKS
    offsets = [sum(widths[:c]) for c in range(CHUNKS)]

    def along(value, to):
        pairs = [(s, to(s)) for s in range(slabs)]
        return lax.ppermute(value, "slab", pairs)

    def spread(value, other, d):
        if not (other or d):
            return value
        pairs = [
            (s * groups + a, (s ^ other) * groups + (a + d) % groups) for s in range(slabs) for a in range(groups)
        ]
        return lax.ppermute(value, ("slab", "ang"), pairs)

    def facing(s):
        return s ^ 2

    def step(up, busy):
        def to(s):
            there = s + 4 if up(s) else s - 4
            if 0 <= there < slabs:
                return there
            return there % slabs if busy else facing(s)
        return to

    def beyond(c):
        return step(lambda s: not s & 2, c < CHUNKS - 1)

    def back_from_beyond(c):
        return step(lambda s: s & 2, c > 0)

    odd = lax.rem(lax.axis_index("slab"), 2)
    theirs = along(
        lax.dynamic_slice_in_dim(measured, (1 - odd) * half, half, 2).astype(F32), lambda s: s ^ 1
    )

    sums, kept, left = [], [[] for _ in range(CHUNKS)], None
    for c in range(CHUNKS):
        parts = []
        for halves in RAY_HALVES[c]:
            made = ray_sums(
                dims, c, halves, offsets[c], widths[c], left, (order, foot_start, foot_len), table, volume
            )
            parts += made[:len(halves) * groups]
            if left is None:
                left = made[-1]
                parts[0], table = lax.optimization_barrier((parts[0], table))
            elif c:
                kept[c] += [(h, made[-1]) for h in halves]
        parts = [spread(parts[h * groups + d], h, d) for h in range(2) for d in range(groups)]
        if c:
            parts, _ = lax.optimization_barrier((parts, sums[-1][0]))
        own = jnp.stack([sum(parts[:groups]), sum(parts[groups:])])
        near = along(own, facing)
        if c == 0:
            first_columns, update_left = prepare_step(dims, rdev, widths[0], order, table, own, near, volume)
            kept[0] = [(h, first_columns) for h in range(2)]
        if c == 1:
            near, first_columns = lax.optimization_barrier((near, first_columns))
        far = along(near, beyond(c))
        sums.append((own, near, far))
    pieces, given, mats = [], [], None
    for c in range(CHUNKS):
        mine, sent, own, near, far, *rest = residual_step(
            dims, zdev, c, offsets[c], widths[c], mats, pieces, order, table, sums[c], measured, theirs
        )
        pieces = [mine, sent]
        mats = rest if c == 0 else mats
        near = near + along(far, back_from_beyond(c))
        arrived = along(near, facing)
        halves = [own[i] + arrived[i] for i in range(2)]
        given.append([spread(halves[h], h, d) for h in range(2) for d in range(groups)])
    pieces = [mine, along(sent, lambda s: s ^ 1)]
    out, res = None, []
    for c in range(CHUNKS):
        for halves in UPDATE_HALVES[c]:
            backs = [b for h in halves for b in given[c][h * groups:(h + 1) * groups]]
            write = c == CHUNKS - 1 and halves[0] == 0
            out, *made = update_step(
                dims, c, halves, offsets[c], widths[c], update_left, backs, pieces if write else [],
                dict(kept[c])[halves[0]], volume, out,
            )
            res += made
    return out, res[0]


def solution(mesh):
    return jax.shard_map(
        body,
        mesh=mesh,
        in_specs=(
            P("slab", "ang", None),
            P("ang", "slab", None),
            P("slab", "ang"),
            P("slab", "ang"),
            P(),
            P(),
        ),
        out_specs=(P("slab", "ang", None), P("ang", "slab", None)),
        check_vma=False,
    )
```
